32 devices in a mesh: dp: 16 (over z, y, x), pipe: 2 (over core).
Axes of the slice: x: 2, y: 2, z: 4, core: 2. Of those that a mesh axis runs over, the one named last changes fastest.
Arguments:
- block_input: bfloat16 [32, 1024, 384], P('dp'), may hold values from -6 to 6
- cotangent: bfloat16 [32, 1024, 384], P('dp'), may hold values from -6 to 6
- sigma_index: int32 [32], P('dp'), may hold values from 0 to 255
- class_label: int32 [32], P('dp'), may hold values from 0 to 999
- sigma_table: bfloat16 [256, 768], replicated, may hold values from -6 to 6
- class_table: bfloat16 [1000, 768], replicated, may hold values from -6 to 6
- w_emb: bfloat16 [768, 768], replicated, may hold values from -0.21875 to 0.21875
- b_emb: bfloat16 [768], replicated, may hold values from -3 to 3
- norm1_gain: bfloat16 [384], replicated, may hold values from 0.099609375 to 1.8984375
- norm1_bias: bfloat16 [384], replicated, may hold values from -3 to 3
- w_conv1: bfloat16 [3, 3, 384, 384], replicated, may hold values from -0.109375 to 0.109375
- b_conv1: bfloat16 [384], replicated, may hold values from -3 to 3
- norm2_gain: bfloat16 [384], replicated, may hold values from 0.099609375 to 1.8984375
- norm2_bias: bfloat16 [384], replicated, may hold values from -3 to 3
- w_conv2: bfloat16 [3, 3, 384, 384], replicated, may hold values from -0.109375 to 0.109375
- b_conv2: bfloat16 [384], replicated, may hold values from -3 to 3
- norm3_gain: bfloat16 [384], replicated, may hold values from 0.099609375 to 1.8984375
- norm3_bias: bfloat16 [384], replicated, may hold values from -3 to 3
- w_qkv: bfloat16 [384, 1152], replicated, may hold values from -0.4375 to 0.4375
- b_qv: bfloat16 [768], replicated, may hold values from -3 to 3
- w_proj: bfloat16 [384, 384], replicated, may hold values from -2.5 to 2.5
- b_proj: bfloat16 [384], replicated, may hold values from -3 to 3
Outputs:
- output: bfloat16 [32, 1024, 384], P('dp', 'pipe')
- input_grad: bfloat16 [32, 1024, 384], P('dp', 'pipe')
- sigma_table_grad: float32 [256, 768], P(None, ('dp', 'pipe'))
- class_table_grad: float32 [1000, 768], P(None, ('dp', 'pipe'))
- w_emb_grad: float32 [768, 768], P(None, ('dp', 'pipe'))
- b_emb_grad: float32 [768], P(('dp', 'pipe'))
- norm1_gain_grad: float32 [384], P(('dp', 'pipe'))
- norm1_bias_grad: float32 [384], P(('dp', 'pipe'))
- w_conv1_grad: float32 [3, 3, 384, 384], P(None, None, None, ('dp', 'pipe'))
- b_conv1_grad: float32 [384], P(('dp', 'pipe'))
- norm2_gain_grad: float32 [384], P(('dp', 'pipe'))
- norm2_bias_grad: float32 [384], P(('dp', 'pipe'))
- w_conv2_grad: float32 [3, 3, 384, 384], P(None, None, None, ('dp', 'pipe'))
- b_conv2_grad: float32 [384], P(('dp', 'pipe'))
- norm3_gain_grad: float32 [384], P(('dp', 'pipe'))
- norm3_bias_grad: float32 [384], P(('dp', 'pipe'))
- w_qkv_grad: float32 [384, 1152], P(None, ('dp', 'pipe'))
- b_qv_grad: float32 [768], P(('dp', 'pipe'))
- w_proj_grad: float32 [384, 384], P(None, ('dp', 'pipe'))
- b_proj_grad: float32 [384], P(('dp', 'pipe'))
The draws below stay inside these ranges and needn't reach their ends.
All inputs are finite; a program needn't handle non-finite values.
Results may differ from the reference program's by a relative error of at most 0.02.
The reference program's roundings to bfloat16 on the way count: a program that leaves them out, or rounds other values in their place, can miss the bound.
Values may be sent and summed in bfloat16 or wider, within the bound.
No kernel may reach another device: no remote copies, remote signals or barrier semaphores. Data moves between devices by JAX's collectives and lax.ppermute only.
A program may use at most 192 MiB of HBM per device.

```python
import math
import jax
import jax.numpy as jnp
import numpy as np
from jax import lax

C = 384
EMB = 768
HEADS = 6
CLASSES = 1000
GROUPS = 32
SIDE = 32
PIX = 1024
NSIG = 256
IMAGES = 32


def with_ends(values, own_key, low, high):
    extent = values.shape
    index_at = [jax.random.randint(jax.random.fold_in(own_key, axis), (), 0, extent[axis]) for axis in range(len(extent))]
    values = values.at[tuple(index_at)].set(low)
    longest = extent.index(max(extent))
    index_at[longest] = (index_at[longest] + 1) % extent[longest]
    return values.at[tuple(index_at)].set(high)


def steps_of(rng, dims, shards, smallest, top_value):
    loudness = 1.0
    for position, blocks in shards:
        heights = jax.random.uniform(jax.random.fold_in(jax.random.fold_in(rng, 6), position), (blocks,), jnp.float32, smallest / len(shards), top_value / len(shards))
        loudness = loudness * jnp.repeat(jnp.exp(heights), dims[position] // blocks).reshape((-1,) + (1,) * (len(dims) - 1 - position))
    return loudness


def rank_bounds(count, lean):
    loads = [(1 << 20) // math.isqrt(grade ** lean) + 1 for grade in range(1, count + 1)]
    spread = 1 + sum(loads) // (1 << 30)
    return np.cumsum(np.array([max(1, weight // spread) for weight in loads]))


def skewed_ids(stream_key, dims, amount, lean):
    table = rank_bounds(amount, lean)
    lot = jax.random.randint(jax.random.fold_in(stream_key, 1), dims, 0, int(table[amount - 1]))
    standing = jnp.searchsorted(jnp.asarray(table, jnp.int32), lot, side="right")
    return jax.random.permutation(jax.random.fold_in(stream_key, 2), amount)[standing].astype(jnp.int32)


def bell_draw(key, extent, spread, most, shards=(), dtype=jnp.bfloat16):
    level = steps_of(key, extent, shards, -0.22, 0.18) if shards else 1.0
    drawn = jax.random.normal(key, extent, jnp.float32) * spread * level
    return jnp.minimum(jnp.maximum(drawn, -most), most).astype(dtype)


def setup_inputs(seed: int = 0) -> dict:
    key_of = jax.random.split(jax.random.key(seed), 23)
    block_input = bell_draw(key_of[0], (IMAGES, PIX, C), 1.0, 6.0, ((0, 16),))
    cotangent = bell_draw(key_of[1], (IMAGES, PIX, C), 1.0, 6.0, ((0, 16),))
    sigma_index = with_ends(skewed_ids(key_of[2], (IMAGES,), NSIG, 2), jax.random.fold_in(key_of[2], 3), 0, NSIG - 1).astype(jnp.int32)
    class_label = with_ends(jax.random.randint(key_of[3], (IMAGES,), 0, CLASSES), jax.random.fold_in(key_of[3], 1), 0, CLASSES - 1).astype(jnp.int32)
    sigma_table = bell_draw(key_of[4], (NSIG, EMB), 1.0, 6.0)
    class_table = bell_draw(key_of[5], (CLASSES, EMB), 1.0, 6.0)
    w_emb = bell_draw(key_of[6], (EMB, 2 * C), EMB ** -0.5, 0.21875)
    b_emb = bell_draw(key_of[7], (2 * C,), 0.5, 3.0)
    norm1_gain = jnp.clip(1.0 + 0.18 * jax.random.normal(key_of[8], (C,), jnp.float32), 0.099609375, 1.8984375).astype(jnp.bfloat16)
    norm1_bias = bell_draw(key_of[9], (C,), 0.5, 3.0)
    w_conv1 = bell_draw(key_of[10], (3, 3, C, C), (9 * C) ** -0.5, 0.109375)
    b_conv1 = bell_draw(key_of[11], (C,), 0.5, 3.0)
    norm2_gain = jnp.clip(1.0 + 0.18 * jax.random.normal(key_of[12], (C,), jnp.float32), 0.099609375, 1.8984375).astype(jnp.bfloat16)
    norm2_bias = bell_draw(key_of[13], (C,), 0.5, 3.0)
    w_conv2 = bell_draw(key_of[14], (3, 3, C, C), (9 * C) ** -0.5, 0.109375)
    b_conv2 = bell_draw(key_of[15], (C,), 0.5, 3.0)
    norm3_gain = jnp.clip(1.0 + 0.18 * jax.random.normal(key_of[16], (C,), jnp.float32), 0.099609375, 1.8984375).astype(jnp.bfloat16)
    norm3_bias = bell_draw(key_of[17], (C,), 0.5, 3.0)
    w_qkv = bell_draw(key_of[18], (C, 3 * C), (C // 2) ** -0.5, 0.4375)
    b_qv = bell_draw(key_of[19], (2 * C,), 0.5, 3.0)
    w_proj = bell_draw(key_of[20], (C, C), (C // 64) ** -0.5, 2.5)
    b_proj = bell_draw(key_of[21], (C,), 0.5, 3.0)
    return dict(block_input=block_input, cotangent=cotangent, sigma_index=sigma_index, class_label=class_label, sigma_table=sigma_table, class_table=class_table, w_emb=w_emb, b_emb=b_emb, norm1_gain=norm1_gain, norm1_bias=norm1_bias, w_conv1=w_conv1, b_conv1=b_conv1, norm2_gain=norm2_gain, norm2_bias=norm2_bias, w_conv2=w_conv2, b_conv2=b_conv2, norm3_gain=norm3_gain, norm3_bias=norm3_bias, w_qkv=w_qkv, b_qv=b_qv, w_proj=w_proj, b_proj=b_proj)


@jax.custom_vjp
def low(v):
    return lax.optimization_barrier(v.astype(jnp.bfloat16)).astype(jnp.float32)

@jax.custom_vjp
def low_back(v):
    return v

def low_keep(v):
    return (low(v), None)

def low_pass(kept, grad):
    return (grad,)

def back_keep(v):
    return (v, None)

def back_low(kept, grad):
    return (low(grad),)
low.defvjp(low_keep, low_pass)
low_back.defvjp(back_keep, back_low)
EPS = 1e-05
HIGH = lax.Precision.HIGHEST

def rounded_both(value):
    return low_back(low(value))

def group_norm(values, gain, bias):
    pixels, channels = values.shape
    grouped = values.reshape(pixels, GROUPS, channels // GROUPS)
    mean_val = lax.optimization_barrier(jnp.mean(grouped, axis=(0, 2), keepdims=True))
    centred = grouped - mean_val
    var_val = lax.optimization_barrier(jnp.mean(centred * centred, axis=(0, 2), keepdims=True))
    return (centred * lax.rsqrt(var_val + EPS)).reshape(pixels, channels) * gain + bias

def convolve(values, weight):
    channels = values.shape[1]
    image = values.reshape(1, SIDE, SIDE, channels)
    result = lax.conv_general_dilated(image, weight, (1, 1), 'SAME', dimension_numbers=('NHWC', 'HWIO', 'NHWC'), precision=HIGH)
    return result.reshape(SIDE * SIDE, weight.shape[3])

def one_image(inputs, params):
    image_rows, sigma_row, class_row = inputs
    sigma_table, class_table, w_emb, b_emb, norm1_gain, norm1_bias, w_conv1, b_conv1, norm2_gain, norm2_bias, w_conv2, b_conv2, norm3_gain, norm3_bias, w_qkv, b_qv, w_proj, b_proj = params
    channels = image_rows.shape[1]
    head_dim = channels // HEADS
    emb_input = sigma_table[sigma_row] + class_table[class_row]
    embedded = low(jax.nn.silu(emb_input))
    affine = jnp.dot(embedded, w_emb, precision=HIGH) + b_emb
    emb_scale = affine[:channels]
    emb_shift = affine[channels:]
    act_one = low(jax.nn.silu(group_norm(image_rows, norm1_gain, norm1_bias)))
    conv_one = low_back(convolve(act_one, w_conv1) + b_conv1)
    modulated = group_norm(conv_one, norm2_gain, norm2_bias) * (1.0 + emb_scale) + emb_shift
    act_two = low(jax.nn.silu(modulated))
    conv_two = low_back(convolve(act_two, w_conv2) + b_conv2)
    hidden = rounded_both(image_rows + conv_two)
    normed = low(group_norm(hidden, norm3_gain, norm3_bias))
    projected = jnp.dot(normed, w_qkv, precision=HIGH)
    queries = rounded_both(projected[:, :channels] + b_qv[:channels]).reshape(-1, HEADS, head_dim)
    key_rows = rounded_both(projected[:, channels:2 * channels]).reshape(-1, HEADS, head_dim)
    values = rounded_both(projected[:, 2 * channels:] + b_qv[channels:]).reshape(-1, HEADS, head_dim)
    scores = low_back(jnp.einsum('qhd,khd->hqk', queries, key_rows, precision=HIGH) * head_dim ** (-0.5))
    soft_weights = low(jax.nn.softmax(scores, axis=-1))
    attended = rounded_both(jnp.einsum('hqk,khd->qhd', soft_weights, values, precision=HIGH).reshape(-1, channels))
    return hidden + jnp.dot(attended, w_proj, precision=HIGH) + b_proj

def reference(block_input, cotangent, sigma_index, class_label, sigma_table, class_table, w_emb, b_emb, norm1_gain, norm1_bias, w_conv1, b_conv1, norm2_gain, norm2_bias, w_conv2, b_conv2, norm3_gain, norm3_bias, w_qkv, b_qv, w_proj, b_proj):
    params = tuple((weight.astype(jnp.float32) for weight in (sigma_table, class_table, w_emb, b_emb, norm1_gain, norm1_bias, w_conv1, b_conv1, norm2_gain, norm2_bias, w_conv2, b_conv2, norm3_gain, norm3_bias, w_qkv, b_qv, w_proj, b_proj)))

    def forward(inputs, weights):

        def single(items):
            return one_image(items, weights)
        return lax.map(jax.checkpoint(single), (inputs, sigma_index, class_label))
    outputs, pullback = jax.vjp(forward, block_input.astype(jnp.float32), params)
    input_grad, grads = pullback(cotangent.astype(jnp.float32))
    grad_sigma, grad_class, grad_w_emb, grad_b_emb, grad_gain_one, grad_bias_one, grad_conv_one, grad_cbias_one, grad_gain_two, grad_bias_two, grad_conv_two, grad_cbias_two, grad_gain_three, grad_bias_three, grad_w_qkv, grad_b_qv, grad_w_proj, grad_b_proj = grads
    return (outputs.astype(jnp.bfloat16), input_grad.astype(jnp.bfloat16), grad_sigma, grad_class, grad_w_emb, grad_b_emb, grad_gain_one, grad_bias_one, grad_conv_one, grad_cbias_one, grad_gain_two, grad_bias_two, grad_conv_two, grad_cbias_two, grad_gain_three, grad_bias_three, grad_w_qkv, grad_b_qv, grad_w_proj, grad_b_proj)
```

```python
import jax
import jax.numpy as jnp
import numpy as np
from jax import lax
from jax.experimental import pallas as pl
from jax.experimental.pallas import tpu as pltpu
from jax.sharding import PartitionSpec as P

HEADS = 6
GROUPS = 32
SIDE = 32
EPS = 1e-05
BF = jnp.bfloat16
F32 = jnp.float32
NN = (((1,), (0,)), ((), ()))
NT = (((1,), (1,)), ((), ()))
TN = (((0,), (0,)), ((), ()))


def mm(a, b, dims=NN):
    return lax.dot_general(a, b, dims, preferred_element_type=F32)


def silu(v):
    return v * jax.nn.sigmoid(v)


def silu_slope(v):
    s = jax.nn.sigmoid(v)
    return s * (1.0 + v * (1.0 - s))


def lanes(shape):
    return lax.broadcasted_iota(jnp.int32, shape, 1)


def shift_cols(a, d):
    if d == 0:
        return a
    n = a.shape[1]
    col = lanes(a.shape) & (SIDE - 1)
    ok = (col + d >= 0) & (col + d < SIDE)
    return jnp.where(ok, pltpu.roll(a, (-d) % n, 1), 0)


def shift_rows(a, d):
    if d == 0:
        return a
    n = a.shape[1]
    at = lanes(a.shape) + SIDE * d
    return jnp.where((at >= 0) & (at < n), pltpu.roll(a, (-SIDE * d) % n, 1), 0)


def split3(v):
    hi = v.astype(BF).astype(F32)
    mid = (v - hi).astype(BF).astype(F32)
    return hi, mid, v - hi - mid


def columns(cols, rows):
    lane = lanes((rows, 128))
    out = jnp.zeros((rows, 128), F32)
    for at, col in enumerate(cols):
        out = jnp.where(lane == at, col, out)
    return out


def exact_mm(matrix, cols):
    parts = [part for col in cols for part in split3(col)]
    got = mm(matrix, columns(parts, cols[0].shape[0]).astype(BF))
    return [
        jnp.sum(got[:, 3 * at : 3 * at + 3], axis=1, keepdims=True) for at in range(len(cols))
    ]


def group_matrix(channels):
    size = channels // GROUPS
    scale = -(-(1 << 19) // size)
    row = lax.broadcasted_iota(jnp.int32, (channels, channels), 0) * scale >> 19
    col = lax.broadcasted_iota(jnp.int32, (channels, channels), 1) * scale >> 19
    return jnp.where(row == col, 1.0, 0.0).astype(BF)


def group_means(cols, count):
    matrix = group_matrix(cols[0].shape[0])
    return [got * (1.0 / count) for got in exact_mm(matrix, cols)]


def group_stats(v):
    channels, pixels = v.shape
    count = channels // GROUPS * pixels
    (mean,) = group_means([jnp.sum(v, axis=1, keepdims=True)], count)
    centred = v - mean
    (var,) = group_means([jnp.sum(centred * centred, axis=1, keepdims=True)], count)
    inverse = lax.rsqrt(var + EPS)
    return centred * inverse, inverse


def group_back(t, u, inverse, gain, sum_t, sum_tu):
    channels, pixels = t.shape
    count = channels // GROUPS * pixels
    first, second = group_means([gain * sum_t, gain * sum_tu], count)
    return inverse * (t * gain - first - u * second)


def rowsum(v):
    return jnp.sum(v, axis=1, keepdims=True)


def fill_cols(ref, a, sign):
    c = a.shape[0]
    for j in range(3):
        ref[j * c : (j + 1) * c, :] = shift_cols(a, sign * (j - 1)).astype(BF)


def conv_apply(w_ref, cat_ref, sign, channels):
    total = None
    for i in range(3):
        y = mm(w_ref[i * channels : (i + 1) * channels, :], cat_ref[...])
        y = shift_rows(y, sign * (i - 1))
        total = y if total is None else total + y
    return total


def kernel_forward(
    sel, x_ref, cot_ref, sig_ref, cls_ref, prm_ref, wemb_ref, bemb_ref, w1_ref, w2_ref, wqkv_ref, wproj_ref, perm_ref,
    a1_ref, a2_ref, u1_ref, u2_ref, stat_ref, out_ref, hg_ref, keep_ref, send_ref,
    cott_ref, wide, tall, wf, k_nt, v_nt, q_nt, q_t, k_t, v_t, ga_t, at_t, gq_t,
):
    channels = x_ref.shape[2]
    head = channels // HEADS
    row16 = lax.broadcasted_iota(jnp.int32, sig_ref.shape, 0)
    sig = jnp.where(row16 == sel[1] % 16, sig_ref[...].astype(F32), 0.0)
    cls = jnp.where(row16 == sel[2] % 16, cls_ref[...].astype(F32), 0.0)
    emb = jnp.sum(sig + cls, axis=0, keepdims=True)
    low = jnp.broadcast_to(silu(emb), (16, emb.shape[1])).astype(BF)
    affine = mm(low, wemb_ref[...])[0:1] + bemb_ref[...]
    row = lax.broadcasted_iota(jnp.int32, prm_ref.shape, 0)
    prm = prm_ref[...]
    prm = jnp.where(row == 14, affine[:, :channels], prm)
    prm = jnp.where(row == 15, affine[:, channels:], prm)
    prm = jnp.where(row == 16, emb[:, :channels], prm)
    prm = jnp.where(row == 17, emb[:, channels:], prm)
    prm = prm.T
    stat_ref[...] = prm
    col = lambda at: prm[:, at : at + 1]
    g1, b1, bc1, g2, b2, bc2, g3, b3, bq, bv, bp = [col(at) for at in range(11)]
    scale, shift = col(14), col(15)
    xt = x_ref[0].astype(F32).T
    u1, inv1 = group_stats(xt)
    u1_ref[...] = u1
    fill_cols(a1_ref, silu(u1 * g1 + b1), 1)
    for i in range(3):
        for j in range(3):
            wf[i * channels : (i + 1) * channels, j * channels : (j + 1) * channels] = w1_ref[
                3 * i + j
            ].T
    c1 = conv_apply(wf, a1_ref, 1, channels) + bc1
    u2, inv2 = group_stats(c1)
    u2_ref[...] = u2
    gm = g2 * (1.0 + scale)
    fill_cols(a2_ref, silu(u2 * gm + (b2 * (1.0 + scale) + shift)), 1)
    for i in range(3):
        for j in range(3):
            wf[i * channels : (i + 1) * channels, j * channels : (j + 1) * channels] = w2_ref[
                3 * i + j
            ].T
    hidden = (xt + conv_apply(wf, a2_ref, 1, channels) + bc2).astype(BF)
    hf = hidden.astype(F32)
    u3, inv3 = group_stats(hf)
    normed = (u3 * g3 + b3).astype(BF)
    projected = mm(wqkv_ref[...], normed, TN)
    q_t[...] = (projected[:channels] + bq).astype(BF)
    k_t[...] = projected[channels : 2 * channels].astype(BF)
    v_t[...] = (projected[2 * channels :] + bv).astype(BF)
    cot = cot_ref[0].astype(F32).T
    cott_ref[...] = cot.astype(BF)
    ga_t[...] = mm(wproj_ref[...], cott_ref[...]).astype(BF)
    pix = xt.shape[1]
    lane = lanes((pix, 128))
    for h in range(HEADS):
        at = slice(h * head, (h + 1) * head)
        q_nt[h] = q_t[at, :].T
        k_nt[h] = k_t[at, :].T
        v_nt[h] = v_t[at, :].T
    factor = head ** (-0.5)

    def one_head(h, _):
        at = pl.ds(pl.multiple_of(h * head, head), head)
        qh = q_t[at, :]
        s = mm(k_nt[h], qh)
        top = jnp.max(s, axis=0, keepdims=True)
        e = jnp.exp((s - top) * factor)
        eb = e.astype(BF)
        vh = jnp.concatenate([v_t[at, :], jnp.ones((16, pix), BF)], axis=0)
        o = mm(vh, eb)
        inv_l = 1.0 / o[head : head + 1]
        o = o[:head] * inv_l
        at_t[at, :] = o.astype(BF)
        g = ga_t[at, :].astype(F32)
        centre = jnp.sum(g * o, axis=0, keepdims=True) * inv_l
        gl = (g * inv_l).astype(BF)
        dp = mm(v_nt[h], gl)
        ds = (eb.astype(F32) * (dp - centre)).astype(BF)
        gq_t[at, :] = (mm(k_t[at, :], ds) * factor).astype(BF)
        dk = mm(ds, q_nt[h]) * factor
        gq_t[pl.ds(pl.multiple_of(channels + h * head, head), head), :] = dk.T.astype(BF)
        dv = mm(eb, gl.T)
        gq_t[pl.ds(pl.multiple_of(2 * channels + h * head, head), head), :] = dv.T.astype(BF)
        return 0

    lax.fori_loop(0, HEADS, one_head, 0)
    out = hf + mm(wproj_ref[...], at_t[...], TN) + bp
    out_ref[...] = out.T.astype(BF)
    perm = perm_ref[...]
    half = channels // 2
    got = mm(gq_t[...], normed, NT)
    tiles = channels // 128
    for t in range(tiles):
        wide[t] = got[:, t * 128 : (t + 1) * 128]
    for n in range(4):
        if n < 3:
            part = jnp.concatenate(
                [wide[t, pl.ds(n, channels, stride=3), :] for t in range(tiles)], axis=1
            )
        else:
            part = mm(cott_ref[...], at_t[...], NT)
        part = mm(perm, part.astype(BF))
        at = slice(n * channels, (n + 1) * channels)
        keep_ref[:, at] = part[:half]
        send_ref[:, at] = part[half:].astype(BF)
    gn = mm(wqkv_ref[...], gq_t[...])
    s3 = rowsum(gn)
    su3 = rowsum(gn * u3)
    hg = cott_ref[...].astype(F32) + group_back(gn, u3, inv3, g3, s3, su3)
    hg_ref[...] = hg.astype(BF)
    gq = gq_t[...].astype(F32)
    tall[:channels] = jnp.broadcast_to(rowsum(gq[:channels]), (channels, 128))
    tall[channels:] = jnp.broadcast_to(rowsum(gq[2 * channels :]), (channels, 128))
    extra = [
        inv1, inv2, su3, s3,
        tall[pl.ds(0, channels, stride=2), :], tall[pl.ds(1, channels, stride=2), :],
        rowsum(cott_ref[...].astype(F32)), rowsum(hg_ref[...].astype(F32)),
    ]
    stat_ref[...] = with_columns(stat_ref[...], 32, extra)


def with_columns(stat, start, extra):
    lane = lanes(stat.shape)
    for n, c in enumerate(extra):
        stat = jnp.where(lane == start + n, c, stat)
    return stat


def kernel_weight(g_ref, a_ref, perm_ref, keep_ref, send_ref, stack):
    channels = g_ref.shape[0]
    half = channels // 2
    g = mm(perm_ref[...], g_ref[...])
    for i in range(3):
        stack[i * channels : (i + 1) * channels, :] = shift_rows(g, 1 - i).astype(BF)
    for i in range(3):
        got = mm(stack[i * channels : (i + 1) * channels, :], a_ref[...], NT)
        at = slice(i * 3 * channels, (i + 1) * 3 * channels)
        keep_ref[:, at] = got[:half]
        send_ref[:, at] = got[half:].astype(BF)


def kernel_weight_side(
    img, g_ref, a_ref, perm_ref, stat_ref, keep_ref, send_ref, stack
):
    channels = g_ref.shape[0]
    half = channels // 2
    taps = 9 * channels
    kernel_weight(g_ref, a_ref, perm_ref, keep_ref, send_ref, stack)
    stat = stat_ref[...]
    width = keep_ref.shape[1] - taps
    lane = lanes((channels, width))
    side = jnp.zeros((channels, width), F32)
    for n in range(11):
        side = jnp.where(lane == n, stat[:, 34 + n : 35 + n], side)
    for n in range(4):
        side = jnp.where(lane == 128 + 4 * img[0] + n, stat[:, 48 + n : 49 + n], side)
    side = sum(mm(perm_ref[...], part.astype(BF)) for part in split3(side))
    keep_ref[:, taps:] = side[:half]
    send_ref[:, taps:] = side[half:].astype(BF)


def copy_back(wb, w_ref, channels):
    for i in range(3):
        for j in range(3):
            wb[i * channels : (i + 1) * channels, j * channels : (j + 1) * channels] = w_ref[
                3 * i + j
            ]


def kernel_second(hg_ref, w2_ref, u2_ref, stat_ref, wemb_ref, dc_ref, stat_out, wb, cat, tall):
    channels = hg_ref.shape[0]
    stat = stat_ref[...]
    col = lambda at: stat[:, at : at + 1]
    g2, b2, scale, shift, inv2 = col(3), col(4), col(14), col(15), col(33)
    fill_cols(cat, hg_ref[...].astype(F32), -1)
    copy_back(wb, w2_ref, channels)
    da = conv_apply(wb, cat, -1, channels)
    u2 = u2_ref[...]
    gm = g2 * (1.0 + scale)
    dm = da * silu_slope(u2 * gm + (b2 * (1.0 + scale) + shift))
    s = rowsum(dm)
    su = rowsum(dm * u2)
    dc = group_back(dm, u2, inv2, gm, s, su).astype(BF)
    dc_ref[...] = dc
    tall[:channels] = jnp.broadcast_to(g2 * su + b2 * s, (channels, 128))
    tall[channels:] = jnp.broadcast_to(s, (channels, 128))
    wide = tall[...]
    ga = [tall[pl.ds(n, channels, stride=2), :] for n in range(2)]
    (ge,) = exact_mm(wemb_ref[...], [wide[:, :1]])
    tall[:channels] = jnp.broadcast_to(ge[:channels] * silu_slope(col(16)), (channels, 128))
    tall[channels:] = jnp.broadcast_to(ge[channels:] * silu_slope(col(17)), (channels, 128))
    ge = [tall[pl.ds(n, channels, stride=2), :] for n in range(2)]
    stat = with_columns(
        stat, 40, [(1.0 + scale) * su, (1.0 + scale) * s, rowsum(dc.astype(F32))]
    )
    stat_out[...] = with_columns(stat, 48, ga + ge)


def kernel_first(dc_ref, hg_ref, w1_ref, u1_ref, stat_ref, ig_ref, stat_out, wb, cat):
    channels = hg_ref.shape[0]
    stat = stat_ref[...]
    col = lambda at: stat[:, at : at + 1]
    g1, b1, inv1 = col(0), col(1), col(32)
    fill_cols(cat, dc_ref[...].astype(F32), -1)
    copy_back(wb, w1_ref, channels)
    da = conv_apply(wb, cat, -1, channels)
    u1 = u1_ref[...]
    dp = da * silu_slope(u1 * g1 + b1)
    s = rowsum(dp)
    su = rowsum(dp * u1)
    ig = hg_ref[...].astype(F32) + group_back(dp, u1, inv1, g1, s, su)
    ig_ref[...] = ig.T.astype(BF)
    stat_out[...] = with_columns(stat, 43, [su, s])


def whole(shape, prefetch=0):
    if prefetch:
        return pl.BlockSpec(shape, lambda i, s: (0,) * len(shape))
    return pl.BlockSpec(shape, lambda i: (0,) * len(shape))


def call(kernel, ins, outs, scratch, prefetch=None, blocks=None, limit=56, name=None):
    count = 0 if prefetch is None else 1
    specs = [whole(v.shape, count) for v in ins]
    for at, spec in (blocks or {}).items():
        specs[at] = spec
    grid = pltpu.PrefetchScalarGridSpec(
        num_scalar_prefetch=count,
        grid=(1,),
        in_specs=specs,
        out_specs=[whole(shape, count) for shape, _ in outs],
        scratch_shapes=[pltpu.VMEM(shape, dtype) for shape, dtype in scratch],
    )
    operands = ([] if prefetch is None else [prefetch]) + list(ins)
    return pl.pallas_call(
        kernel,
        out_shape=[jax.ShapeDtypeStruct(shape, dtype) for shape, dtype in outs],
        grid_spec=grid,
        compiler_params=pltpu.CompilerParams(vmem_limit_bytes=limit * 2**20),
        name=name,
    )(*operands)


def stream_order(core, bits):
    order = list(range(bits))
    if core:
        for at in range(0, bits - 1, 2):
            order[at], order[at + 1] = order[at + 1], order[at]
    return order


def row_order(core, bits, rows):
    groups = 1 << bits
    size = rows // (2 * groups)
    found = []
    for part in (core, 1 - core):
        order = stream_order(part, bits)
        for at in range(groups):
            dp = 0
            for t in range(bits):
                dp |= ((at >> (bits - 1 - t)) & 1) << order[t]
            share = 2 * dp + part
            found.extend(range(share * size, (share + 1) * size))
    return np.array(found, np.int32)


def swap_core(v):
    return lax.ppermute(v, "pipe", [(0, 1), (1, 0)])


def exchange(v, step, bits):
    pairs = []
    for dp in range(1 << bits):
        for core in range(2):
            to = dp ^ (1 << stream_order(core, bits)[step])
            pairs.append((2 * dp + core, 2 * to + core))
    return lax.ppermute(v, ("dp", "pipe"), pairs)


def reduce_rows(keep, send, bits):
    core = lax.axis_index("pipe")
    dp = lax.axis_index("dp")
    got = swap_core(send)
    total = keep + got.astype(F32)
    for step in range(bits):
        half = total.shape[0] // 2
        at = jnp.where(core == 0, stream_order(0, bits)[step], stream_order(1, bits)[step])
        bit = (dp >> at) & 1
        send = lax.dynamic_slice_in_dim(total, (1 - bit) * half, half, 0).astype(BF)
        keep = lax.dynamic_slice_in_dim(total, bit * half, half, 0)
        total = keep + exchange(send, step, bits).astype(F32)
    return total


def body(
    block_input, cotangent, sigma_index, class_label, sigma_table, class_table, w_emb, b_emb,
    norm1_gain, norm1_bias, w_conv1, b_conv1, norm2_gain, norm2_bias, w_conv2, b_conv2,
    norm3_gain, norm3_bias, w_qkv, b_qv, w_proj, b_proj,
):
    core = lax.axis_index("pipe")
    dp = lax.axis_index("dp")
    data = lax.axis_size("dp")
    bits = data.bit_length() - 1
    images, pix, c = block_input.shape
    total_images = 2 * data
    emb_width = sigma_table.shape[1]
    head = c // HEADS
    half = c // 2
    size = c // (2 * data)
    rows = jnp.where(core == 0, row_order(0, bits, c), row_order(1, bits, c))
    perm = (rows[:, None] == jnp.arange(c, dtype=jnp.int32)[None, :]).astype(BF)
    index = jnp.stack([core, sigma_index[core], class_label[core]]).astype(jnp.int32)
    params = jnp.stack(
        [norm1_gain, norm1_bias, b_conv1, norm2_gain, norm2_bias, b_conv2, norm3_gain, norm3_bias,
         b_qv[:c], b_qv[c:], b_proj]
    ).astype(F32)
    params = jnp.concatenate([params, jnp.zeros((128 - params.shape[0], c), F32)], axis=0)
    w1 = w_conv1.reshape(9, c, c)
    w2 = w_conv2.reshape(9, c, c)
    own = lambda: pl.BlockSpec((1, pix, c), lambda i, s: (s[0], 0, 0))
    a1, a2, u1, u2, stat, out, hg, keep0, send0 = call(
        kernel_forward,
        [block_input, cotangent, sigma_table, class_table, params, w_emb,
         b_emb.astype(F32)[None], w1, w2, w_qkv, w_proj, perm],
        [((3 * c, pix), BF), ((3 * c, pix), BF), ((c, pix), F32), ((c, pix), F32), ((c, 128), F32),
         ((pix, c), BF), ((c, pix), BF), ((half, 4 * c), F32), ((half, 4 * c), BF)],
        [((c, pix), BF), ((c // 128, 3 * c, 128), F32), ((2 * c, 128), F32), ((3 * c, 3 * c), BF)]
        + [((HEADS, pix, head), BF)] * 3 + [((c, pix), BF)] * 5 + [((3 * c, pix), BF)],
        prefetch=index,
        blocks={0: own(), 1: own(),
                2: pl.BlockSpec((16, emb_width), lambda i, s: (s[1] // 16, 0)),
                3: pl.BlockSpec((16, emb_width), lambda i, s: (s[2] // 16, 0))},
        limit=60,
    )
    keep2, send2 = call(
        kernel_weight, [hg, a2, perm],
        [((half, 9 * c), F32), ((half, 9 * c), BF)], [((3 * c, pix), BF)],
    )
    later = reduce_rows(
        jnp.concatenate([keep0, keep2], axis=1), jnp.concatenate([send0, send2], axis=1), bits
    )
    dc, stat = call(
        kernel_second, [hg, w2, u2, stat, w_emb],
        [((c, pix), BF), ((c, 128), F32)],
        [((3 * c, 3 * c), BF), ((3 * c, pix), BF), ((2 * c, 128), F32)],
    )
    ig, stat = call(
        kernel_first, [dc, hg, w1, u1, stat],
        [((pix, c), BF), ((c, 128), F32)],
        [((3 * c, 3 * c), BF), ((3 * c, pix), BF)],
    )
    side = 128 + max(128, 4 * total_images)
    keep1, send1 = call(
        kernel_weight_side, [dc, a1, perm, stat],
        [((half, 9 * c + side), F32), ((half, 9 * c + side), BF)], [((3 * c, pix), BF)],
        prefetch=(2 * dp + core).astype(jnp.int32)[None],
    )
    first = reduce_rows(keep1, send1, bits)
    def halves(mine):
        top, low = mine[: pix // 2], mine[pix // 2 :]
        got = swap_core(jnp.where(core == 0, low, top))
        stay = jnp.where(core == 0, top, low)
        return jnp.stack([jnp.where(core == 0, stay, got), jnp.where(core == 0, got, stay)])
    output = halves(out)
    input_grad = halves(ig)
    conv = lambda v: jnp.transpose(v.reshape(size, 3, 3, c), (1, 2, 3, 0))
    g_qkv = jnp.transpose(later[:, : 3 * c].reshape(size, 3, c), (2, 0, 1)).reshape(c, 3 * size)
    g_proj = later[:, 3 * c : 4 * c].T
    g_conv2 = conv(later[:, 4 * c :])
    g_conv1 = conv(first[:, : 9 * c])
    side = first[:, 9 * c : 9 * c + 128]
    emb = first[:, 9 * c + 128 : 9 * c + 128 + 4 * total_images].reshape(size, total_images, 2, 2)
    emb = jnp.transpose(emb, (2, 1, 0, 3)).reshape(2, total_images, 2 * size)
    affine, into = emb[0], emb[1]
    all_index = lax.all_gather(
        jnp.stack([sigma_index, class_label]), "dp", axis=1, tiled=True
    )
    hot = lambda index, table: (
        index[:, None] == jnp.arange(table.shape[0], dtype=jnp.int32)[None, :]
    )
    hot_sigma, hot_class = hot(all_index[0], sigma_table), hot(all_index[1], class_table)
    look = lambda h, t: jnp.dot(h.astype(BF), t, preferred_element_type=F32)
    embedded = silu(look(hot_sigma, sigma_table) + look(hot_class, class_table)).astype(BF)
    high = lax.Precision.HIGHEST
    g_sigma = jnp.dot(hot_sigma.astype(F32).T, into, precision=high)
    g_class = jnp.dot(hot_class.astype(F32).T, into, precision=high)
    g_wemb = jnp.dot(embedded.astype(F32).T, affine, precision=high)
    g_bemb = jnp.sum(affine, axis=0)
    v = lambda at: side[:, at]
    g_bqv = side[:, 2:4].reshape(2 * size)
    return (
        output, input_grad, g_sigma, g_class, g_wemb, g_bemb, v(9), v(10), g_conv1, v(8), v(6), v(7),
        g_conv2, v(5), v(0), v(1), g_qkv, g_bqv, g_proj, v(4),
    )


def solution(mesh):
    every = ("dp", "pipe")
    return jax.shard_map(
        body,
        mesh=mesh,
        in_specs=(P("dp", None, None), P("dp", None, None), P("dp"), P("dp")) + (P(),) * 18,
        out_specs=(
            P("dp", "pipe", None), P("dp", "pipe", None), P(None, every), P(None, every),
            P(None, every), P(every), P(every), P(every), P(None, None, None, every), P(every),
            P(every), P(every), P(None, None, None, every), P(every), P(every), P(every),
            P(None, every), P(every), P(None, every), P(every),
        ),
        check_vma=False,
    )
```

```python
import jax
import jax.numpy as jnp
from jax import lax
from jax.experimental import pallas as pl
from jax.experimental.pallas import tpu as pltpu
from jax.sharding import PartitionSpec as P

HEADS = 6
GROUPS = 32
SIDE = 32
EPS = 1e-05
LOG2E = 1.4426950408889634
BF = jnp.bfloat16
F32 = jnp.float32
NN = (((1,), (0,)), ((), ()))
NT = (((1,), (1,)), ((), ()))
TN = (((0,), (0,)), ((), ()))


def mm(a, b, dims=NN):
    return lax.dot_general(a, b, dims, preferred_element_type=F32)


def silu(v):
    return v * jax.nn.sigmoid(v)


def silu_slope(v):
    s = jax.nn.sigmoid(v)
    return s * (1.0 + v * (1.0 - s))


def lanes(shape):
    return lax.broadcasted_iota(jnp.int32, shape, 1)


def rowsum(v):
    return jnp.sum(v, axis=1, keepdims=True)


def shift_cols(a, d):
    if d == 0:
        return a
    n = a.shape[1]
    col = lanes(a.shape) & (SIDE - 1)
    ok = (col + d >= 0) & (col + d < SIDE)
    return jnp.where(ok, pltpu.roll(a, (-d) % n, 1), 0)


def shift_rows(a, d):
    if d == 0:
        return a
    n = a.shape[1]
    at = lanes(a.shape) + SIDE * d
    return jnp.where((at >= 0) & (at < n), pltpu.roll(a, (-SIDE * d) % n, 1), 0)


def split3(v):
    hi = v.astype(BF).astype(F32)
    mid = (v - hi).astype(BF).astype(F32)
    return hi, mid, v - hi - mid


def exact_left(matrix, v, dims=NN):
    return sum(mm(matrix, part.astype(BF), dims) for part in split3(v))


def exact_right(v, matrix, dims=NN):
    return sum(mm(part.astype(BF), matrix, dims) for part in split3(v))


def with_columns(block, start, extra):
    lane = lanes(block.shape)
    for n, c in enumerate(extra):
        block = jnp.where(lane == start + n, c, block)
    return block


def exact_columns(matrix, cols):
    parts = [part for col in cols for part in split3(col)]
    block = with_columns(jnp.zeros((cols[0].shape[0], 128), F32), 0, parts)
    got = mm(matrix, block.astype(BF))
    return [rowsum(got[:, 3 * at : 3 * at + 3]) for at in range(len(cols))]


def divide(v, size, top):
    scale = -(-(1 << 19) // size)
    assert all((n * scale) >> 19 == n // size for n in range(top))
    return (v * scale) >> 19


def group_matrix(channels):
    size = channels // GROUPS
    shape = (channels, channels)
    row = divide(lax.broadcasted_iota(jnp.int32, (channels, 1), 0), size, channels)
    col = divide(lax.broadcasted_iota(jnp.int32, (1, channels), 1), size, channels)
    return jnp.where(row == col, 1.0, jnp.zeros(shape, F32)).astype(BF)


def group_means(cols, pixels):
    channels = cols[0].shape[0]
    count = channels // GROUPS * pixels
    return [got * (1.0 / count) for got in exact_columns(group_matrix(channels), cols)]


def group_stats(v):
    pixels = v.shape[1]
    (mean,) = group_means([rowsum(v)], pixels)
    centred = v - mean
    (var,) = group_means([rowsum(centred * centred)], pixels)
    inverse = lax.rsqrt(var + EPS)
    return centred * inverse, inverse


def group_back(t, u, inverse, gain, sum_t, sum_tu):
    first, second = group_means([gain * sum_t, gain * sum_tu], t.shape[1])
    return (inverse * gain) * t - inverse * first - u * (inverse * second)


def fill_cols(ref, a, sign):
    c = a.shape[0]
    for j in range(3):
        ref[j * c : (j + 1) * c, :] = shift_cols(a, sign * (j - 1)).astype(BF)


def conv_apply(w_ref, cat_ref, sign, channels):
    total = None
    for i in range(3):
        y = mm(w_ref[i * channels : (i + 1) * channels, :], cat_ref[...])
        y = shift_rows(y, sign * (i - 1))
        total = y if total is None else total + y
    return total


def fill_forward(wf, w_ref, channels):
    for i in range(3):
        for j in range(3):
            at = (slice(i * channels, (i + 1) * channels), slice(j * channels, (j + 1) * channels))
            wf[at] = w_ref[i, j].T


def copies(pairs, sems):
    made = [pltpu.make_async_copy(src, dst, sems.at[n]) for n, (src, dst) in enumerate(pairs)]
    for one in made:
        one.start()
    return made


def tap_pairs(w_ref, wb, channels):
    return [
        (
            w_ref.at[i, j],
            wb.at[
                i * channels : (i + 1) * channels, j * channels : (j + 1) * channels
            ],
        )
        for i in range(3)
        for j in range(3)
    ]


def stream_order(core, bits):
    order = list(range(bits))
    if core:
        for at in range(0, bits - 1, 2):
            order[at], order[at + 1] = order[at + 1], order[at]
    return order


def row_matrix(channels, bits):
    dp, core = lax.axis_index("dp"), lax.axis_index("pipe")
    size = channels // (2 << bits)
    quarter = channels // 4
    row = lax.broadcasted_iota(jnp.int32, (channels, 1), 0)
    part_of = sum(jnp.where(row >= quarter * n, 1, 0) for n in (1, 2, 3))
    rest = row - part_of * quarter
    at = divide(rest, size, quarter)
    within = rest - at * size
    part = jnp.where(part_of < 2, core, 1 - core)
    flips = []
    for p in (0, 1):
        order = stream_order(p, bits)
        flip = (part_of & 1) << order[0]
        for t in range(bits - 1):
            flip = flip | (((at >> (bits - 2 - t)) & 1) << order[t + 1])
        flips.append(flip)
    peer = dp ^ jnp.where(part == 0, flips[0], flips[1])
    wanted = (2 * peer + part) * size + within
    shape = (channels, channels)
    return jnp.where(wanted == lanes((1, channels)), 1.0, jnp.zeros(shape, F32)).astype(BF)


def own_image():
    return 2 * lax.axis_index("dp") + lax.axis_index("pipe")


def kernel_start(
    sig_at, cls_at, sig0, sig1, cls0, cls1, bemb, g1, b1, bc1, g2, b2, bc2, g3, b3, bqv, bp,
    x_ref, wemb_ref, w1_ref,
    stat_ref, act1_ref, act2_ref, u1_ref, u2_ref,
    x, wemb, w1, act1, act2, u1, u2, wf, cat, sems,
):
    core = lax.axis_index("pipe")
    channels = x.shape[1]
    loads = copies([(x_ref.at[core], x), (wemb_ref, wemb), (w1_ref, w1)], sems)
    row16 = lax.broadcasted_iota(jnp.int32, sig0.shape, 0)

    def table_row(at, first, second):
        block = jnp.where(core == 0, first[...].astype(F32), second[...].astype(F32))
        found = jnp.where(core == 0, at[0], at[1])
        return jnp.sum(jnp.where(row16 == found % 16, block, 0.0), axis=0, keepdims=True)

    emb = table_row(sig_at, sig0, sig1) + table_row(cls_at, cls0, cls1)
    flat = lambda ref: ref[...].astype(F32).reshape(1, ref.shape[0])
    bqv_row = flat(bqv)
    rows = [flat(ref) for ref in (g1, b1, bc1, g2, b2, bc2, g3, b3)]
    rows += [bqv_row[:, :channels], bqv_row[:, channels:], flat(bp)]
    prm = jnp.zeros((128, channels), F32)
    at = lax.broadcasted_iota(jnp.int32, prm.shape, 0)
    loads[0].wait()
    loads[1].wait()
    low = jnp.broadcast_to(silu(emb), (16, emb.shape[1])).astype(BF)
    affine = mm(low, wemb[...])[0:1] + flat(bemb)
    rows += [affine[:, :channels], affine[:, channels:], emb[:, :channels], emb[:, channels:]]
    for n, line in enumerate(rows):
        prm = jnp.where(at == n, line, prm)
    stat = prm.T
    col = lambda n: stat[:, n : n + 1]
    v1, inv1 = group_stats(x[...].astype(F32).T)
    u1[...] = v1
    a1 = silu(v1 * col(0) + col(1))
    act1[...] = a1.astype(BF)
    stores = copies([(u1, u1_ref), (act1, act1_ref)], sems.at[3:5])
    fill_cols(cat, a1, 1)
    loads[2].wait()
    fill_forward(wf, w1, channels)
    v2, inv2 = group_stats(conv_apply(wf, cat, 1, channels) + col(2))
    u2[...] = v2
    scale, shift = col(11), col(12)
    a2 = silu(v2 * (col(3) * (1.0 + scale)) + (col(4) * (1.0 + scale) + shift))
    act2[...] = a2.astype(BF)
    stores += copies([(u2, u2_ref), (act2, act2_ref)], sems.at[5:7])
    stat_ref[...] = with_columns(stat, 32, [inv1, inv2])
    for one in stores:
        one.wait()


def prepare_heads(q_t, k_t, v_t, q_nt, k_nt, v_nt, head):
    pix = q_t.shape[1]
    ones = jnp.where(lanes((pix, head)) < 2, 1.0, 0.0).astype(BF)
    for h in range(HEADS):
        at = slice(h * head, (h + 1) * head)
        q_nt[h] = q_t[at, :].T
        k_nt[h] = k_t[at, :].T
        v_nt[h, :, :head] = v_t[at, :].T
        v_nt[h, :, head:] = ones


def one_head(h, head, q_t, k_t, v_t, ga_t, q_nt, k_nt, v_nt, at_t, gq_t):
    channels, pix = q_t.shape
    factor = head ** (-0.5)
    rows = lambda base: pl.ds(pl.multiple_of(base + h * head, head), head)
    at = rows(0)
    s = mm(k_nt[h], q_t[at, :])
    top = jnp.max(s, axis=0, keepdims=True)
    e = jnp.exp2((s - top) * (factor * LOG2E)).astype(BF)
    o = mm(jnp.concatenate([v_t[at, :], jnp.ones((16, pix), BF)], axis=0), e)
    inv = 1.0 / o[head : head + 1]
    o = o[:head] * inv
    at_t[at, :] = o.astype(BF)
    g = ga_t[at, :].astype(F32)
    centre = -jnp.sum(g * o, axis=0, keepdims=True) * inv
    g = (g * inv).astype(BF)
    hi = centre.astype(BF).astype(F32)
    line = lax.broadcasted_iota(jnp.int32, (head, pix), 0)
    tail = jnp.where(line == 0, hi, jnp.where(line == 1, centre - hi, 0.0)).astype(BF)
    ds = (e.astype(F32) * mm(v_nt[h], jnp.concatenate([g, tail], axis=0))).astype(BF)
    gq_t[at, :] = (mm(k_t[at, :], ds) * factor).astype(BF)
    gq_t[rows(channels), :] = (mm(ds, q_nt[h]) * factor).T.astype(BF)
    gq_t[rows(2 * channels), :] = mm(e, g.T).T.astype(BF)


def kernel_attention(
    bits, sig_at, cls_at, stat_in, act2_ref, x_ref, cot_ref, w2_ref, wqkv_ref, wproj_ref,
    stat_ref, out_ref, outs_ref, hg_ref, gown_ref, gcore_ref, gsame_ref, gcross_ref, keep_ref, send_ref,
    act2, x, cot, w2, wqkv, wproj, wf, cat, wide, tall, q_nt, k_nt, v_nt, q_t, k_t, v_t, ga_t, at_t,
    gq_t, cot_t, out, sems,
):
    core = lax.axis_index("pipe")
    channels, pix = act2.shape
    head = channels // HEADS
    half = channels // 2
    loads = copies(
        [(act2_ref, act2), (w2_ref, w2), (x_ref.at[core], x), (wqkv_ref, wqkv),
         (cot_ref.at[core], cot), (wproj_ref, wproj)],
        sems,
    )
    stat = stat_in[...]
    col = lambda n: stat[:, n : n + 1]
    loads[0].wait()
    fill_cols(cat, act2[...].astype(F32), 1)
    loads[1].wait()
    fill_forward(wf, w2, channels)
    conv = conv_apply(wf, cat, 1, channels) + col(5)
    loads[2].wait()
    hidden = (x[...].astype(F32).T + conv).astype(BF).astype(F32)
    u3, inv3 = group_stats(hidden)
    normed = (u3 * col(6) + col(7)).astype(BF)
    loads[3].wait()
    projected = mm(wqkv[...], normed, TN)
    q_t[...] = (projected[:channels] + col(8)).astype(BF)
    k_t[...] = projected[channels : 2 * channels].astype(BF)
    v_t[...] = (projected[2 * channels :] + col(9)).astype(BF)
    loads[4].wait()
    cot_t[...] = cot[...].T
    loads[5].wait()
    ga_t[...] = mm(wproj[...], cot_t[...]).astype(BF)
    prepare_heads(q_t, k_t, v_t, q_nt, k_nt, v_nt, head)

    def two_heads(t, _):
        for n in range(2):
            one_head(2 * t + n, head, q_t, k_t, v_t, ga_t, q_nt, k_nt, v_nt, at_t, gq_t)
        return 0

    lax.fori_loop(0, HEADS // 2, two_heads, 0)
    out[...] = (hidden + mm(wproj[...], at_t[...], TN) + col(10)).T.astype(BF)
    rows = lambda c: pl.ds(pl.multiple_of(c * (pix // 2), pix // 2), pix // 2)
    stores = copies(
        [(out.at[rows(core)], out_ref.at[core]), (out.at[rows(1 - core)], outs_ref)], sems.at[6:8]
    )
    perm = row_matrix(channels, bits)
    got = mm(gq_t[...], normed, NT)
    tiles = channels // 128
    for t in range(tiles):
        wide[t] = got[:, t * 128 : (t + 1) * 128]
    for n in range(4):
        if n < 3:
            part = jnp.concatenate(
                [wide[t, pl.ds(n, channels, stride=3), :] for t in range(tiles)], axis=1
            )
        else:
            part = mm(cot_t[...], at_t[...], NT)
        part = mm(perm, part.astype(BF))
        at = slice(n * channels, (n + 1) * channels)
        keep_ref[:, at] = part[:half]
        send_ref[:, at] = part[half:].astype(BF)
    gn = mm(wqkv[...], gq_t[...])
    s3 = rowsum(gn)
    su3 = rowsum(gn * u3)
    cot_f = cot_t[...].astype(F32)
    hg = (cot_f + group_back(gn, u3, inv3, col(6), s3, su3)).astype(BF)
    hg_ref[...] = hg
    parts = mm(perm, hg).astype(BF)
    quarter = channels // 4
    for n, ref in enumerate((gown_ref, gsame_ref, gcore_ref, gcross_ref)):
        ref[...] = parts[n * quarter : (n + 1) * quarter]
    gq = gq_t[...].astype(F32)
    tall[:channels] = jnp.broadcast_to(rowsum(gq[:channels]), (channels, 128))
    tall[channels:] = jnp.broadcast_to(rowsum(gq[2 * channels :]), (channels, 128))
    side = with_columns(
        jnp.zeros((channels, 128), F32), 0,
        [su3, s3, tall[pl.ds(0, channels, stride=2), :], tall[pl.ds(1, channels, stride=2), :],
         rowsum(cot_f), rowsum(hg.astype(F32))],
    )
    side = exact_left(perm, side)
    keep_ref[:, 4 * channels : 4 * channels + 128] = side[:half]
    send_ref[:, 4 * channels : 4 * channels + 128] = side[half:].astype(BF)
    base = 4 * channels + 128
    total = (keep_ref.shape[1] - base) // 4
    sig = jnp.where(core == 0, sig_at[0], sig_at[1])
    cls = jnp.where(core == 0, cls_at[0], cls_at[1])
    lane = lanes((half, 4 * total))
    told = jnp.zeros((half, 4 * total), F32)
    for n, digit in enumerate((sig // 32, sig % 32, cls // 32, cls % 32)):
        told = jnp.where(lane == n * total + own_image(), digit.astype(F32), told)
    keep_ref[:, base:] = told
    send_ref[:, base:] = told.astype(BF)
    stat_ref[...] = stat
    for one in stores:
        one.wait()


def kernel_second(
    bits, hg, stat_in, w2_ref, u2_ref, wemb_ref,
    stat_ref, dc_ref, gown_ref, gcore_ref, gsame_ref, gcross_ref,
    wb, u2v, wemb, cat, tall, sems,
):
    channels = hg.shape[0]
    loads = copies(tap_pairs(w2_ref, wb, channels) + [(u2_ref, u2v), (wemb_ref, wemb)], sems)
    stat = stat_in[...]
    col = lambda n: stat[:, n : n + 1]
    g2, b2, scale, shift, inv2 = col(3), col(4), col(11), col(12), col(33)
    fill_cols(cat, hg[...].astype(F32), -1)
    for one in loads[:9]:
        one.wait()
    da = conv_apply(wb, cat, -1, channels)
    loads[9].wait()
    u2 = u2v[...]
    gm = g2 * (1.0 + scale)
    dm = da * silu_slope(u2 * gm + (b2 * (1.0 + scale) + shift))
    s = rowsum(dm)
    su = rowsum(dm * u2)
    dc = group_back(dm, u2, inv2, gm, s, su).astype(BF)
    dc_ref[...] = dc
    parts = mm(row_matrix(channels, bits), dc).astype(BF)
    quarter = channels // 4
    for n, ref in enumerate((gown_ref, gsame_ref, gcore_ref, gcross_ref)):
        ref[...] = parts[n * quarter : (n + 1) * quarter]
    tall[:channels] = jnp.broadcast_to(g2 * su + b2 * s, (channels, 128))
    tall[channels:] = jnp.broadcast_to(s, (channels, 128))
    ga = [tall[pl.ds(n, channels, stride=2), :] for n in range(2)]
    loads[10].wait()
    (ge,) = exact_columns(wemb[...], [tall[...][:, :1]])
    tall[:channels] = jnp.broadcast_to(ge[:channels] * silu_slope(col(13)), (channels, 128))
    tall[channels:] = jnp.broadcast_to(ge[channels:] * silu_slope(col(14)), (channels, 128))
    ge = [tall[pl.ds(n, channels, stride=2), :] for n in range(2)]
    stat = with_columns(
        stat, 40, [(1.0 + scale) * su, (1.0 + scale) * s, rowsum(dc.astype(F32))]
    )
    stat_ref[...] = with_columns(stat, 48, ga + ge)


def kernel_first(
    bits, dc, hg, stat_in, w1_ref, u1_ref,
    ig_ref, igs_ref, keep_ref, send_ref,
    wb, u1v, cat, ig, sems,
):
    core = lax.axis_index("pipe")
    channels, pix = hg.shape
    half = channels // 2
    loads = copies(tap_pairs(w1_ref, wb, channels) + [(u1_ref, u1v)], sems)
    stat = stat_in[...]
    col = lambda n: stat[:, n : n + 1]
    g1, b1, inv1 = col(0), col(1), col(32)
    fill_cols(cat, dc[...].astype(F32), -1)
    for one in loads[:9]:
        one.wait()
    da = conv_apply(wb, cat, -1, channels)
    loads[9].wait()
    u1 = u1v[...]
    dp = da * silu_slope(u1 * g1 + b1)
    s = rowsum(dp)
    su = rowsum(dp * u1)
    ig[...] = (hg[...].astype(F32) + group_back(dp, u1, inv1, g1, s, su)).T.astype(BF)
    rows = lambda c: pl.ds(pl.multiple_of(c * (pix // 2), pix // 2), pix // 2)
    stores = copies(
        [(ig.at[rows(core)], ig_ref.at[core]), (ig.at[rows(1 - core)], igs_ref)], sems.at[10:12]
    )
    width = keep_ref.shape[1]
    total = (width - 128) // 4
    side = with_columns(
        jnp.zeros((channels, width), F32), 0, [col(40), col(41), col(42), su, s]
    )
    lane = lanes((channels, width))
    for n in range(4):
        side = jnp.where(lane == 128 + n * total + own_image(), col(48 + n), side)
    side = exact_left(row_matrix(channels, bits), side)
    keep_ref[...] = side[:half]
    send_ref[...] = side[half:].astype(BF)
    for one in stores:
        one.wait()


def kernel_weight(*refs):
    acts, grads, rest = refs[:4], refs[4:8], refs[8:]
    extra = rest[:2] if len(rest) > 8 else None
    keep_ref, send_ref, act, grad, stack, total, sems = rest[len(rest) - 7 :]
    rows = grads[0].shape[0]
    channels = acts[0].shape[0]
    half = rows // 2
    loads = copies(
        [(ref, grad.at[n]) for n, ref in enumerate(grads)]
        + [(ref, act.at[n]) for n, ref in enumerate(acts)],
        sems,
    )
    for n in range(4):
        loads[n].wait()
        loads[4 + n].wait()
        g = grad[n].astype(F32)
        for j in range(3):
            moved = shift_cols(g, 1 - j)
            for i in range(3):
                at = (3 * i + j) * rows
                stack[n % 2, at : at + rows, :] = shift_rows(moved, 1 - i).astype(BF)
        got = mm(stack[n % 2], act[n], NT)
        total[...] = got if n == 0 else total[...] + got
    for tap in range(9):
        at = slice(tap * channels, (tap + 1) * channels)
        keep_ref[:, at] = total[tap * rows : tap * rows + half, :]
        send_ref[:, at] = total[tap * rows + half : (tap + 1) * rows, :].astype(BF)
    if extra is not None:
        more = extra[0][...] + extra[1][...].astype(F32)
        keep_ref[:, 9 * channels :] = more[:half]
        send_ref[:, 9 * channels :] = more[half:].astype(BF)


def interleave(ref, parts):
    size = parts[0].shape[0]
    for r in range(size):
        for n, part in enumerate(parts):
            at = len(parts) * r + n
            ref[at : at + 1, : part.shape[1]] = part[r : r + 1]


def kernel_last_two(
    channels, keep, got, sig_table, cls_table,
    conv_ref, qkv_ref, proj_ref, bconv_ref, gain_ref, bias_ref, bqv_ref, bproj_ref, emb_ref, told_ref,
    rows,
):
    total = keep[...] + got[...].astype(F32)
    size = total.shape[0]
    for i in range(3):
        for j in range(3):
            at = (3 * i + j) * channels
            conv_ref[i, j] = total[:, at : at + channels]
    rest = total[:, 9 * channels :]
    interleave(qkv_ref, [rest[:, n * channels : (n + 1) * channels] for n in range(3)])
    proj_ref[...] = rest[:, 3 * channels : 4 * channels]
    side = rest[:, 4 * channels : 4 * channels + 128]
    lines = side.T
    for n, ref in ((0, gain_ref), (1, bias_ref), (4, bproj_ref), (5, bconv_ref)):
        ref[...] = lines[n]
    interleave(rows, [jnp.broadcast_to(side[:, n : n + 1], (size, 128)) for n in (2, 3)])
    bqv_ref[...] = rows[...].T[0]
    told = rest[0:1, 4 * channels + 128 :]
    told_ref[...] = told
    images = told.shape[1] // 4
    hot_sig, hot_cls = hot_rows(told, images, sig_table.shape[0], cls_table.shape[0])
    emb = mm(hot_sig, sig_table[...], TN) + mm(hot_cls, cls_table[...], TN)
    emb_ref[...] = silu(emb).astype(BF)


def hot_rows(told, images, sig_count, cls_count):
    digit = lambda n: told[:, n * images : (n + 1) * images].astype(jnp.int32)
    sig = 32 * digit(0) + digit(1)
    cls = 32 * digit(2) + digit(3)

    def hot(index, count):
        line = lax.broadcasted_iota(jnp.int32, (count, images), 0)
        return jnp.where(line == index, 1.0, 0.0).astype(BF)

    return hot(sig, sig_count), hot(cls, cls_count)


def kernel_last_one(
    channels, keep, got, told_ref, emb_ref,
    conv_ref, gain2_ref, bias2_ref, bconv_ref, gain1_ref, bias1_ref, sig_ref, cls_ref, wemb_ref, bemb_ref,
    rows,
):
    total = keep[...] + got[...].astype(F32)
    for i in range(3):
        for j in range(3):
            at = (3 * i + j) * channels
            conv_ref[i, j] = total[:, at : at + channels]
    rest = total[:, 9 * channels :]
    lines = rest[:, :128].T
    for n, ref in enumerate((gain2_ref, bias2_ref, bconv_ref, gain1_ref, bias1_ref)):
        ref[...] = lines[n]
    told = told_ref[...]
    images = told.shape[1] // 4
    part = lambda n: rest[:, 128 + n * images : 128 + (n + 1) * images]
    hot_sig, hot_cls = hot_rows(told, images, sig_ref.shape[1], cls_ref.shape[1])
    into = [part(2), part(3)]
    interleave(sig_ref, [exact_right(v, hot_sig, NT) for v in into])
    interleave(cls_ref, [exact_right(v, hot_cls, NT) for v in into])
    affine = [part(0), part(1)]
    interleave(wemb_ref, [exact_right(v, emb_ref[...]) for v in affine])
    interleave(rows, [jnp.broadcast_to(rowsum(v), (v.shape[0], 128)) for v in affine])
    bemb_ref[...] = rows[...].T[0]


VM = pl.BlockSpec(memory_space=pltpu.VMEM)
ANY = pl.BlockSpec(memory_space=pl.ANY)
SM = pl.BlockSpec(memory_space=pltpu.SMEM)


def vmem(shape, dtype=BF):
    return pltpu.VMEM(shape, dtype)


def call(kernel, operands, outs, scratch, limit=56, flops=0, name=None):
    return pl.pallas_call(
        kernel,
        out_shape=[jax.ShapeDtypeStruct(shape, dtype) for shape, dtype, _ in outs],
        in_specs=[spec for _, spec in operands],
        out_specs=[spec for _, _, spec in outs],
        scratch_shapes=scratch,
        compiler_params=pltpu.CompilerParams(vmem_limit_bytes=limit * 2**20),
        cost_estimate=pl.CostEstimate(flops=flops, bytes_accessed=10**6, transcendentals=0),
        name=name,
    )(*[operand for operand, _ in operands])


def swap_core(v):
    return lax.ppermute(v, "pipe", [(0, 1), (1, 0)])


def joint(v, target):
    pairs = []
    for dp in range(lax.axis_size("dp")):
        for core in range(2):
            to_dp, to_core = target(dp, core)
            pairs.append((2 * dp + core, 2 * to_dp + to_core))
    return lax.ppermute(v, ("dp", "pipe"), pairs)


def exchange(v, step, bits):
    return joint(v, lambda dp, core: (dp ^ (1 << stream_order(core, bits)[step]), core))


def cross(v, bits):
    return joint(v, lambda dp, core: (dp ^ (1 << stream_order(1 - core, bits)[0]), 1 - core))


def parted(total):
    half = total.shape[0] // 2
    return total[:half], total[half:].astype(BF)


def gathered(own, to_core, to_same, to_cross, bits):
    return [own, swap_core(to_core), exchange(to_same, 0, bits), cross(to_cross, bits)]


def body(
    block_input, cotangent, sigma_index, class_label, sigma_table, class_table, w_emb, b_emb,
    norm1_gain, norm1_bias, w_conv1, b_conv1, norm2_gain, norm2_bias, w_conv2, b_conv2,
    norm3_gain, norm3_bias, w_qkv, b_qv, w_proj, b_proj,
):
    core = lax.axis_index("pipe")
    data = lax.axis_size("dp")
    bits = data.bit_length() - 1
    images, pix, c = block_input.shape
    total = 2 * data
    width = sigma_table.shape[1]
    head, half, quarter, size = c // HEADS, c // 2, c // 4, c // (2 * data)
    dma = lambda count: pltpu.SemaphoreType.DMA((count,))
    field = ((c, pix), BF)
    row_block = lambda index: pl.BlockSpec((16, width), index)
    whole = lambda shape: pl.BlockSpec(shape, lambda i, s, t: (0,) * len(shape))
    vectors = [b_emb, norm1_gain, norm1_bias, b_conv1, norm2_gain, norm2_bias, b_conv2, norm3_gain,
               norm3_bias, b_qv, b_proj]
    stat, act1, act2, u1, u2 = pl.pallas_call(
        kernel_start,
        out_shape=[jax.ShapeDtypeStruct(*v) for v in
                   [((c, 128), F32), field, field, ((c, pix), F32), ((c, pix), F32)]],
        grid_spec=pltpu.PrefetchScalarGridSpec(
            num_scalar_prefetch=2,
            grid=(1,),
            in_specs=[row_block(lambda i, s, t: (s[0] // 16, 0)),
                      row_block(lambda i, s, t: (s[1] // 16, 0)),
                      row_block(lambda i, s, t: (t[0] // 16, 0)),
                      row_block(lambda i, s, t: (t[1] // 16, 0))]
            + [whole(v.shape) for v in vectors] + [ANY] * 3,
            out_specs=[whole((c, 128))] + [ANY] * 4,
            scratch_shapes=[vmem((pix, c)), vmem(w_emb.shape), vmem(w_conv1.shape), vmem((c, pix)),
                            vmem((c, pix)), vmem((c, pix), F32), vmem((c, pix), F32),
                            vmem((3 * c, 3 * c)), vmem((3 * c, pix)), dma(7)],
        ),
        compiler_params=pltpu.CompilerParams(vmem_limit_bytes=56 * 2**20),
        cost_estimate=pl.CostEstimate(flops=8 * 10**9, bytes_accessed=10**7, transcendentals=0),
        name="start",
    )(sigma_index, class_label, sigma_table, sigma_table, class_table, class_table, *vectors,
      block_input, w_emb, w_conv1)
    acts1 = gathered(act1, act1, act1, act1, bits)
    acts2 = gathered(act2, act2, act2, act2, bits)
    told = 4 * total
    w0 = 4 * c + 128 + told
    nat = vmem((HEADS, pix, head))
    piece = ((quarter, pix), BF, VM)
    stat, out, out_send, hg, gown, gcore, gsame, gcross, keep0, send0 = call(
        lambda *refs: kernel_attention(bits, *refs),
        [(sigma_index, SM), (class_label, SM), (stat, VM), (act2, ANY), (block_input, ANY),
         (cotangent, ANY), (w_conv2, ANY), (w_qkv, ANY), (w_proj, ANY)],
        [((c, 128), F32, VM), ((images, pix // 2, c), BF, ANY), ((pix // 2, c), BF, ANY),
         field + (VM,), piece, piece, piece, piece, ((half, w0), F32, VM), ((half, w0), BF, VM)],
        [vmem((c, pix)), vmem((pix, c)), vmem((pix, c)), vmem(w_conv2.shape), vmem(w_qkv.shape),
         vmem(w_proj.shape), vmem((3 * c, 3 * c)), vmem((3 * c, pix)),
         vmem((c // 128, 3 * c, 128), F32), vmem((2 * c, 128), F32), nat, nat,
         vmem((HEADS, pix, 2 * head)), vmem((c, pix)), vmem((c, pix)), vmem((c, pix)),
         vmem((c, pix)), vmem((c, pix)), vmem((3 * c, pix)), vmem((c, pix)), vmem((pix, c)), dma(8)],
        limit=60, flops=40 * 10**9, name="attention",
    )
    keep, send = parted(keep0 + swap_core(send0).astype(F32))
    extra = [keep, exchange(send, 0, bits)]
    grads2 = gathered(gown, gcore, gsame, gcross, bits)
    out_got = swap_core(out_send)
    stat, dc, gown, gcore, gsame, gcross = call(
        lambda *refs: kernel_second(bits, *refs),
        [(hg, VM), (stat, VM), (w_conv2, ANY), (u2, ANY), (w_emb, ANY)],
        [((c, 128), F32, VM), field + (VM,), piece, piece, piece, piece],
        [vmem((3 * c, 3 * c)), vmem((c, pix), F32), vmem(w_emb.shape), vmem((3 * c, pix)),
         vmem((2 * c, 128), F32), dma(11)],
        flops=5 * 10**9, name="second",
    )
    grads1 = gathered(gown, gcore, gsame, gcross, bits)

    def weight(acts, grads, more, name):
        columns = 9 * c + (more[0].shape[1] if more else 0)
        return call(
            kernel_weight,
            [(v, ANY) for v in acts + grads] + [(v, VM) for v in more],
            [((quarter // 2, columns), F32, VM), ((quarter // 2, columns), BF, VM)],
            [vmem((4, c, pix)), vmem((4, quarter, pix)), vmem((2, 9 * quarter, pix)),
             vmem((9 * quarter, c), F32), dma(8)],
            flops=5 * 10**9, name=name,
        )

    keep2, send2 = weight(acts2, grads2, extra, "weight_two")
    ig, ig_send, keepv, sendv = call(
        lambda *refs: kernel_first(bits, *refs),
        [(dc, VM), (hg, VM), (stat, VM), (w_conv1, ANY), (u1, ANY)],
        [((images, pix // 2, c), BF, ANY), ((pix // 2, c), BF, ANY),
         ((half, 128 + told), F32, VM), ((half, 128 + told), BF, VM)],
        [vmem((3 * c, 3 * c)), vmem((c, pix), F32), vmem((3 * c, pix)), vmem((pix, c)), dma(12)],
        flops=5 * 10**9, name="first",
    )
    keep1, send1 = weight(acts1, grads1, [], "weight_one")
    total_v = keepv + swap_core(sendv).astype(F32)
    for step in range(2):
        keep, send = parted(total_v)
        total_v = keep + exchange(send, step, bits).astype(F32)
    for step in range(1, bits):
        got2 = exchange(send2, step, bits)
        if step < bits - 1:
            keep2, send2 = parted(keep2 + got2.astype(F32))
    for step in range(1, bits):
        got1 = exchange(send1, step, bits)
        if step < bits - 1:
            sum1 = keep1 + got1.astype(F32)
            if step == 1:
                sum1 = jnp.concatenate([sum1, total_v], axis=1)
            keep1, send1 = parted(sum1)
    line = lambda n: ((n,), F32, VM)
    conv = ((3, 3, size, c), F32, VM)
    g_conv2, g_qkv, g_proj, g_bconv2, g_gain3, g_bias3, g_bqv, g_bproj, emb, index = call(
        lambda *refs: kernel_last_two(c, *refs),
        [(keep2, VM), (got2, VM), (sigma_table, VM), (class_table, VM)],
        [conv, ((3 * size, c), F32, VM), ((size, c), F32, VM), line(size), line(size), line(size),
         line(2 * size), line(size), ((total, width), BF, VM), ((1, told), F32, VM)],
        [vmem((2 * size, 128), F32)], name="last_two",
    )
    tables = lambda count: ((2 * size, count), F32, VM)
    (g_conv1, g_gain2, g_bias2, g_bconv1, g_gain1, g_bias1, g_sigma, g_class, g_wemb, g_bemb) = call(
        lambda *refs: kernel_last_one(c, *refs),
        [(keep1, VM), (got1, VM), (index, VM), (emb, VM)],
        [conv] + [line(size)] * 5
        + [tables(sigma_table.shape[0]), tables(class_table.shape[0]), tables(width), line(2 * size)],
        [vmem((2 * size, 128), F32)], name="last_one",
    )
    other = lambda full, got: lax.dynamic_update_slice(full, got[None], (1 - core, 0, 0))
    output = other(out, out_got)
    input_grad = other(ig, swap_core(ig_send))
    place = lambda v: jnp.transpose(v, (0, 1, 3, 2))
    return (
        output, input_grad, g_sigma.T, g_class.T, g_wemb.T, g_bemb, g_gain1, g_bias1, place(g_conv1),
        g_bconv1, g_gain2, g_bias2, place(g_conv2), g_bconv2, g_gain3, g_bias3, g_qkv.T, g_bqv,
        g_proj.T, g_bproj,
    )


def solution(mesh):
    every = ("dp", "pipe")
    return jax.shard_map(
        body,
        mesh=mesh,
        in_specs=(P("dp", None, None), P("dp", None, None), P("dp"), P("dp")) + (P(),) * 18,
        out_specs=(
            P("dp", "pipe", None), P("dp", "pipe", None), P(None, every), P(None, every),
            P(None, every), P(every), P(every), P(every), P(None, None, None, every), P(every),
            P(every), P(every), P(None, None, None, every), P(every), P(every), P(every),
            P(None, every), P(every), P(None, every), P(every),
        ),
        check_vma=False,
    )
```

```python
import jax
import jax.numpy as jnp
from jax import lax
from jax.experimental import pallas as pl
from jax.experimental.pallas import tpu as pltpu
from jax.sharding import PartitionSpec as P

HEADS = 6
GROUPS = 32
SIDE = 32
EPS = 1e-05
LOG2E = 1.4426950408889634
BF = jnp.bfloat16
F32 = jnp.float32
NN = (((1,), (0,)), ((), ()))
NT = (((1,), (1,)), ((), ()))
TN = (((0,), (0,)), ((), ()))


def mm(a, b, dims=NN):
    return lax.dot_general(a, b, dims, preferred_element_type=F32)


def silu(v):
    return v * jax.nn.sigmoid(v)


def silu_slope(v):
    s = jax.nn.sigmoid(v)
    return s * (1.0 + v * (1.0 - s))


def lanes(shape):
    return lax.broadcasted_iota(jnp.int32, shape, 1)


def rowsum(v):
    return jnp.sum(v, axis=1, keepdims=True)


def shift_cols(a, d):
    if d == 0:
        return a
    n = a.shape[1]
    col = lanes(a.shape) & (SIDE - 1)
    ok = (col + d >= 0) & (col + d < SIDE)
    return jnp.where(ok, pltpu.roll(a, (-d) % n, 1), 0)


def shift_rows(a, d):
    if d == 0:
        return a
    n = a.shape[1]
    at = lanes(a.shape) + SIDE * d
    return jnp.where((at >= 0) & (at < n), pltpu.roll(a, (-SIDE * d) % n, 1), 0)


def split3(v):
    hi = v.astype(BF).astype(F32)
    mid = (v - hi).astype(BF).astype(F32)
    return hi, mid, v - hi - mid


def exact_left(matrix, v, dims=NN):
    return sum(mm(matrix, part.astype(BF), dims) for part in split3(v))


def exact_right(v, matrix, dims=NN):
    return sum(mm(part.astype(BF), matrix, dims) for part in split3(v))


def with_columns(block, start, extra):
    lane = lanes(block.shape)
    for n, c in enumerate(extra):
        block = jnp.where(lane == start + n, c, block)
    return block


def exact_columns(matrix, cols):
    parts = [part for col in cols for part in split3(col)]
    block = with_columns(jnp.zeros((cols[0].shape[0], 128), F32), 0, parts)
    got = mm(matrix, block.astype(BF))
    return [rowsum(got[:, 3 * at : 3 * at + 3]) for at in range(len(cols))]


def divide(v, size, top):
    scale = -(-(1 << 19) // size)
    assert all((n * scale) >> 19 == n // size for n in range(top))
    return (v * scale) >> 19


def group_matrix(channels):
    size = channels // GROUPS
    shape = (channels, channels)
    row = divide(lax.broadcasted_iota(jnp.int32, (channels, 1), 0), size, channels)
    col = divide(lax.broadcasted_iota(jnp.int32, (1, channels), 1), size, channels)
    return jnp.where(row == col, 1.0, jnp.zeros(shape, F32)).astype(BF)


def group_means(cols, pixels):
    channels = cols[0].shape[0]
    count = channels // GROUPS * pixels
    return [got * (1.0 / count) for got in exact_columns(group_matrix(channels), cols)]


def group_stats(v):
    pixels = v.shape[1]
    (mean,) = group_means([rowsum(v)], pixels)
    centred = v - mean
    (var,) = group_means([rowsum(centred * centred)], pixels)
    inverse = lax.rsqrt(var + EPS)
    return centred * inverse, inverse


def group_back(t, u, inverse, gain, sum_t, sum_tu):
    first, second = group_means([gain * sum_t, gain * sum_tu], t.shape[1])
    return (inverse * gain) * t - inverse * first - u * (inverse * second)


def fill_cols(ref, a, sign):
    c = a.shape[0]
    for j in range(3):
        ref[j * c : (j + 1) * c, :] = shift_cols(a, sign * (j - 1)).astype(BF)


def conv_apply(w_ref, cat_ref, sign, channels):
    total = None
    for i in range(3):
        y = mm(w_ref[i * channels : (i + 1) * channels, :], cat_ref[...])
        y = shift_rows(y, sign * (i - 1))
        total = y if total is None else total + y
    return total


def fill_forward(wf, w_ref, channels):
    for i in range(3):
        for j in range(3):
            at = (slice(i * channels, (i + 1) * channels), slice(j * channels, (j + 1) * channels))
            wf[at] = w_ref[i, j].T


def copies(pairs, sems):
    made = [pltpu.make_async_copy(src, dst, sems.at[n]) for n, (src, dst) in enumerate(pairs)]
    for one in made:
        one.start()
    return made


def tap_pairs(w_ref, wb, channels):
    return [
        (
            w_ref.at[i, j],
            wb.at[
                i * channels : (i + 1) * channels, j * channels : (j + 1) * channels
            ],
        )
        for i in range(3)
        for j in range(3)
    ]


def stream_order(core, bits):
    order = list(range(bits))
    if core:
        for at in range(0, bits - 1, 2):
            order[at], order[at + 1] = order[at + 1], order[at]
    return order


def row_matrix(channels, bits):
    dp, core = lax.axis_index("dp"), lax.axis_index("pipe")
    size = channels // (2 << bits)
    quarter = channels // 4
    row = lax.broadcasted_iota(jnp.int32, (channels, 1), 0)
    part_of = sum(jnp.where(row >= quarter * n, 1, 0) for n in (1, 2, 3))
    rest = row - part_of * quarter
    at = divide(rest, size, quarter)
    within = rest - at * size
    part = jnp.where(part_of < 2, core, 1 - core)
    flips = []
    for p in (0, 1):
        order = stream_order(p, bits)
        flip = (part_of & 1) << order[0]
        for t in range(bits - 1):
            flip = flip | (((at >> (bits - 2 - t)) & 1) << order[t + 1])
        flips.append(flip)
    peer = dp ^ jnp.where(part == 0, flips[0], flips[1])
    wanted = (2 * peer + part) * size + within
    shape = (channels, channels)
    return jnp.where(wanted == lanes((1, channels)), 1.0, jnp.zeros(shape, F32)).astype(BF)


def own_image():
    return 2 * lax.axis_index("dp") + lax.axis_index("pipe")


def kernel_start(
    sig_at, cls_at, sig0, sig1, cls0, cls1, bemb, g1, b1, bc1, g2, b2, bc2, g3, b3, bqv, bp,
    x_ref, wemb_ref, w1_ref,
    stat_ref, acts_ref, u1_ref, u2_ref,
    x, wemb, w1, act1, act2, u1, u2, wf, cat, sems,
):
    core = lax.axis_index("pipe")
    channels = x.shape[1]
    loads = copies([(x_ref.at[core], x), (wemb_ref, wemb), (w1_ref, w1)], sems)
    row16 = lax.broadcasted_iota(jnp.int32, sig0.shape, 0)

    def table_row(at, first, second):
        block = jnp.where(core == 0, first[...].astype(F32), second[...].astype(F32))
        found = jnp.where(core == 0, at[0], at[1])
        return jnp.sum(jnp.where(row16 == found % 16, block, 0.0), axis=0, keepdims=True)

    emb = table_row(sig_at, sig0, sig1) + table_row(cls_at, cls0, cls1)
    flat = lambda ref: ref[...].astype(F32).reshape(1, ref.shape[0])
    bqv_row = flat(bqv)
    rows = [flat(ref) for ref in (g1, b1, bc1, g2, b2, bc2, g3, b3)]
    rows += [bqv_row[:, :channels], bqv_row[:, channels:], flat(bp)]
    prm = jnp.zeros((128, channels), F32)
    at = lax.broadcasted_iota(jnp.int32, prm.shape, 0)
    loads[0].wait()
    loads[1].wait()
    low = jnp.broadcast_to(silu(emb), (16, emb.shape[1])).astype(BF)
    affine = mm(low, wemb[...])[0:1] + flat(bemb)
    rows += [affine[:, :channels], affine[:, channels:], emb[:, :channels], emb[:, channels:]]
    for n, line in enumerate(rows):
        prm = jnp.where(at == n, line, prm)
    stat = prm.T
    col = lambda n: stat[:, n : n + 1]
    v1, inv1 = group_stats(x[...].astype(F32).T)
    u1[...] = v1
    a1 = silu(v1 * col(0) + col(1))
    act1[...] = a1.astype(BF)
    stores = copies([(u1, u1_ref), (act1, acts_ref.at[0])], sems.at[3:5])
    fill_cols(cat, a1, 1)
    loads[2].wait()
    fill_forward(wf, w1, channels)
    v2, inv2 = group_stats(conv_apply(wf, cat, 1, channels) + col(2))
    u2[...] = v2
    scale, shift = col(11), col(12)
    a2 = silu(v2 * (col(3) * (1.0 + scale)) + (col(4) * (1.0 + scale) + shift))
    act2[...] = a2.astype(BF)
    stores += copies([(u2, u2_ref), (act2, acts_ref.at[1])], sems.at[5:7])
    stat_ref[...] = with_columns(stat, 32, [inv1, inv2])
    for one in stores:
        one.wait()


def prepare_heads(q_t, k_t, v_t, q_nt, k_nt, v_nt, head):
    pix = q_t.shape[1]
    ones = jnp.where(lanes((pix, head)) < 2, 1.0, 0.0).astype(BF)
    for h in range(HEADS):
        at = slice(h * head, (h + 1) * head)
        q_nt[h] = q_t[at, :].T
        k_nt[h] = k_t[at, :].T
        v_nt[h, :, :head] = v_t[at, :].T
        v_nt[h, :, head:] = ones


def one_head(h, head, q_t, k_t, v_t, ga_t, q_nt, k_nt, v_nt, at_t, gq_t):
    channels, pix = q_t.shape
    factor = head ** (-0.5)
    rows = lambda base: pl.ds(pl.multiple_of(base + h * head, head), head)
    at = rows(0)
    s = mm(k_nt[h], q_t[at, :])
    top = jnp.max(s, axis=0, keepdims=True)
    e = jnp.exp2((s - top) * (factor * LOG2E)).astype(BF)
    o = mm(jnp.concatenate([v_t[at, :], jnp.ones((16, pix), BF)], axis=0), e)
    inv = 1.0 / o[head : head + 1]
    o = o[:head] * inv
    at_t[at, :] = o.astype(BF)
    g = ga_t[at, :].astype(F32)
    centre = -jnp.sum(g * o, axis=0, keepdims=True) * inv
    g = (g * inv).astype(BF)
    hi = centre.astype(BF).astype(F32)
    line = lax.broadcasted_iota(jnp.int32, (head, pix), 0)
    tail = jnp.where(line == 0, hi, jnp.where(line == 1, centre - hi, 0.0)).astype(BF)
    ds = (e.astype(F32) * mm(v_nt[h], jnp.concatenate([g, tail], axis=0))).astype(BF)
    gq_t[at, :] = (mm(k_t[at, :], ds) * factor).astype(BF)
    gq_t[rows(channels), :] = (mm(ds, q_nt[h]) * factor).T.astype(BF)
    gq_t[rows(2 * channels), :] = mm(e, g.T).T.astype(BF)


def kernel_attention(
    bits, sig_at, cls_at, stat_in, acts_ref, x_ref, cot_ref, w2_ref, wqkv_ref, wproj_ref,
    stat_ref, out_ref, outs_ref, hg_ref, gown_ref, gcore_ref, gsame_ref, gcross_ref, keep_ref, send_ref,
    act2, x, cot, w2, wqkv, wproj, wf, cat, wide, tall, q_nt, k_nt, v_nt, q_t, k_t, v_t, ga_t, at_t,
    gq_t, cot_t, out, sems,
):
    core = lax.axis_index("pipe")
    channels, pix = act2.shape
    head = channels // HEADS
    half = channels // 2
    loads = copies(
        [(acts_ref.at[1], act2), (w2_ref, w2), (x_ref.at[core], x), (wqkv_ref, wqkv),
         (cot_ref.at[core], cot), (wproj_ref, wproj)],
        sems,
    )
    stat = stat_in[...]
    col = lambda n: stat[:, n : n + 1]
    loads[0].wait()
    fill_cols(cat, act2[...].astype(F32), 1)
    loads[1].wait()
    fill_forward(wf, w2, channels)
    conv = conv_apply(wf, cat, 1, channels) + col(5)
    loads[2].wait()
    hidden = (x[...].astype(F32).T + conv).astype(BF).astype(F32)
    u3, inv3 = group_stats(hidden)
    normed = (u3 * col(6) + col(7)).astype(BF)
    loads[3].wait()
    projected = mm(wqkv[...], normed, TN)
    q_t[...] = (projected[:channels] + col(8)).astype(BF)
    k_t[...] = projected[channels : 2 * channels].astype(BF)
    v_t[...] = (projected[2 * channels :] + col(9)).astype(BF)
    loads[4].wait()
    cot_t[...] = cot[...].T
    loads[5].wait()
    ga_t[...] = mm(wproj[...], cot_t[...]).astype(BF)
    prepare_heads(q_t, k_t, v_t, q_nt, k_nt, v_nt, head)

    def two_heads(t, _):
        for n in range(2):
            one_head(2 * t + n, head, q_t, k_t, v_t, ga_t, q_nt, k_nt, v_nt, at_t, gq_t)
        return 0

    lax.fori_loop(0, HEADS // 2, two_heads, 0)
    out[...] = (hidden + mm(wproj[...], at_t[...], TN) + col(10)).T.astype(BF)
    rows = lambda c: pl.ds(pl.multiple_of(c * (pix // 2), pix // 2), pix // 2)
    stores = copies(
        [(out.at[rows(core)], out_ref.at[core]), (out.at[rows(1 - core)], outs_ref)], sems.at[6:8]
    )
    perm = row_matrix(channels, bits)
    got = mm(gq_t[...], normed, NT)
    tiles = channels // 128
    for t in range(tiles):
        wide[t] = got[:, t * 128 : (t + 1) * 128]
    for n in range(4):
        if n < 3:
            part = jnp.concatenate(
                [wide[t, pl.ds(n, channels, stride=3), :] for t in range(tiles)], axis=1
            )
        else:
            part = mm(cot_t[...], at_t[...], NT)
        part = mm(perm, part.astype(BF))
        at = slice(n * channels, (n + 1) * channels)
        keep_ref[:, at] = part[:half]
        send_ref[:, at] = part[half:].astype(BF)
    gn = mm(wqkv[...], gq_t[...])
    s3 = rowsum(gn)
    su3 = rowsum(gn * u3)
    cot_f = cot_t[...].astype(F32)
    hg = (cot_f + group_back(gn, u3, inv3, col(6), s3, su3)).astype(BF)
    hg_ref[...] = hg
    parts = mm(perm, hg).astype(BF)
    quarter = channels // 4
    for n, ref in enumerate((gown_ref, gsame_ref, gcore_ref, gcross_ref)):
        ref[...] = parts[n * quarter : (n + 1) * quarter]
    gq = gq_t[...].astype(F32)
    tall[:channels] = jnp.broadcast_to(rowsum(gq[:channels]), (channels, 128))
    tall[channels:] = jnp.broadcast_to(rowsum(gq[2 * channels :]), (channels, 128))
    side = with_columns(
        jnp.zeros((channels, 128), F32), 0,
        [su3, s3, tall[pl.ds(0, channels, stride=2), :], tall[pl.ds(1, channels, stride=2), :],
         rowsum(cot_f), rowsum(hg.astype(F32))],
    )
    side = exact_left(perm, side)
    keep_ref[:, 4 * channels : 4 * channels + 128] = side[:half]
    send_ref[:, 4 * channels : 4 * channels + 128] = side[half:].astype(BF)
    base = 4 * channels + 128
    total = (keep_ref.shape[1] - base) // 4
    sig = jnp.where(core == 0, sig_at[0], sig_at[1])
    cls = jnp.where(core == 0, cls_at[0], cls_at[1])
    lane = lanes((half, 4 * total))
    told = jnp.zeros((half, 4 * total), F32)
    for n, digit in enumerate((sig // 32, sig % 32, cls // 32, cls % 32)):
        told = jnp.where(lane == n * total + own_image(), digit.astype(F32), told)
    keep_ref[:, base:] = told
    send_ref[:, base:] = told.astype(BF)
    stat_ref[...] = stat
    for one in stores:
        one.wait()


def kernel_second(
    bits, hg, stat_in, w2_ref, u2_ref, wemb_ref,
    stat_ref, dc_ref, gown_ref, gcore_ref, gsame_ref, gcross_ref,
    wb, u2v, wemb, cat, tall, sems,
):
    channels = hg.shape[0]
    loads = copies(tap_pairs(w2_ref, wb, channels) + [(u2_ref, u2v), (wemb_ref, wemb)], sems)
    stat = stat_in[...]
    col = lambda n: stat[:, n : n + 1]
    g2, b2, scale, shift, inv2 = col(3), col(4), col(11), col(12), col(33)
    fill_cols(cat, hg[...].astype(F32), -1)
    for one in loads[:9]:
        one.wait()
    da = conv_apply(wb, cat, -1, channels)
    loads[9].wait()
    u2 = u2v[...]
    gm = g2 * (1.0 + scale)
    dm = da * silu_slope(u2 * gm + (b2 * (1.0 + scale) + shift))
    s = rowsum(dm)
    su = rowsum(dm * u2)
    dc = group_back(dm, u2, inv2, gm, s, su).astype(BF)
    dc_ref[...] = dc
    parts = mm(row_matrix(channels, bits), dc).astype(BF)
    quarter = channels // 4
    for n, ref in enumerate((gown_ref, gsame_ref, gcore_ref, gcross_ref)):
        ref[...] = parts[n * quarter : (n + 1) * quarter]
    tall[:channels] = jnp.broadcast_to(g2 * su + b2 * s, (channels, 128))
    tall[channels:] = jnp.broadcast_to(s, (channels, 128))
    ga = [tall[pl.ds(n, channels, stride=2), :] for n in range(2)]
    loads[10].wait()
    (ge,) = exact_columns(wemb[...], [tall[...][:, :1]])
    tall[:channels] = jnp.broadcast_to(ge[:channels] * silu_slope(col(13)), (channels, 128))
    tall[channels:] = jnp.broadcast_to(ge[channels:] * silu_slope(col(14)), (channels, 128))
    ge = [tall[pl.ds(n, channels, stride=2), :] for n in range(2)]
    stat = with_columns(
        stat, 40, [(1.0 + scale) * su, (1.0 + scale) * s, rowsum(dc.astype(F32))]
    )
    stat_ref[...] = with_columns(stat, 48, ga + ge)


def kernel_first(
    bits, dc, hg, stat_in, w1_ref, u1_ref,
    ig_ref, igs_ref, keep_ref, send_ref,
    wb, u1v, cat, ig, sems,
):
    core = lax.axis_index("pipe")
    channels, pix = hg.shape
    half = channels // 2
    loads = copies(tap_pairs(w1_ref, wb, channels) + [(u1_ref, u1v)], sems)
    stat = stat_in[...]
    col = lambda n: stat[:, n : n + 1]
    g1, b1, inv1 = col(0), col(1), col(32)
    fill_cols(cat, dc[...].astype(F32), -1)
    for one in loads[:9]:
        one.wait()
    da = conv_apply(wb, cat, -1, channels)
    loads[9].wait()
    u1 = u1v[...]
    dp = da * silu_slope(u1 * g1 + b1)
    s = rowsum(dp)
    su = rowsum(dp * u1)
    ig[...] = (hg[...].astype(F32) + group_back(dp, u1, inv1, g1, s, su)).T.astype(BF)
    rows = lambda c: pl.ds(pl.multiple_of(c * (pix // 2), pix // 2), pix // 2)
    stores = copies(
        [(ig.at[rows(core)], ig_ref.at[core]), (ig.at[rows(1 - core)], igs_ref)], sems.at[10:12]
    )
    width = keep_ref.shape[1]
    total = (width - 128) // 4
    side = with_columns(
        jnp.zeros((channels, width), F32), 0, [col(40), col(41), col(42), su, s]
    )
    lane = lanes((channels, width))
    for n in range(4):
        side = jnp.where(lane == 128 + n * total + own_image(), col(48 + n), side)
    side = exact_left(row_matrix(channels, bits), side)
    keep_ref[...] = side[:half]
    send_ref[...] = side[half:].astype(BF)
    for one in stores:
        one.wait()


def kernel_weight(which, *refs):
    acts, grads, rest = refs[:4], refs[4:8], refs[8:]
    keep_ref, send_ref, act, grad, stack, total, sems = rest[len(rest) - 7 :]
    rows = grads[0].shape[0]
    channels = act.shape[1]
    half = rows // 2
    loads = copies(
        [(ref, grad.at[n]) for n, ref in enumerate(grads)]
        + [(ref.at[which], act.at[n]) for n, ref in enumerate(acts)],
        sems,
    )
    for n in range(4):
        loads[n].wait()
        loads[4 + n].wait()
        g = grad[n].astype(F32)
        for j in range(3):
            moved = shift_cols(g, 1 - j)
            for i in range(3):
                at = (3 * i + j) * rows
                stack[n % 2, at : at + rows, :] = shift_rows(moved, 1 - i).astype(BF)
        got = mm(stack[n % 2], act[n], NT)
        total[...] = got if n == 0 else total[...] + got
    for tap in range(9):
        at = slice(tap * channels, (tap + 1) * channels)
        keep_ref[:, at] = total[tap * rows : tap * rows + half, :]
        send_ref[:, at] = total[tap * rows + half : (tap + 1) * rows, :].astype(BF)


def interleave(ref, parts):
    size = parts[0].shape[0]
    for r in range(size):
        for n, part in enumerate(parts):
            at = len(parts) * r + n
            ref[at : at + 1, : part.shape[1]] = part[r : r + 1]


def kernel_last_two(
    channels, keep, got, sig_table, cls_table,
    conv_ref, qkv_ref, proj_ref, bconv_ref, gain_ref, bias_ref, bqv_ref, bproj_ref, emb_ref, told_ref,
    rows,
):
    total = keep[...] + got[...].astype(F32)
    size = total.shape[0]
    for i in range(3):
        for j in range(3):
            at = (3 * i + j) * channels
            conv_ref[i, j] = total[:, at : at + channels]
    rest = total[:, 9 * channels :]
    interleave(qkv_ref, [rest[:, n * channels : (n + 1) * channels] for n in range(3)])
    proj_ref[...] = rest[:, 3 * channels : 4 * channels]
    side = rest[:, 4 * channels : 4 * channels + 128]
    lines = side.T
    for n, ref in ((0, gain_ref), (1, bias_ref), (4, bproj_ref), (5, bconv_ref)):
        ref[...] = lines[n]
    interleave(rows, [jnp.broadcast_to(side[:, n : n + 1], (size, 128)) for n in (2, 3)])
    bqv_ref[...] = rows[...].T[0]
    told = rest[0:1, 4 * channels + 128 :]
    told_ref[...] = told
    images = told.shape[1] // 4
    hot_sig, hot_cls = hot_rows(told, images, sig_table.shape[0], cls_table.shape[0])
    emb = mm(hot_sig, sig_table[...], TN) + mm(hot_cls, cls_table[...], TN)
    emb_ref[...] = silu(emb).astype(BF)


def hot_rows(told, images, sig_count, cls_count):
    digit = lambda n: told[:, n * images : (n + 1) * images].astype(jnp.int32)
    sig = 32 * digit(0) + digit(1)
    cls = 32 * digit(2) + digit(3)

    def hot(index, count):
        line = lax.broadcasted_iota(jnp.int32, (count, images), 0)
        return jnp.where(line == index, 1.0, 0.0).astype(BF)

    return hot(sig, sig_count), hot(cls, cls_count)


def kernel_last_one(
    channels, keep, got, keepv, gotv, told_ref, emb_ref,
    conv_ref, gain2_ref, bias2_ref, bconv_ref, gain1_ref, bias1_ref, sig_ref, cls_ref, wemb_ref, bemb_ref,
    rows,
):
    total = keep[...] + got[...].astype(F32)
    for i in range(3):
        for j in range(3):
            at = (3 * i + j) * channels
            conv_ref[i, j] = total[:, at : at + channels]
    rest = keepv[...] + gotv[...].astype(F32)
    lines = rest[:, :128].T
    for n, ref in enumerate((gain2_ref, bias2_ref, bconv_ref, gain1_ref, bias1_ref)):
        ref[...] = lines[n]
    told = told_ref[...]
    images = told.shape[1] // 4
    part = lambda n: rest[:, 128 + n * images : 128 + (n + 1) * images]
    hot_sig, hot_cls = hot_rows(told, images, sig_ref.shape[1], cls_ref.shape[1])
    into = [part(2), part(3)]
    interleave(sig_ref, [exact_right(v, hot_sig, NT) for v in into])
    interleave(cls_ref, [exact_right(v, hot_cls, NT) for v in into])
    affine = [part(0), part(1)]
    interleave(wemb_ref, [exact_right(v, emb_ref[...]) for v in affine])
    interleave(rows, [jnp.broadcast_to(rowsum(v), (v.shape[0], 128)) for v in affine])
    bemb_ref[...] = rows[...].T[0]


VM = pl.BlockSpec(memory_space=pltpu.VMEM)
ANY = pl.BlockSpec(memory_space=pl.ANY)
SM = pl.BlockSpec(memory_space=pltpu.SMEM)


def vmem(shape, dtype=BF):
    return pltpu.VMEM(shape, dtype)


def call(kernel, operands, outs, scratch, after=(), limit=56, flops=0, name=None):
    count = len(operands)
    operands = list(operands) + [(v, ANY) for v in after]

    def ordered(*refs):
        kernel(*refs[:count], *refs[len(operands) :])

    return pl.pallas_call(
        ordered,
        out_shape=[jax.ShapeDtypeStruct(shape, dtype) for shape, dtype, _ in outs],
        in_specs=[spec for _, spec in operands],
        out_specs=[spec for _, _, spec in outs],
        scratch_shapes=scratch,
        compiler_params=pltpu.CompilerParams(vmem_limit_bytes=limit * 2**20),
        cost_estimate=pl.CostEstimate(flops=flops, bytes_accessed=10**6, transcendentals=0),
        name=name,
    )(*[operand for operand, _ in operands])


def swap_core(v):
    return lax.ppermute(v, "pipe", [(0, 1), (1, 0)])


def joint(v, target):
    pairs = []
    for dp in range(lax.axis_size("dp")):
        for core in range(2):
            to_dp, to_core = target(dp, core)
            pairs.append((2 * dp + core, 2 * to_dp + to_core))
    return lax.ppermute(v, ("dp", "pipe"), pairs)


def exchange(v, step, bits):
    return joint(v, lambda dp, core: (dp ^ (1 << stream_order(core, bits)[step]), core))


def cross(v, bits):
    return joint(v, lambda dp, core: (dp ^ (1 << stream_order(1 - core, bits)[0]), 1 - core))


def parted(total):
    half = total.shape[0] // 2
    return total[:half], total[half:].astype(BF)


def gathered(own, to_core, to_same, to_cross, bits):
    return [own, swap_core(to_core), exchange(to_same, 0, bits), cross(to_cross, bits)]


def body(
    block_input, cotangent, sigma_index, class_label, sigma_table, class_table, w_emb, b_emb,
    norm1_gain, norm1_bias, w_conv1, b_conv1, norm2_gain, norm2_bias, w_conv2, b_conv2,
    norm3_gain, norm3_bias, w_qkv, b_qv, w_proj, b_proj,
):
    core = lax.axis_index("pipe")
    data = lax.axis_size("dp")
    bits = data.bit_length() - 1
    images, pix, c = block_input.shape
    total = 2 * data
    width = sigma_table.shape[1]
    head, half, quarter, size = c // HEADS, c // 2, c // 4, c // (2 * data)
    dma = lambda count: pltpu.SemaphoreType.DMA((count,))
    field = ((c, pix), BF)
    row_block = lambda index: pl.BlockSpec((16, width), index)
    whole = lambda shape: pl.BlockSpec(shape, lambda i, s, t: (0,) * len(shape))
    vectors = [b_emb, norm1_gain, norm1_bias, b_conv1, norm2_gain, norm2_bias, b_conv2, norm3_gain,
               norm3_bias, b_qv, b_proj]
    stat, acts, u1, u2 = pl.pallas_call(
        kernel_start,
        out_shape=[jax.ShapeDtypeStruct(*v) for v in
                   [((c, 128), F32), ((2, c, pix), BF), ((c, pix), F32), ((c, pix), F32)]],
        grid_spec=pltpu.PrefetchScalarGridSpec(
            num_scalar_prefetch=2,
            grid=(1,),
            in_specs=[row_block(lambda i, s, t: (s[0] // 16, 0)),
                      row_block(lambda i, s, t: (s[1] // 16, 0)),
                      row_block(lambda i, s, t: (t[0] // 16, 0)),
                      row_block(lambda i, s, t: (t[1] // 16, 0))]
            + [whole(v.shape) for v in vectors] + [ANY] * 3,
            out_specs=[whole((c, 128))] + [ANY] * 3,
            scratch_shapes=[vmem((pix, c)), vmem(w_emb.shape), vmem(w_conv1.shape), vmem((c, pix)),
                            vmem((c, pix)), vmem((c, pix), F32), vmem((c, pix), F32),
                            vmem((3 * c, 3 * c)), vmem((3 * c, pix)), dma(7)],
        ),
        compiler_params=pltpu.CompilerParams(vmem_limit_bytes=56 * 2**20),
        cost_estimate=pl.CostEstimate(flops=100 * 10**9, bytes_accessed=10**7, transcendentals=0),
        name="start",
    )(sigma_index, class_label, sigma_table, sigma_table, class_table, class_table, *vectors,
      block_input, w_emb, w_conv1)
    acts = gathered(acts, acts, acts, acts, bits)
    told = 4 * total
    w0 = 4 * c + 128 + told
    nat = vmem((HEADS, pix, head))
    piece = ((quarter, pix), BF, VM)
    stat, out, out_send, hg, gown, gcore, gsame, gcross, keep0, send0 = call(
        lambda *refs: kernel_attention(bits, *refs),
        [(sigma_index, SM), (class_label, SM), (stat, VM), (acts[0], ANY), (block_input, ANY),
         (cotangent, ANY), (w_conv2, ANY), (w_qkv, ANY), (w_proj, ANY)],
        [((c, 128), F32, VM), ((images, pix // 2, c), BF, ANY), ((pix // 2, c), BF, ANY),
         field + (VM,), piece, piece, piece, piece, ((half, w0), F32, VM), ((half, w0), BF, VM)],
        [vmem((c, pix)), vmem((pix, c)), vmem((pix, c)), vmem(w_conv2.shape), vmem(w_qkv.shape),
         vmem(w_proj.shape), vmem((3 * c, 3 * c)), vmem((3 * c, pix)),
         vmem((c // 128, 3 * c, 128), F32), vmem((2 * c, 128), F32), nat, nat,
         vmem((HEADS, pix, 2 * head)), vmem((c, pix)), vmem((c, pix)), vmem((c, pix)),
         vmem((c, pix)), vmem((c, pix)), vmem((3 * c, pix)), vmem((c, pix)), vmem((pix, c)), dma(8)],
        limit=60, flops=400 * 10**9, name="attention",
    )
    got0 = swap_core(send0)
    grads2 = gathered(gown, gcore, gsame, gcross, bits)
    out_got = swap_core(out_send)
    stat, dc, gown, gcore, gsame, gcross = call(
        lambda *refs: kernel_second(bits, *refs),
        [(hg, VM), (stat, VM), (w_conv2, ANY), (u2, ANY), (w_emb, ANY)],
        [((c, 128), F32, VM), field + (VM,), piece, piece, piece, piece],
        [vmem((3 * c, 3 * c)), vmem((c, pix), F32), vmem(w_emb.shape), vmem((3 * c, pix)),
         vmem((2 * c, 128), F32), dma(11)],
        after=acts[1:], flops=200 * 10**9, name="second",
    )
    got0, dc = lax.optimization_barrier((got0, dc))
    keep0, send0 = parted(keep0 + got0.astype(F32))
    got0 = exchange(send0, 0, bits)
    grads1 = gathered(gown, gcore, gsame, gcross, bits)

    def weight(which, grads, after, name):
        columns = 9 * c
        return call(
            lambda *refs: kernel_weight(which, *refs),
            [(v, ANY) for v in acts + grads],
            [((quarter // 2, columns), F32, VM), ((quarter // 2, columns), BF, VM)],
            [vmem((4, c, pix)), vmem((4, quarter, pix)), vmem((2, 9 * quarter, pix)),
             vmem((9 * quarter, c), F32), dma(8)],
            after=after, flops=200 * 10**9, name=name,
        )

    keep2, send2 = weight(1, grads2, [dc, send0, out_got], "weight_two")
    got2 = exchange(send2, 1, bits)
    got0, keep2 = lax.optimization_barrier((got0, keep2))
    keep0, send0 = parted(keep0 + got0.astype(F32))
    got0 = exchange(send0, 1, bits)
    keep1, send1 = weight(0, grads1, [keep2, send0], "weight_one")
    got1 = exchange(send1, 1, bits)
    got2, got0, keep1 = lax.optimization_barrier((got2, got0, keep1))
    keep2, send2 = parted(
        jnp.concatenate([keep2 + got2.astype(F32), keep0 + got0.astype(F32)], axis=1)
    )
    got2 = exchange(send2, 2, bits)
    ig, ig_send, keepv, sendv = call(
        lambda *refs: kernel_first(bits, *refs),
        [(dc, VM), (hg, VM), (stat, VM), (w_conv1, ANY), (u1, ANY)],
        [((images, pix // 2, c), BF, ANY), ((pix // 2, c), BF, ANY),
         ((half, 128 + told), F32, VM), ((half, 128 + told), BF, VM)],
        [vmem((3 * c, 3 * c)), vmem((c, pix), F32), vmem((3 * c, pix)), vmem((pix, c)), dma(12)],
        after=[keep1, send2], flops=200 * 10**9, name="first",
    )
    got1, got2, sendv, ig_send = lax.optimization_barrier((got1, got2, sendv, ig_send))
    ig_got = swap_core(ig_send)
    total_v = keepv + swap_core(sendv).astype(F32)
    keepv, sendv = parted(total_v)
    for step in range(bits):
        gotv = exchange(sendv, step, bits)
        if step < bits - 1:
            keepv, sendv = parted(keepv + gotv.astype(F32))
    for step in range(2, bits):
        if step > 2:
            got2 = exchange(send2, step, bits)
        if step < bits - 1:
            keep2, send2 = parted(keep2 + got2.astype(F32))
    for step in range(1, bits):
        if step > 1:
            got1 = exchange(send1, step, bits)
        if step < bits - 1:
            keep1, send1 = parted(keep1 + got1.astype(F32))
    line = lambda n: ((n,), F32, VM)
    conv = ((3, 3, size, c), F32, VM)
    g_conv2, g_qkv, g_proj, g_bconv2, g_gain3, g_bias3, g_bqv, g_bproj, emb, index = call(
        lambda *refs: kernel_last_two(c, *refs),
        [(keep2, VM), (got2, VM), (sigma_table, VM), (class_table, VM)],
        [conv, ((3 * size, c), F32, VM), ((size, c), F32, VM), line(size), line(size), line(size),
         line(2 * size), line(size), ((total, width), BF, VM), ((1, told), F32, VM)],
        [vmem((2 * size, 128), F32)], name="last_two",
    )
    tables = lambda count: ((2 * size, count), F32, VM)
    (g_conv1, g_gain2, g_bias2, g_bconv1, g_gain1, g_bias1, g_sigma, g_class, g_wemb, g_bemb) = call(
        lambda *refs: kernel_last_one(c, *refs),
        [(keep1, VM), (got1, VM), (keepv, VM), (gotv, VM), (index, VM), (emb, VM)],
        [conv] + [line(size)] * 5
        + [tables(sigma_table.shape[0]), tables(class_table.shape[0]), tables(width), line(2 * size)],
        [vmem((2 * size, 128), F32)], name="last_one",
    )
    other = lambda full, got: lax.dynamic_update_slice(full, got[None], (1 - core, 0, 0))
    output = other(out, out_got)
    input_grad = other(ig, ig_got)
    place = lambda v: jnp.transpose(v, (0, 1, 3, 2))
    return (
        output, input_grad, g_sigma.T, g_class.T, g_wemb.T, g_bemb, g_gain1, g_bias1, place(g_conv1),
        g_bconv1, g_gain2, g_bias2, place(g_conv2), g_bconv2, g_gain3, g_bias3, g_qkv.T, g_bqv,
        g_proj.T, g_bproj,
    )


def solution(mesh):
    every = ("dp", "pipe")
    return jax.shard_map(
        body,
        mesh=mesh,
        in_specs=(P("dp", None, None), P("dp", None, None), P("dp"), P("dp")) + (P(),) * 18,
        out_specs=(
            P("dp", "pipe", None), P("dp", "pipe", None), P(None, every), P(None, every),
            P(None, every), P(every), P(every), P(every), P(None, None, None, every), P(every),
            P(every), P(every), P(None, None, None, every), P(every), P(every), P(every),
            P(None, every), P(every), P(None, every), P(every),
        ),
        check_vma=False,
    )
```

```python
import jax
import jax.numpy as jnp
from jax import lax
from jax.experimental import pallas as pl
from jax.experimental.pallas import tpu as pltpu
from jax.sharding import PartitionSpec as P

HEADS = 6
GROUPS = 32
SIDE = 32
EPS = 1e-05
LOG2E = 1.4426950408889634
BF = jnp.bfloat16
F32 = jnp.float32
NN = (((1,), (0,)), ((), ()))
NT = (((1,), (1,)), ((), ()))
TN = (((0,), (0,)), ((), ()))


def mm(a, b, dims=NN):
    return lax.dot_general(a, b, dims, preferred_element_type=F32)


def silu(v):
    return v * jax.nn.sigmoid(v)


def silu_slope(v):
    s = jax.nn.sigmoid(v)
    return s * (1.0 + v * (1.0 - s))


def lanes(shape):
    return lax.broadcasted_iota(jnp.int32, shape, 1)


def rowsum(v):
    return jnp.sum(v, axis=1, keepdims=True)


def shift_cols(a, d):
    if d == 0:
        return a
    n = a.shape[1]
    col = lanes(a.shape) & (SIDE - 1)
    ok = (col + d >= 0) & (col + d < SIDE)
    return jnp.where(ok, pltpu.roll(a, (-d) % n, 1), 0)


def shift_rows(a, d):
    if d == 0:
        return a
    n = a.shape[1]
    at = lanes(a.shape) + SIDE * d
    return jnp.where((at >= 0) & (at < n), pltpu.roll(a, (-SIDE * d) % n, 1), 0)


def split3(v):
    hi = v.astype(BF).astype(F32)
    mid = (v - hi).astype(BF).astype(F32)
    return hi, mid, v - hi - mid


def exact_left(matrix, v, dims=NN):
    return sum(mm(matrix, part.astype(BF), dims) for part in split3(v))


def exact_right(v, matrix, dims=NN):
    return sum(mm(part.astype(BF), matrix, dims) for part in split3(v))


def with_columns(block, start, extra):
    lane = lanes(block.shape)
    for n, c in enumerate(extra):
        block = jnp.where(lane == start + n, c, block)
    return block


def exact_columns(matrix, cols):
    parts = [part for col in cols for part in split3(col)]
    block = with_columns(jnp.zeros((cols[0].shape[0], 128), F32), 0, parts)
    got = mm(matrix, block.astype(BF))
    return [rowsum(got[:, 3 * at : 3 * at + 3]) for at in range(len(cols))]


def divide(v, size, top):
    scale = -(-(1 << 19) // size)
    assert all((n * scale) >> 19 == n // size for n in range(top))
    return (v * scale) >> 19


def group_matrix(channels):
    size = channels // GROUPS
    shape = (channels, channels)
    row = divide(lax.broadcasted_iota(jnp.int32, (channels, 1), 0), size, channels)
    col = divide(lax.broadcasted_iota(jnp.int32, (1, channels), 1), size, channels)
    return jnp.where(row == col, 1.0, jnp.zeros(shape, F32)).astype(BF)


def group_means(cols, pixels):
    channels = cols[0].shape[0]
    count = channels // GROUPS * pixels
    return [got * (1.0 / count) for got in exact_columns(group_matrix(channels), cols)]


def group_stats(v):
    pixels = v.shape[1]
    (mean,) = group_means([rowsum(v)], pixels)
    centred = v - mean
    (var,) = group_means([rowsum(centred * centred)], pixels)
    inverse = lax.rsqrt(var + EPS)
    return centred * inverse, inverse


def group_back(t, u, inverse, gain, sum_t, sum_tu):
    first, second = group_means([gain * sum_t, gain * sum_tu], t.shape[1])
    return (inverse * gain) * t - inverse * first - u * (inverse * second)


def fill_cols(ref, a, sign):
    c = a.shape[0]
    for j in range(3):
        ref[j * c : (j + 1) * c, :] = shift_cols(a, sign * (j - 1)).astype(BF)


def conv_apply(w_ref, cat_ref, sign, channels):
    total = None
    for i in range(3):
        y = mm(w_ref[i * channels : (i + 1) * channels, :], cat_ref[...])
        y = shift_rows(y, sign * (i - 1))
        total = y if total is None else total + y
    return total


def fill_forward(wf, w_ref, channels):
    for i in range(3):
        for j in range(3):
            at = (slice(i * channels, (i + 1) * channels), slice(j * channels, (j + 1) * channels))
            wf[at] = w_ref[i, j].T


def copies(pairs, sems):
    made = [pltpu.make_async_copy(src, dst, sems.at[n]) for n, (src, dst) in enumerate(pairs)]
    for one in made:
        one.start()
    return made


def tap_pairs(w_ref, wb, channels):
    return [
        (
            w_ref.at[i, j],
            wb.at[
                i * channels : (i + 1) * channels, j * channels : (j + 1) * channels
            ],
        )
        for i in range(3)
        for j in range(3)
    ]


def stream_order(core, bits):
    order = list(range(bits))
    if core:
        for at in range(0, bits - 1, 2):
            order[at], order[at + 1] = order[at + 1], order[at]
    return order


def row_matrix(channels, bits):
    dp, core = lax.axis_index("dp"), lax.axis_index("pipe")
    size = channels // (2 << bits)
    quarter = channels // 4
    row = lax.broadcasted_iota(jnp.int32, (channels, 1), 0)
    part_of = sum(jnp.where(row >= quarter * n, 1, 0) for n in (1, 2, 3))
    rest = row - part_of * quarter
    at = divide(rest, size, quarter)
    within = rest - at * size
    part = jnp.where(part_of < 2, core, 1 - core)
    flips = []
    for p in (0, 1):
        order = stream_order(p, bits)
        flip = (part_of & 1) << order[0]
        for t in range(bits - 1):
            flip = flip | (((at >> (bits - 2 - t)) & 1) << order[t + 1])
        flips.append(flip)
    peer = dp ^ jnp.where(part == 0, flips[0], flips[1])
    wanted = (2 * peer + part) * size + within
    shape = (channels, channels)
    return jnp.where(wanted == lanes((1, channels)), 1.0, jnp.zeros(shape, F32)).astype(BF)


def own_image():
    return 2 * lax.axis_index("dp") + lax.axis_index("pipe")


def kernel_start(
    total, sig_at, cls_at, sig0, sig1, cls0, cls1, bemb, g1, b1, bc1, g2, b2, bc2, g3, b3, bqv, bp,
    x, wemb_ref, w1_ref,
    stat_ref, acts_ref, u1_ref, u2_ref,
    wemb, w1, act1, act2, told, u1, u2, wf, cat, sems,
):
    core = lax.axis_index("pipe")
    channels = x.shape[2]
    loads = copies([(w1_ref, w1), (wemb_ref, wemb)], sems)
    sig = jnp.where(core == 0, sig_at[0], sig_at[1])
    cls = jnp.where(core == 0, cls_at[0], cls_at[1])
    lane = lanes(told.shape)
    line = jnp.zeros(told.shape, F32)
    for n, digit in enumerate((sig // 32, sig % 32, cls // 32, cls % 32)):
        line = jnp.where(lane == n * total + own_image(), digit.astype(F32), line)
    told[...] = line.astype(BF)
    row16 = lax.broadcasted_iota(jnp.int32, sig0.shape, 0)

    def table_row(at, first, second):
        block = jnp.where(core == 0, first[...].astype(F32), second[...].astype(F32))
        found = jnp.where(core == 0, at[0], at[1])
        return jnp.sum(jnp.where(row16 == found % 16, block, 0.0), axis=0, keepdims=True)

    emb = table_row(sig_at, sig0, sig1) + table_row(cls_at, cls0, cls1)
    flat = lambda ref: ref[...].astype(F32).reshape(1, ref.shape[0])
    bqv_row = flat(bqv)
    rows = [flat(ref) for ref in (g1, b1, bc1, g2, b2, bc2, g3, b3)]
    rows += [bqv_row[:, :channels], bqv_row[:, channels:], flat(bp)]
    prm = jnp.zeros((128, channels), F32)
    at = lax.broadcasted_iota(jnp.int32, prm.shape, 0)
    v1, inv1 = group_stats(x[core].astype(F32).T)
    u1[...] = v1
    loads[0].wait()
    fill_forward(wf, w1, channels)
    loads[1].wait()
    low = jnp.broadcast_to(silu(emb), (16, emb.shape[1])).astype(BF)
    affine = mm(low, wemb[...])[0:1] + flat(bemb)
    rows += [affine[:, :channels], affine[:, channels:], emb[:, :channels], emb[:, channels:]]
    for n, line in enumerate(rows):
        prm = jnp.where(at == n, line, prm)
    stat = prm.T
    col = lambda n: stat[:, n : n + 1]
    a1 = silu(v1 * col(0) + col(1))
    act1[...] = a1.astype(BF)
    stores = copies([(u1, u1_ref), (act1, acts_ref.at[:channels]),
                     (told, acts_ref.at[2 * channels :])], sems.at[2:5])
    fill_cols(cat, a1, 1)
    v2, inv2 = group_stats(conv_apply(wf, cat, 1, channels) + col(2))
    u2[...] = v2
    scale, shift = col(11), col(12)
    a2 = silu(v2 * (col(3) * (1.0 + scale)) + (col(4) * (1.0 + scale) + shift))
    act2[...] = a2.astype(BF)
    stores += copies([(u2, u2_ref), (act2, acts_ref.at[channels : 2 * channels])], sems.at[5:7])
    stat_ref[...] = with_columns(stat, 32, [inv1, inv2])
    for one in stores:
        one.wait()


def prepare_heads(q_t, k_t, v_t, q_nt, k_nt, v_nt, head):
    pix = q_t.shape[1]
    ones = jnp.where(lanes((pix, head)) < 2, 1.0, 0.0).astype(BF)
    for h in range(HEADS):
        at = slice(h * head, (h + 1) * head)
        q_nt[h] = q_t[at, :].T
        k_nt[h] = k_t[at, :].T
        v_nt[h, :, :head] = v_t[at, :].T
        v_nt[h, :, head:] = ones


def largest_score(q_t, k_t, head):
    worst = jnp.zeros((1, 1), F32)
    for h in range(HEADS):
        longest = []
        for ref in (q_t, k_t):
            v = ref[h * head : (h + 1) * head, :].astype(F32)
            longest.append(
                jnp.max(jnp.sum(v * v, axis=0, keepdims=True), axis=1, keepdims=True)
            )
        worst = jnp.maximum(worst, longest[0] * longest[1])
    return worst[0, 0]


def one_head(bounded, h, head, q_t, k_t, v_t, ga_t, q_nt, k_nt, v_nt, at_t, gq_t):
    channels, pix = q_t.shape
    factor = head ** (-0.5)
    rows = lambda base: pl.ds(pl.multiple_of(base + h * head, head), head)
    at = rows(0)
    s = mm(k_nt[h], q_t[at, :])
    if not bounded:
        s = s - jnp.max(s, axis=0, keepdims=True)
    e = jnp.exp2(s * (factor * LOG2E)).astype(BF)
    o = mm(jnp.concatenate([v_t[at, :], jnp.ones((16, pix), BF)], axis=0), e)
    inv = 1.0 / o[head : head + 1]
    o = o[:head] * inv
    at_t[at, :] = o.astype(BF)
    g = ga_t[at, :].astype(F32)
    centre = -jnp.sum(g * o, axis=0, keepdims=True) * inv
    g = (g * inv).astype(BF)
    hi = centre.astype(BF).astype(F32)
    line = lax.broadcasted_iota(jnp.int32, (head, pix), 0)
    tail = jnp.where(line == 0, hi, jnp.where(line == 1, centre - hi, 0.0)).astype(BF)
    ds = (e.astype(F32) * mm(v_nt[h], jnp.concatenate([g, tail], axis=0))).astype(BF)
    gq_t[at, :] = (mm(k_t[at, :], ds) * factor).astype(BF)
    gq_t[rows(channels), :] = (mm(ds, q_nt[h]) * factor).T.astype(BF)
    gq_t[rows(2 * channels), :] = mm(e, g.T).T.astype(BF)


def kernel_attention(
    bits, stat, acts_ref, x_ref, cot_ref, w2_ref, wqkv_ref, wproj_ref,
    out_ref, outs_ref, hg_ref, gown_ref, gsame_ref, gcore_ref, gcross_ref, gproj_ref,
    act2, x, cot, w2, wqkv, wproj, wf, cat, wide, tall, q_nt, k_nt, v_nt, q_t, k_t, v_t, ga_t, at_t,
    gq_t, cot_t, out, sems,
):
    core = lax.axis_index("pipe")
    channels, pix = act2.shape
    head = channels // HEADS
    half = channels // 2
    loads = copies(
        [(acts_ref.at[channels : 2 * channels], act2), (w2_ref, w2), (x_ref.at[core], x), (wqkv_ref, wqkv),
         (cot_ref.at[core], cot), (wproj_ref, wproj)],
        sems,
    )
    col = lambda n: stat[:, n : n + 1]
    loads[0].wait()
    fill_cols(cat, act2[...].astype(F32), 1)
    loads[1].wait()
    fill_forward(wf, w2, channels)
    conv = conv_apply(wf, cat, 1, channels) + col(5)
    loads[2].wait()
    hidden = (x[...].astype(F32).T + conv).astype(BF).astype(F32)
    u3, inv3 = group_stats(hidden)
    normed = (u3 * col(6) + col(7)).astype(BF)
    loads[3].wait()
    projected = mm(wqkv[...], normed, TN)
    q_t[...] = (projected[:channels] + col(8)).astype(BF)
    k_t[...] = projected[channels : 2 * channels].astype(BF)
    v_t[...] = (projected[2 * channels :] + col(9)).astype(BF)
    loads[4].wait()
    cot_t[...] = cot[...].T
    loads[5].wait()
    ga_t[...] = mm(wproj[...], cot_t[...]).astype(BF)
    prepare_heads(q_t, k_t, v_t, q_nt, k_nt, v_nt, head)

    def all_heads(bounded):
        def two_heads(t, _):
            for n in range(2):
                one_head(
                    bounded, 2 * t + n, head, q_t, k_t, v_t, ga_t, q_nt, k_nt, v_nt, at_t, gq_t
                )
            return 0

        lax.fori_loop(0, HEADS // 2, two_heads, 0)

    small = largest_score(q_t, k_t, head) <= (60.0 / head ** (-0.5)) ** 2
    pl.when(small)(lambda: all_heads(True))
    pl.when(jnp.logical_not(small))(lambda: all_heads(False))
    out[...] = (hidden + mm(wproj[...], at_t[...], TN) + col(10)).T.astype(BF)
    rows = lambda c: pl.ds(pl.multiple_of(c * (pix // 2), pix // 2), pix // 2)
    stores = copies(
        [(out.at[rows(core)], out_ref.at[core]), (out.at[rows(1 - core)], outs_ref)], sems.at[6:8]
    )
    perm = row_matrix(channels, bits)
    got = mm(gq_t[...], normed, NT)
    tiles = channels // 128
    for t in range(tiles):
        wide[t] = got[:, t * 128 : (t + 1) * 128]
    quarter = channels // 4
    pieces = (gown_ref, gsame_ref, gcore_ref, gcross_ref)

    def spread(base, rows):
        for n, ref in enumerate(pieces):
            ref[:, base : base + rows.shape[1]] = rows[n * quarter : (n + 1) * quarter].astype(BF)

    for n in range(3):
        part = jnp.concatenate(
            [wide[t, pl.ds(n, channels, stride=3), :] for t in range(tiles)], axis=1
        )
        spread(pix + n * channels, mm(perm, part.astype(BF)))
    gproj_ref[...] = mm(perm, mm(cot_t[...], at_t[...], NT).astype(BF)).astype(BF)
    gn = mm(wqkv[...], gq_t[...])
    s3 = rowsum(gn)
    su3 = rowsum(gn * u3)
    cot_f = cot_t[...].astype(F32)
    hg = (cot_f + group_back(gn, u3, inv3, col(6), s3, su3)).astype(BF)
    hg_ref[...] = hg
    spread(0, mm(perm, hg))
    gq = gq_t[...].astype(F32)
    tall[:channels] = jnp.broadcast_to(rowsum(gq[:channels]), (channels, 128))
    tall[channels:] = jnp.broadcast_to(rowsum(gq[2 * channels :]), (channels, 128))
    side = with_columns(
        jnp.zeros((channels, 128), F32), 0,
        [su3, s3, tall[pl.ds(0, channels, stride=2), :], tall[pl.ds(1, channels, stride=2), :],
         rowsum(cot_f), rowsum(hg.astype(F32))],
    )
    spread(pix + 3 * channels, exact_left(perm, side))
    for one in stores:
        one.wait()


def kernel_second(
    bits, hg, stat_in, gproj, w2_ref, u2_ref, wemb_ref,
    stat_ref, dc_ref, gown_ref, gsame_ref, gcore_ref, gcross_ref,
    wb, u2v, wemb, cat, tall, sems,
):
    channels = hg.shape[0]
    loads = copies(tap_pairs(w2_ref, wb, channels) + [(u2_ref, u2v), (wemb_ref, wemb)], sems)
    stat = stat_in[...]
    col = lambda n: stat[:, n : n + 1]
    g2, b2, scale, shift, inv2 = col(3), col(4), col(11), col(12), col(33)
    fill_cols(cat, hg[...].astype(F32), -1)
    for one in loads[:9]:
        one.wait()
    da = conv_apply(wb, cat, -1, channels)
    loads[9].wait()
    u2 = u2v[...]
    gm = g2 * (1.0 + scale)
    dm = da * silu_slope(u2 * gm + (b2 * (1.0 + scale) + shift))
    s = rowsum(dm)
    su = rowsum(dm * u2)
    dc = group_back(dm, u2, inv2, gm, s, su).astype(BF)
    dc_ref[...] = dc
    parts = mm(row_matrix(channels, bits), dc).astype(BF)
    quarter = channels // 4
    for n, ref in enumerate((gown_ref, gsame_ref, gcore_ref, gcross_ref)):
        at = slice(n * quarter, (n + 1) * quarter)
        ref[:, : hg.shape[1]] = parts[at]
        ref[:, hg.shape[1] :] = gproj[at, :]
    tall[:channels] = jnp.broadcast_to(g2 * su + b2 * s, (channels, 128))
    tall[channels:] = jnp.broadcast_to(s, (channels, 128))
    ga = [tall[pl.ds(n, channels, stride=2), :] for n in range(2)]
    loads[10].wait()
    (ge,) = exact_columns(wemb[...], [tall[...][:, :1]])
    tall[:channels] = jnp.broadcast_to(ge[:channels] * silu_slope(col(13)), (channels, 128))
    tall[channels:] = jnp.broadcast_to(ge[channels:] * silu_slope(col(14)), (channels, 128))
    ge = [tall[pl.ds(n, channels, stride=2), :] for n in range(2)]
    stat = with_columns(
        stat, 40, [(1.0 + scale) * su, (1.0 + scale) * s, rowsum(dc.astype(F32))]
    )
    stat_ref[...] = with_columns(stat, 48, ga + ge)


def kernel_first(
    bits, dc, stat_in, w1_ref, u1_ref, dp_ref, stat_ref, own_ref, same_ref, core_ref, cross_ref,
    wb, u1v, cat, sems,
):
    channels = dc.shape[0]
    quarter = channels // 4
    loads = copies(tap_pairs(w1_ref, wb, channels) + [(u1_ref, u1v)], sems)
    stat = stat_in[...]
    col = lambda n: stat[:, n : n + 1]
    fill_cols(cat, dc[...].astype(F32), -1)
    for one in loads[:9]:
        one.wait()
    da = conv_apply(wb, cat, -1, channels)
    loads[9].wait()
    u1 = u1v[...]
    dp = da * silu_slope(u1 * col(0) + col(1))
    s = rowsum(dp)
    su = rowsum(dp * u1)
    dp_ref[...] = dp
    stat_ref[...] = with_columns(stat, 43, [su, s])
    width = own_ref.shape[1]
    total = (width - 128) // 4
    side = with_columns(
        jnp.zeros((channels, width), F32), 0, [col(40), col(41), col(42), su, s]
    )
    lane = lanes((channels, width))
    for n in range(4):
        side = jnp.where(lane == 128 + n * total + own_image(), col(48 + n), side)
    side = exact_left(row_matrix(channels, bits), side)
    for n, ref in enumerate((own_ref, same_ref, core_ref, cross_ref)):
        ref[...] = side[n * quarter : (n + 1) * quarter].astype(ref.dtype)


def kernel_input(dp, u1, hg, stat, ig_ref, igs_ref, ig, sems):
    core = lax.axis_index("pipe")
    pix = hg.shape[1]
    col = lambda n: stat[:, n : n + 1]
    back = group_back(dp[...], u1[...], col(32), col(0), col(44), col(43))
    ig[...] = (hg[...].astype(F32) + back).T.astype(BF)
    rows = lambda c: pl.ds(pl.multiple_of(c * (pix // 2), pix // 2), pix // 2)
    stores = copies(
        [(ig.at[rows(core)], ig_ref.at[core]), (ig.at[rows(1 - core)], igs_ref)], sems
    )
    for one in stores:
        one.wait()


def kernel_weight(which, total_images, *refs):
    acts, pieces = refs[:4], refs[4:8]
    keep_ref, send_ref, act, piece, told, stack, total, sems = refs[8:]
    rows, channels, pix = piece.shape[1], act.shape[1], act.shape[2]
    half = rows // 2
    at = slice(which * channels, (which + 1) * channels)
    pairs = [(ref, piece.at[n]) for n, ref in enumerate(pieces)]
    pairs += [(ref.at[at], act.at[n]) for n, ref in enumerate(acts)]
    if total_images:
        pairs += [(ref.at[2 * channels :], told.at[n]) for n, ref in enumerate(acts)]
    loads = copies(pairs, sems)

    def build(n):
        g = piece[n, :, :pix].astype(F32)
        for j in range(3):
            moved = shift_cols(g, 1 - j)
            for i in range(3):
                base = (3 * i + j) * rows
                stack[n, base : base + rows, :] = shift_rows(moved, 1 - i).astype(BF)

    loads[0].wait()
    build(0)
    for one in loads[1:8]:
        one.wait()
    for n in range(4):
        if n < 3:
            build(n + 1)
        got = mm(stack[n], act[n], NT)
        total[...] = got if n == 0 else total[...] + got
    for tap in range(9):
        at = slice(tap * channels, (tap + 1) * channels)
        keep_ref[:, at] = total[tap * rows : tap * rows + half, :]
        send_ref[:, at] = total[tap * rows + half : (tap + 1) * rows, :].astype(BF)
    at = slice(9 * channels, 9 * channels + piece.shape[2] - pix)
    more = sum(piece[n, :, pix:].astype(F32) for n in range(4))
    keep_ref[:, at] = more[:half]
    send_ref[:, at] = more[half:].astype(BF)
    if total_images:
        for one in loads[8:]:
            one.wait()
        line = sum(told[n].astype(F32) for n in range(4))[:1, : 4 * total_images]
        line = jnp.broadcast_to(line, (half, 4 * total_images))
        keep_ref[:, at.stop :] = line
        send_ref[:, at.stop :] = line.astype(BF)


def interleave(ref, parts):
    size = parts[0].shape[0]
    for r in range(size):
        for n, part in enumerate(parts):
            at = len(parts) * r + n
            ref[at : at + 1, : part.shape[1]] = part[r : r + 1]


def summed(parts, size):
    return sum(part[:size].astype(F32) for part in parts)


def kernel_last_two(
    channels, size, parts, sig_table, cls_table, conv_ref, qkv_ref, bconv_ref, gain_ref, bias_ref, bqv_ref, bproj_ref, emb_ref, told_ref, rows,
):
    total = summed(parts, size)
    for i in range(3):
        for j in range(3):
            at = (3 * i + j) * channels
            conv_ref[i, j] = total[:, at : at + channels]
    rest = total[:, 9 * channels :]
    interleave(qkv_ref, [rest[:, n * channels : (n + 1) * channels] for n in range(3)])
    side = rest[:, 3 * channels : 3 * channels + 128]
    lines = side.T
    for n, ref in ((0, gain_ref), (1, bias_ref), (4, bproj_ref), (5, bconv_ref)):
        ref[...] = lines[n]
    interleave(rows, [jnp.broadcast_to(side[:, n : n + 1], (size, 128)) for n in (2, 3)])
    bqv_ref[...] = rows[...].T[0]
    told = rest[0:1, 3 * channels + 128 :]
    told_ref[...] = told
    images = told.shape[1] // 4
    hot_sig, hot_cls = hot_rows(told, images, sig_table.shape[0], cls_table.shape[0])
    emb = mm(hot_sig, sig_table[...], TN) + mm(hot_cls, cls_table[...], TN)
    emb_ref[...] = silu(emb).astype(BF)


def hot_rows(told, images, sig_count, cls_count):
    digit = lambda n: told[:, n * images : (n + 1) * images].astype(jnp.int32)
    sig = 32 * digit(0) + digit(1)
    cls = 32 * digit(2) + digit(3)

    def hot(index, count):
        line = lax.broadcasted_iota(jnp.int32, (count, images), 0)
        return jnp.where(line == index, 1.0, 0.0).astype(BF)

    return hot(sig, sig_count), hot(cls, cls_count)


def kernel_last_one(channels, size, parts, conv_ref, proj_ref):
    total = summed(parts, size)
    for i in range(3):
        for j in range(3):
            at = (3 * i + j) * channels
            conv_ref[i, j] = total[:, at : at + channels]
    proj_ref[...] = total[:, 9 * channels :]


def kernel_last_side(
    size, parts, told_ref, emb_ref, gain2_ref, bias2_ref, bconv_ref, gain1_ref, bias1_ref, sig_ref, cls_ref, wemb_ref, bemb_ref,
    rows,
):
    rest = summed(parts, size)
    lines = rest[:, :128].T
    for n, ref in enumerate((gain2_ref, bias2_ref, bconv_ref, gain1_ref, bias1_ref)):
        ref[...] = lines[n]
    told = told_ref[...]
    images = told.shape[1] // 4
    part = lambda n: rest[:, 128 + n * images : 128 + (n + 1) * images]
    hot_sig, hot_cls = hot_rows(told, images, sig_ref.shape[1], cls_ref.shape[1])
    into = [part(2), part(3)]
    interleave(sig_ref, [exact_right(v, hot_sig, NT) for v in into])
    interleave(cls_ref, [exact_right(v, hot_cls, NT) for v in into])
    affine = [part(0), part(1)]
    interleave(wemb_ref, [exact_right(v, emb_ref[...]) for v in affine])
    interleave(rows, [jnp.broadcast_to(rowsum(v), (v.shape[0], 128)) for v in affine])
    bemb_ref[...] = rows[...].T[0]


VM = pl.BlockSpec(memory_space=pltpu.VMEM)
ANY = pl.BlockSpec(memory_space=pl.ANY)
SM = pl.BlockSpec(memory_space=pltpu.SMEM)


def vmem(shape, dtype=BF):
    return pltpu.VMEM(shape, dtype)


def call(kernel, operands, outs, scratch, after=(), limit=20, flops=0, name=None):
    count = len(operands)
    operands = list(operands) + [(v, ANY) for v in after]

    def ordered(*refs):
        kernel(*refs[:count], *refs[len(operands) :])

    return pl.pallas_call(
        ordered,
        out_shape=[jax.ShapeDtypeStruct(shape, dtype) for shape, dtype, _ in outs],
        in_specs=[spec for _, spec in operands],
        out_specs=[spec for _, _, spec in outs],
        scratch_shapes=scratch,
        compiler_params=pltpu.CompilerParams(vmem_limit_bytes=limit * 2**20),
        cost_estimate=pl.CostEstimate(flops=flops, bytes_accessed=10**6, transcendentals=0),
        name=name,
    )(*[operand for operand, _ in operands])


def swap_core(v):
    return lax.ppermute(v, "pipe", [(0, 1), (1, 0)])


def joint(v, target):
    pairs = []
    for dp in range(lax.axis_size("dp")):
        for core in range(2):
            to_dp, to_core = target(dp, core)
            pairs.append((2 * dp + core, 2 * to_dp + to_core))
    return lax.ppermute(v, ("dp", "pipe"), pairs)


def exchange(v, step, bits):
    return joint(v, lambda dp, core: (dp ^ (1 << stream_order(core, bits)[step]), core))


def cross(v, bits):
    return joint(v, lambda dp, core: (dp ^ (1 << stream_order(1 - core, bits)[0]), 1 - core))


def leaving(parts, rows):
    return sum(part[rows // 2 : rows].astype(F32) for part in parts).astype(BF)


def gathered(own, to_core, to_same, to_cross, bits):
    return [own, swap_core(to_core), exchange(to_same, 0, bits), cross(to_cross, bits)]


def body(
    block_input, cotangent, sigma_index, class_label, sigma_table, class_table, w_emb, b_emb,
    norm1_gain, norm1_bias, w_conv1, b_conv1, norm2_gain, norm2_bias, w_conv2, b_conv2,
    norm3_gain, norm3_bias, w_qkv, b_qv, w_proj, b_proj,
):
    core = lax.axis_index("pipe")
    data = lax.axis_size("dp")
    bits = data.bit_length() - 1
    images, pix, c = block_input.shape
    total = 2 * data
    width = sigma_table.shape[1]
    head, half, quarter, size = c // HEADS, c // 2, c // 4, c // (2 * data)
    dma = lambda count: pltpu.SemaphoreType.DMA((count,))
    field = ((c, pix), BF)
    row_block = lambda index: pl.BlockSpec((16, width), index)
    whole = lambda shape: pl.BlockSpec(shape, lambda i, s, t: (0,) * len(shape))
    vectors = [b_emb, norm1_gain, norm1_bias, b_conv1, norm2_gain, norm2_bias, b_conv2, norm3_gain,
               norm3_bias, b_qv, b_proj]
    told = 4 * total
    stat, acts, u1, u2 = pl.pallas_call(
        lambda *refs: kernel_start(total, *refs),
        out_shape=[jax.ShapeDtypeStruct(*v) for v in
                   [((c, 128), F32), ((2 * c + 16, pix), BF), ((c, pix), F32), ((c, pix), F32)]],
        grid_spec=pltpu.PrefetchScalarGridSpec(
            num_scalar_prefetch=2,
            grid=(1,),
            in_specs=[row_block(lambda i, s, t: (s[0] // 16, 0)),
                      row_block(lambda i, s, t: (s[1] // 16, 0)),
                      row_block(lambda i, s, t: (t[0] // 16, 0)),
                      row_block(lambda i, s, t: (t[1] // 16, 0))]
            + [whole(v.shape) for v in vectors] + [whole(block_input.shape)] + [ANY] * 2,
            out_specs=[whole((c, 128))] + [ANY] * 3,
            scratch_shapes=[vmem(w_emb.shape), vmem(w_conv1.shape), vmem((c, pix)), vmem((c, pix)),
                            vmem((16, pix)), vmem((c, pix), F32), vmem((c, pix), F32),
                            vmem((3 * c, 3 * c)), vmem((3 * c, pix)), dma(7)],
        ),
        compiler_params=pltpu.CompilerParams(vmem_limit_bytes=62 * 2**20),
        cost_estimate=pl.CostEstimate(flops=10**11, bytes_accessed=10**7, transcendentals=0),
        name="start",
    )(sigma_index, class_label, sigma_table, sigma_table, class_table, class_table, *vectors,
      block_input, w_emb, w_conv1)
    acts = gathered(acts, acts, acts, acts, bits)
    nat = vmem((HEADS, pix, head))
    piece = lambda more: [((quarter, pix + more), BF, VM)] * 4
    more2 = 3 * c + 128
    out, out_send, hg, gown, gsame, gcore, gcross, gproj = call(
        lambda *refs: kernel_attention(bits, *refs),
        [(stat, VM), (acts[0], ANY), (block_input, ANY),
         (cotangent, ANY), (w_conv2, ANY), (w_qkv, ANY), (w_proj, ANY)],
        [((images, pix // 2, c), BF, ANY), ((pix // 2, c), BF, ANY),
         field + (VM,)] + piece(more2) + [((c, c), BF, VM)],
        [vmem((c, pix)), vmem((pix, c)), vmem((pix, c)), vmem(w_conv2.shape), vmem(w_qkv.shape),
         vmem(w_proj.shape), vmem((3 * c, 3 * c)), vmem((3 * c, pix)),
         vmem((c // 128, 3 * c, 128), F32), vmem((2 * c, 128), F32), nat, nat,
         vmem((HEADS, pix, 2 * head)), vmem((c, pix)), vmem((c, pix)), vmem((c, pix)),
         vmem((c, pix)), vmem((c, pix)), vmem((3 * c, pix)), vmem((c, pix)), vmem((pix, c)), dma(8)],
        limit=48, flops=400 * 10**9, name="attention",
    )
    grads2 = gathered(gown, gcore, gsame, gcross, bits)
    out_got = swap_core(out_send)
    stat, dc, gown, gsame, gcore, gcross = call(
        lambda *refs: kernel_second(bits, *refs),
        [(hg, VM), (stat, VM), (gproj, VM), (w_conv2, ANY), (u2, ANY), (w_emb, ANY)],
        [((c, 128), F32, VM), field + (VM,)] + piece(c),
        [vmem((3 * c, 3 * c)), vmem((c, pix), F32), vmem(w_emb.shape), vmem((3 * c, pix)),
         vmem((2 * c, 128), F32), dma(11)],
        after=acts[1:], flops=200 * 10**9, name="second",
    )
    grads1 = gathered(gown, gcore, gsame, gcross, bits)

    def weight(which, grads, count, after, name):
        more = grads[0].shape[1] - pix
        columns = 9 * c + more + 4 * count
        return call(
            lambda *refs: kernel_weight(which, count, *refs),
            [(v, ANY) for v in acts + grads],
            [((quarter // 2, columns), F32, VM), ((quarter // 2, columns), BF, VM)],
            [vmem((4, c, pix)), vmem((4, quarter, pix + more)), vmem((4, 16, pix)),
             vmem((4, 9 * quarter, pix)), vmem((9 * quarter, c), F32), dma(12)],
            after=after, limit=28, flops=200 * 10**9, name=name,
        )

    rows = [quarter >> step for step in range(bits)]
    keep2, send2 = weight(1, grads2, total, [dc, out_got], "weight_two")
    two = [keep2, exchange(send2, 1, bits)]
    keep1, send1 = weight(0, grads1, 0, [keep2], "weight_one")
    one = [keep1, exchange(send1, 1, bits)]
    two[1], keep1 = lax.optimization_barrier((two[1], keep1))
    send2 = leaving(two, rows[1])
    two.append(exchange(send2, 2, bits))
    dp, stat, own, same, to_core, to_cross = call(
        lambda *refs: kernel_first(bits, *refs),
        [(dc, VM), (stat, VM), (w_conv1, ANY), (u1, ANY)],
        [((c, pix), F32, VM), ((c, 128), F32, VM), ((quarter, 128 + told), F32, VM)]
        + [((quarter, 128 + told), BF, VM)] * 3,
        [vmem((3 * c, 3 * c)), vmem((c, pix), F32), vmem((3 * c, pix)), dma(10)],
        after=[keep1, send2], flops=200 * 10**9, name="first",
    )
    one[1], two[2], own, dp = lax.optimization_barrier((one[1], two[2], own, dp))
    side = gathered(own, to_core, same, to_cross, bits)
    send1, send2 = leaving(one, rows[1]), leaving(two, rows[2])
    one.append(exchange(send1, 2, bits))
    two.append(exchange(send2, 3, bits))
    ig, ig_send = call(
        kernel_input,
        [(dp, VM), (u1, VM), (hg, VM), (stat, VM)],
        [((images, pix // 2, c), BF, ANY), ((pix // 2, c), BF, ANY)],
        [vmem((pix, c)), dma(2)],
        after=[send1, send2], flops=200 * 10**9, name="input",
    )
    *side, ig_send = lax.optimization_barrier((*side, ig_send))
    side.append(exchange(leaving(side, rows[0]), 1, bits))
    ig_got = swap_core(ig_send)
    side[-1], one[-1], two[-1] = lax.optimization_barrier((side[-1], one[-1], two[-1]))
    side.append(exchange(leaving(side, rows[1]), 2, bits))
    one.append(exchange(leaving(one, rows[2]), 3, bits))
    for step in range(4, bits):
        two.append(exchange(leaving(two, rows[step - 1]), step, bits))
    line = lambda n: ((n,), F32, VM)
    conv = ((3, 3, size, c), F32, VM)
    count = len(two)
    g_conv2, g_qkv, g_bconv2, g_gain3, g_bias3, g_bqv, g_bproj, emb, index = call(
        lambda *refs: kernel_last_two(c, size, refs[:count], *refs[count:]),
        [(v, VM) for v in two] + [(sigma_table, VM), (class_table, VM)],
        [conv, ((3 * size, c), F32, VM), line(size), line(size), line(size),
         line(2 * size), line(size), ((total, width), BF, VM), ((1, told), F32, VM)],
        [vmem((2 * size, 128), F32)], name="last_two",
    )
    side[-1], emb = lax.optimization_barrier((side[-1], emb))
    for step in range(3, bits):
        side.append(exchange(leaving(side, rows[step - 1]), step, bits))
    for step in range(4, bits):
        one.append(exchange(leaving(one, rows[step - 1]), step, bits))
    count_one = len(one)
    g_conv1, g_proj = call(
        lambda *refs: kernel_last_one(c, size, refs[:count_one], *refs[count_one:]),
        [(v, VM) for v in one], [conv, ((size, c), F32, VM)], [], name="last_one",
    )
    tables = lambda count: ((2 * size, count), F32, VM)
    count_side = len(side)
    g_gain2, g_bias2, g_bconv1, g_gain1, g_bias1, g_sigma, g_class, g_wemb, g_bemb = call(
        lambda *refs: kernel_last_side(size, refs[:count_side], *refs[count_side:]),
        [(v, VM) for v in side] + [(index, VM), (emb, VM)],
        [line(size)] * 5
        + [tables(sigma_table.shape[0]), tables(class_table.shape[0]), tables(width), line(2 * size)],
        [vmem((2 * size, 128), F32)], name="last_side",
    )
    other = lambda full, got: lax.dynamic_update_slice(full, got[None], (1 - core, 0, 0))
    output = other(out, out_got)
    input_grad = other(ig, ig_got)
    place = lambda v: jnp.transpose(v, (0, 1, 3, 2))
    return (
        output, input_grad, g_sigma.T, g_class.T, g_wemb.T, g_bemb, g_gain1, g_bias1, place(g_conv1),
        g_bconv1, g_gain2, g_bias2, place(g_conv2), g_bconv2, g_gain3, g_bias3, g_qkv.T, g_bqv,
        g_proj.T, g_bproj,
    )


def solution(mesh):
    every = ("dp", "pipe")
    return jax.shard_map(
        body,
        mesh=mesh,
        in_specs=(P("dp", None, None), P("dp", None, None), P("dp"), P("dp")) + (P(),) * 18,
        out_specs=(
            P("dp", "pipe", None), P("dp", "pipe", None), P(None, every), P(None, every),
            P(None, every), P(every), P(every), P(every), P(None, None, None, every), P(every),
            P(every), P(every), P(None, None, None, every), P(every), P(every), P(every),
            P(None, every), P(every), P(None, every), P(every),
        ),
        check_vma=False,
    )
```

```python
import jax
import jax.numpy as jnp
from jax import lax
from jax.experimental import pallas as pl
from jax.experimental.pallas import tpu as pltpu
from jax.sharding import PartitionSpec as P

HEADS = 6
GROUPS = 32
SIDE = 32
EPS = 1e-05
LOG2E = 1.4426950408889634
BF = jnp.bfloat16
F32 = jnp.float32
NN = (((1,), (0,)), ((), ()))
NT = (((1,), (1,)), ((), ()))
TN = (((0,), (0,)), ((), ()))


def mm(a, b, dims=NN):
    return lax.dot_general(a, b, dims, preferred_element_type=F32)


def silu(v):
    return v * jax.nn.sigmoid(v)


def silu_slope(v):
    s = jax.nn.sigmoid(v)
    return s * (1.0 + v * (1.0 - s))


def lanes(shape):
    return lax.broadcasted_iota(jnp.int32, shape, 1)


def rowsum(v):
    return jnp.sum(v, axis=1, keepdims=True)


def shift_cols(a, d):
    if d == 0:
        return a
    n = a.shape[1]
    col = lanes(a.shape) & (SIDE - 1)
    ok = (col + d >= 0) & (col + d < SIDE)
    return jnp.where(ok, pltpu.roll(a, (-d) % n, 1), 0)


def shift_rows(a, d):
    if d == 0:
        return a
    n = a.shape[1]
    at = lanes(a.shape) + SIDE * d
    return jnp.where((at >= 0) & (at < n), pltpu.roll(a, (-SIDE * d) % n, 1), 0)


def split3(v):
    hi = v.astype(BF).astype(F32)
    mid = (v - hi).astype(BF).astype(F32)
    return hi, mid, v - hi - mid


def exact_left(matrix, v, dims=NN):
    return sum(mm(matrix, part.astype(BF), dims) for part in split3(v))


def exact_right(v, matrix, dims=NN):
    return sum(mm(part.astype(BF), matrix, dims) for part in split3(v))


def with_columns(block, start, extra):
    lane = lanes(block.shape)
    for n, c in enumerate(extra):
        block = jnp.where(lane == start + n, c, block)
    return block


def exact_columns(matrix, cols):
    parts = [part for col in cols for part in split3(col)]
    block = with_columns(jnp.zeros((cols[0].shape[0], 128), F32), 0, parts)
    got = mm(matrix, block.astype(BF))
    return [rowsum(got[:, 3 * at : 3 * at + 3]) for at in range(len(cols))]


def divide(v, size, top):
    scale = -(-(1 << 19) // size)
    assert all((n * scale) >> 19 == n // size for n in range(top))
    return (v * scale) >> 19


def group_matrix(channels):
    size = channels // GROUPS
    shape = (channels, channels)
    row = divide(lax.broadcasted_iota(jnp.int32, (channels, 1), 0), size, channels)
    col = divide(lax.broadcasted_iota(jnp.int32, (1, channels), 1), size, channels)
    return jnp.where(row == col, 1.0, jnp.zeros(shape, F32)).astype(BF)


def group_means(cols, pixels):
    channels = cols[0].shape[0]
    count = channels // GROUPS * pixels
    return [got * (1.0 / count) for got in exact_columns(group_matrix(channels), cols)]


def group_stats(v):
    pixels = v.shape[1]
    (mean,) = group_means([rowsum(v)], pixels)
    centred = v - mean
    (var,) = group_means([rowsum(centred * centred)], pixels)
    inverse = lax.rsqrt(var + EPS)
    return centred * inverse, inverse


def group_back(t, u, inverse, gain, sum_t, sum_tu):
    first, second = group_means([gain * sum_t, gain * sum_tu], t.shape[1])
    return (inverse * gain) * t - inverse * first - u * (inverse * second)


def fill_cols(ref, a, sign):
    c = a.shape[0]
    for j in range(3):
        ref[j * c : (j + 1) * c, :] = shift_cols(a, sign * (j - 1)).astype(BF)


def conv_apply(w_ref, cat_ref, sign, channels):
    total = None
    for i in range(3):
        y = mm(w_ref[i * channels : (i + 1) * channels, :], cat_ref[...])
        y = shift_rows(y, sign * (i - 1))
        total = y if total is None else total + y
    return total


def fill_forward(wf, w_ref, channels):
    for i in range(3):
        for j in range(3):
            at = (slice(i * channels, (i + 1) * channels), slice(j * channels, (j + 1) * channels))
            wf[at] = w_ref[i, j].T


def copies(pairs, sems):
    made = [pltpu.make_async_copy(src, dst, sems.at[n]) for n, (src, dst) in enumerate(pairs)]
    for one in made:
        one.start()
    return made


def tap_pairs(w_ref, wb, channels):
    return [
        (
            w_ref.at[i, j],
            wb.at[
                i * channels : (i + 1) * channels, j * channels : (j + 1) * channels
            ],
        )
        for i in range(3)
        for j in range(3)
    ]


def stream_order(core, bits, late=False):
    order = list(range(bits))
    if core:
        for at in range(0, bits - 1, 2):
            order[at], order[at + 1] = order[at + 1], order[at]
    if late:
        order.append(order.pop(1))
    return order


def row_matrix(channels, bits, late=False):
    dp, core = lax.axis_index("dp"), lax.axis_index("pipe")
    size = channels // (2 << bits)
    quarter = channels // 4
    row = lax.broadcasted_iota(jnp.int32, (channels, 1), 0)
    part_of = sum(jnp.where(row >= quarter * n, 1, 0) for n in (1, 2, 3))
    rest = row - part_of * quarter
    at = divide(rest, size, quarter)
    within = rest - at * size
    part = jnp.where(part_of < 2, core, 1 - core)
    flips = []
    for p in (0, 1):
        order = stream_order(p, bits, late)
        flip = (part_of & 1) << order[0]
        for t in range(bits - 1):
            flip = flip | (((at >> (bits - 2 - t)) & 1) << order[t + 1])
        flips.append(flip)
    peer = dp ^ jnp.where(part == 0, flips[0], flips[1])
    wanted = (2 * peer + part) * size + within
    shape = (channels, channels)
    return jnp.where(wanted == lanes((1, channels)), 1.0, jnp.zeros(shape, F32)).astype(BF)


def own_image():
    return 2 * lax.axis_index("dp") + lax.axis_index("pipe")


def kernel_start(
    total, sig_at, cls_at, x_ref, w1_ref, *refs
):
    count = 14
    places, rest = refs[:count], refs[count:]
    stat_ref, acts_ref, u1_ref, u2_ref = rest[:4]
    x, w1, act1, act2, told, u1, u2, wf, cat, sems = rest[4:14]
    held = rest[14:]
    bemb, g1, b1, bc1, g2, b2, bc2, g3, b3, bqv, bp, wemb, sig_table, cls_table = held
    core = lax.axis_index("pipe")
    channels = x.shape[1]
    loads = copies(
        [(x_ref.at[core], x), (w1_ref, w1)] + list(zip(places, held)), sems.at[: 2 + count]
    )
    sig = jnp.where(core == 0, sig_at[0], sig_at[1])
    cls = jnp.where(core == 0, cls_at[0], cls_at[1])
    lane = lanes(told.shape)
    line = jnp.zeros(told.shape, F32)
    for n, digit in enumerate((sig // 32, sig % 32, cls // 32, cls % 32)):
        line = jnp.where(lane == n * total + own_image(), digit.astype(F32), line)
    told[...] = line.astype(BF)
    loads[0].wait()
    v1, inv1 = group_stats(x[...].astype(F32).T)
    u1[...] = v1
    loads[1].wait()
    fill_forward(wf, w1, channels)
    for one in loads[2:]:
        one.wait()

    def table_row(table, found):
        hot = jnp.where(lanes((16, table.shape[0])) == found, 1.0, 0.0).astype(BF)
        return mm(hot, table[...])[0:1]

    emb = table_row(sig_table, sig) + table_row(cls_table, cls)
    flat = lambda ref: ref[...].astype(F32).reshape(1, ref.shape[0])
    bqv_row = flat(bqv)
    rows = [flat(ref) for ref in (g1, b1, bc1, g2, b2, bc2, g3, b3)]
    rows += [bqv_row[:, :channels], bqv_row[:, channels:], flat(bp)]
    low = jnp.broadcast_to(silu(emb), (16, emb.shape[1])).astype(BF)
    affine = mm(low, wemb[...])[0:1] + flat(bemb)
    rows += [affine[:, :channels], affine[:, channels:], emb[:, :channels], emb[:, channels:]]
    prm = jnp.zeros((128, channels), F32)
    at = lax.broadcasted_iota(jnp.int32, prm.shape, 0)
    for n, line in enumerate(rows):
        prm = jnp.where(at == n, line, prm)
    stat = prm.T
    col = lambda n: stat[:, n : n + 1]
    a1 = silu(v1 * col(0) + col(1))
    act1[...] = a1.astype(BF)
    stores = copies(
        [(u1, u1_ref), (act1, acts_ref.at[:channels]), (told, acts_ref.at[2 * channels :])],
        sems.at[16:19],
    )
    fill_cols(cat, a1, 1)
    v2, inv2 = group_stats(conv_apply(wf, cat, 1, channels) + col(2))
    u2[...] = v2
    scale, shift = col(11), col(12)
    a2 = silu(v2 * (col(3) * (1.0 + scale)) + (col(4) * (1.0 + scale) + shift))
    act2[...] = a2.astype(BF)
    stores += copies([(u2, u2_ref), (act2, acts_ref.at[channels : 2 * channels])], sems.at[19:21])
    stat_ref[...] = with_columns(stat, 32, [inv1, inv2])
    for one in stores:
        one.wait()


def prepare_heads(q_t, k_t, v_t, q_nt, k_nt, v_nt, head):
    pix = q_t.shape[1]
    ones = jnp.where(lanes((pix, head)) < 2, 1.0, 0.0).astype(BF)
    for h in range(HEADS):
        at = slice(h * head, (h + 1) * head)
        q_nt[h] = q_t[at, :].T
        k_nt[h] = k_t[at, :].T
        v_nt[h, :, :head] = v_t[at, :].T
        v_nt[h, :, head:] = ones


def largest_score(q_t, k_t, head):
    worst = jnp.zeros((1, 1), F32)
    for h in range(HEADS):
        longest = []
        for ref in (q_t, k_t):
            v = ref[h * head : (h + 1) * head, :].astype(F32)
            longest.append(
                jnp.max(jnp.sum(v * v, axis=0, keepdims=True), axis=1, keepdims=True)
            )
        worst = jnp.maximum(worst, longest[0] * longest[1])
    return worst[0, 0]


def head_forward(bounded, h, head, q_t, v_t, ga_t, k_nt, at_t):
    pix = q_t.shape[1]
    at = pl.ds(pl.multiple_of(h * head, head), head)
    s = mm(k_nt[h], q_t[at, :])
    if not bounded:
        s = s - jnp.max(s, axis=0, keepdims=True)
    e = jnp.exp2(s * (head ** (-0.5) * LOG2E)).astype(BF)
    o = mm(jnp.concatenate([v_t[at, :], jnp.ones((16, pix), BF)], axis=0), e)
    inv = 1.0 / o[head : head + 1]
    o = o[:head] * inv
    at_t[at, :] = o.astype(BF)
    g = ga_t[at, :].astype(F32)
    centre = -jnp.sum(g * o, axis=0, keepdims=True) * inv
    g = (g * inv).astype(BF)
    hi = centre.astype(BF).astype(F32)
    line = lax.broadcasted_iota(jnp.int32, (head, pix), 0)
    tail = jnp.where(line == 0, hi, jnp.where(line == 1, centre - hi, 0.0)).astype(BF)
    return e, g, tail


def head_backward(h, head, e, g, tail, k_t, q_nt, v_nt, gq_t):
    channels = k_t.shape[0]
    factor = head ** (-0.5)
    rows = lambda base: pl.ds(pl.multiple_of(base + h * head, head), head)
    ds = (e.astype(F32) * mm(v_nt[h], jnp.concatenate([g, tail], axis=0))).astype(BF)
    gq_t[rows(2 * channels), :] = mm(e, g.T).T.astype(BF)
    gq_t[rows(0), :] = (mm(k_t[rows(0), :], ds) * factor).astype(BF)
    gq_t[rows(channels), :] = (mm(ds, q_nt[h]) * factor).T.astype(BF)


def kernel_attention(
    bits, stat_ref, acts_ref, x_ref, cot_ref, w2_ref, wqkv_ref, wproj_ref,
    out_ref, outs_ref, hg_ref, gown_ref, gsame_ref, gcore_ref, gcross_ref, gproj_ref,
    act2, x, cot, w2, wqkv, wproj, wf, cat, wide, tall, q_nt, k_nt, v_nt, q_t, k_t, v_t, ga_t, at_t,
    gq_t, cot_t, out, stat, sems,
):
    core = lax.axis_index("pipe")
    channels, pix = act2.shape
    head = channels // HEADS
    half = channels // 2
    loads = copies(
        [(acts_ref.at[channels : 2 * channels], act2), (w2_ref, w2), (x_ref.at[core], x), (wqkv_ref, wqkv),
         (cot_ref.at[core], cot), (wproj_ref, wproj), (stat_ref, stat)],
        sems,
    )
    col = lambda n: stat[:, n : n + 1]
    loads[0].wait()
    fill_cols(cat, act2[...].astype(F32), 1)
    loads[1].wait()
    fill_forward(wf, w2, channels)
    loads[6].wait()
    conv = conv_apply(wf, cat, 1, channels) + col(5)
    loads[2].wait()
    hidden = (x[...].astype(F32).T + conv).astype(BF).astype(F32)
    u3, inv3 = group_stats(hidden)
    normed = (u3 * col(6) + col(7)).astype(BF)
    loads[3].wait()
    projected = mm(wqkv[...], normed, TN)
    q_t[...] = (projected[:channels] + col(8)).astype(BF)
    k_t[...] = projected[channels : 2 * channels].astype(BF)
    v_t[...] = (projected[2 * channels :] + col(9)).astype(BF)
    loads[4].wait()
    cot_t[...] = cot[...].T
    loads[5].wait()
    ga_t[...] = mm(wproj[...], cot_t[...]).astype(BF)
    prepare_heads(q_t, k_t, v_t, q_nt, k_nt, v_nt, head)

    forward = lambda bounded, h: head_forward(bounded, h, head, q_t, v_t, ga_t, k_nt, at_t)
    backward = lambda h, kept: head_backward(h, head, *kept, k_t, q_nt, v_nt, gq_t)

    def all_heads(bounded):
        def some_heads(t, _):
            for n in range(2):
                backward(2 * t + n, forward(bounded, 2 * t + n))
            return 0

        lax.fori_loop(0, HEADS // 2, some_heads, 0)

    small = largest_score(q_t, k_t, head) <= (60.0 / head ** (-0.5)) ** 2
    pl.when(small)(lambda: all_heads(True))
    pl.when(jnp.logical_not(small))(lambda: all_heads(False))
    out[...] = (hidden + mm(wproj[...], at_t[...], TN) + col(10)).T.astype(BF)
    rows = lambda c: pl.ds(pl.multiple_of(c * (pix // 2), pix // 2), pix // 2)
    stores = copies(
        [(out.at[rows(core)], out_ref.at[core]), (out.at[rows(1 - core)], outs_ref)], sems.at[7:9]
    )
    perm = row_matrix(channels, bits, True)
    got = mm(gq_t[...], normed, NT)
    tiles = channels // 128
    for t in range(tiles):
        wide[t] = got[:, t * 128 : (t + 1) * 128]
    quarter = channels // 4
    pieces = (gown_ref, gsame_ref, gcore_ref, gcross_ref)

    def spread(base, rows):
        for n, ref in enumerate(pieces):
            ref[:, base : base + rows.shape[1]] = rows[n * quarter : (n + 1) * quarter].astype(BF)

    for n in range(3):
        part = jnp.concatenate(
            [wide[t, pl.ds(n, channels, stride=3), :] for t in range(tiles)], axis=1
        )
        spread(pix + n * channels, mm(perm, part.astype(BF)))
    gproj_ref[...] = mm(
        row_matrix(channels, bits), mm(cot_t[...], at_t[...], NT).astype(BF)
    ).astype(BF)
    gn = mm(wqkv[...], gq_t[...])
    s3 = rowsum(gn)
    su3 = rowsum(gn * u3)
    cot_f = cot_t[...].astype(F32)
    hg = (cot_f + group_back(gn, u3, inv3, col(6), s3, su3)).astype(BF)
    hg_ref[...] = hg
    spread(0, mm(perm, hg))
    gq = gq_t[...].astype(F32)
    tall[:channels] = jnp.broadcast_to(rowsum(gq[:channels]), (channels, 128))
    tall[channels:] = jnp.broadcast_to(rowsum(gq[2 * channels :]), (channels, 128))
    side = with_columns(
        jnp.zeros((channels, 128), F32), 0,
        [su3, s3, tall[pl.ds(0, channels, stride=2), :], tall[pl.ds(1, channels, stride=2), :],
         rowsum(cot_f), rowsum(hg.astype(F32))],
    )
    spread(pix + 3 * channels, exact_left(perm, side))
    for one in stores:
        one.wait()


def kernel_second(
    bits, hg, stat_in, gproj, w2_ref, u2_ref,
    stat_ref, dc_ref, gown_ref, gsame_ref, gcore_ref, gcross_ref,
    wb, u2v, cat, slope, tall, sems,
):
    channels = hg.shape[0]
    loads = copies([(u2_ref, u2v)] + tap_pairs(w2_ref, wb, channels), sems)
    stat = stat_in[...]
    col = lambda n: stat[:, n : n + 1]
    g2, b2, scale, shift, inv2 = col(3), col(4), col(11), col(12), col(33)
    gm = g2 * (1.0 + scale)
    fill_cols(cat, hg[...].astype(F32), -1)
    loads[0].wait()
    slope[...] = silu_slope(u2v[...] * gm + (b2 * (1.0 + scale) + shift))
    for one in loads[1:]:
        one.wait()
    u2 = u2v[...]
    dm = conv_apply(wb, cat, -1, channels) * slope[...]
    s = rowsum(dm)
    su = rowsum(dm * u2)
    dc = group_back(dm, u2, inv2, gm, s, su).astype(BF)
    dc_ref[...] = dc
    parts = mm(row_matrix(channels, bits), dc).astype(BF)
    quarter = channels // 4
    for n, ref in enumerate((gown_ref, gsame_ref, gcore_ref, gcross_ref)):
        at = slice(n * quarter, (n + 1) * quarter)
        ref[:, : hg.shape[1]] = parts[at]
        ref[:, hg.shape[1] :] = gproj[at, :]
    stat_ref[...] = with_columns(
        stat, 40,
        [(1.0 + scale) * su, (1.0 + scale) * s, rowsum(dc.astype(F32)), g2 * su + b2 * s, s],
    )


def kernel_first(
    bits, dc, stat_in, w1_ref, u1_ref, wemb_ref,
    dp_ref, stat_ref, own_ref, same_ref, core_ref, cross_ref,
    wb, u1v, cat, slope, wemb, tall, sems,
):
    channels = dc.shape[0]
    quarter = channels // 4
    loads = copies(
        [(u1_ref, u1v), (wemb_ref, wemb)] + tap_pairs(w1_ref, wb, channels), sems
    )
    stat = stat_in[...]
    col = lambda n: stat[:, n : n + 1]
    fill_cols(cat, dc[...].astype(F32), -1)
    loads[0].wait()
    slope[...] = silu_slope(u1v[...] * col(0) + col(1))
    loads[1].wait()

    def even_odd(top, low):
        tall[:channels] = jnp.broadcast_to(top, (channels, 128))
        tall[channels:] = jnp.broadcast_to(low, (channels, 128))
        return [tall[pl.ds(n, channels, stride=2), :][:, :1] for n in range(2)]

    ga = even_odd(col(43), col(44))
    (ge,) = exact_columns(wemb[...], [tall[...][:, :1]])
    ge = even_odd(ge[:channels] * silu_slope(col(13)), ge[channels:] * silu_slope(col(14)))
    for one in loads[2:]:
        one.wait()
    u1 = u1v[...]
    dp = conv_apply(wb, cat, -1, channels) * slope[...]
    s = rowsum(dp)
    su = rowsum(dp * u1)
    dp_ref[...] = dp
    stat_ref[...] = with_columns(stat, 43, [su, s])
    width = own_ref.shape[1]
    total = (width - 128) // 4
    side = with_columns(
        jnp.zeros((channels, width), F32), 0, [col(40), col(41), col(42), su, s]
    )
    lane = lanes((channels, width))
    for n, one in enumerate(ga + ge):
        side = jnp.where(lane == 128 + n * total + own_image(), one, side)
    side = exact_left(row_matrix(channels, bits), side)
    for n, ref in enumerate((own_ref, same_ref, core_ref, cross_ref)):
        ref[...] = side[n * quarter : (n + 1) * quarter].astype(ref.dtype)


def kernel_input(dp, u1_ref, hg, stat, ig_ref, igs_ref, ig, u1, sems):
    (load,) = copies([(u1_ref, u1)], sems.at[2:3])
    core = lax.axis_index("pipe")
    pix = hg.shape[1]
    col = lambda n: stat[:, n : n + 1]
    first, second = group_means([col(0) * col(44), col(0) * col(43)], pix)
    back = (col(32) * col(0)) * dp[...] - col(32) * first
    load.wait()
    back -= u1[...] * (col(32) * second)
    ig[...] = (hg[...].astype(F32) + back).T.astype(BF)
    rows = lambda c: pl.ds(pl.multiple_of(c * (pix // 2), pix // 2), pix // 2)
    stores = copies(
        [(ig.at[rows(core)], ig_ref.at[core]), (ig.at[rows(1 - core)], igs_ref)], sems.at[0:2]
    )
    for one in stores:
        one.wait()


def kernel_weight(which, total_images, sides, *refs):
    acts, pieces, side = refs[:4], refs[4:8], refs[8 : 8 + sides]
    keep_ref, send_ref, act, piece, told, stack, total, sems = refs[8 + sides :]
    rows, channels, pix = piece.shape[1], act.shape[1], act.shape[2]
    half = rows // 2
    at = slice(which * channels, (which + 1) * channels)
    pairs = [(ref, piece.at[n]) for n, ref in enumerate(pieces)]
    pairs += [(ref.at[at], act.at[n]) for n, ref in enumerate(acts)]
    if total_images:
        pairs += [(ref.at[2 * channels :], told.at[n]) for n, ref in enumerate(acts)]
    loads = copies(pairs, sems)

    def build(n):
        g = piece[n, :, :pix].astype(F32)
        for j in range(3):
            moved = shift_cols(g, 1 - j)
            for i in range(3):
                base = (3 * i + j) * rows
                stack[n, base : base + rows, :] = shift_rows(moved, 1 - i).astype(BF)

    loads[0].wait()
    build(0)
    for one in loads[1:8]:
        one.wait()
    for n in range(4):
        if n < 3:
            build(n + 1)
        got = mm(stack[n], act[n], NT)
        total[...] = got if n == 0 else total[...] + got
    for tap in range(9):
        at = slice(tap * channels, (tap + 1) * channels)
        keep_ref[:, at] = total[tap * rows : tap * rows + half, :]
        send_ref[:, at] = total[tap * rows + half : (tap + 1) * rows, :].astype(BF)
    at = slice(9 * channels, 9 * channels + piece.shape[2] - pix)
    more = sum(piece[n, :, pix:].astype(F32) for n in range(4))
    keep_ref[:, at] = more[:half]
    send_ref[:, at] = more[half:].astype(BF)
    if sides:
        more = sum(ref[...].astype(F32) for ref in side)
        keep_ref[:, at.stop :] = more[:half]
        send_ref[:, at.stop :] = more[half:].astype(BF)
    if total_images:
        for one in loads[8:]:
            one.wait()
        line = sum(told[n].astype(F32) for n in range(4))[:1, : 4 * total_images]
        line = jnp.broadcast_to(line, (half, 4 * total_images))
        keep_ref[:, at.stop :] = line
        send_ref[:, at.stop :] = line.astype(BF)


def interleave(ref, parts):
    size = parts[0].shape[0]
    for r in range(size):
        for n, part in enumerate(parts):
            at = len(parts) * r + n
            ref[at : at + 1, : part.shape[1]] = part[r : r + 1]


def summed(parts, size):
    return sum(part[:size].astype(F32) for part in parts)


def kernel_last_two(
    channels, size, parts, sig_ref, cls_ref, conv_ref, qkv_ref, bconv_ref, gain_ref, bias_ref, bqv_ref, bproj_ref, emb_ref, told_ref, rows,
    sig_table, cls_table, sems,
):
    loads = copies([(sig_ref, sig_table), (cls_ref, cls_table)], sems)
    total = summed(parts, size)
    for i in range(3):
        for j in range(3):
            at = (3 * i + j) * channels
            conv_ref[i, j] = total[:, at : at + channels]
    rest = total[:, 9 * channels :]
    interleave(qkv_ref, [rest[:, n * channels : (n + 1) * channels] for n in range(3)])
    side = rest[:, 3 * channels : 3 * channels + 128]
    lines = side.T
    for n, ref in ((0, gain_ref), (1, bias_ref), (4, bproj_ref), (5, bconv_ref)):
        ref[...] = lines[n]
    interleave(rows, [jnp.broadcast_to(side[:, n : n + 1], (size, 128)) for n in (2, 3)])
    bqv_ref[...] = rows[...].T[0]
    told = rest[0:1, 3 * channels + 128 :]
    told_ref[...] = told
    images = told.shape[1] // 4
    hot_sig, hot_cls = hot_rows(told, images, sig_table.shape[0], cls_table.shape[0])
    for one in loads:
        one.wait()
    emb = mm(hot_sig, sig_table[...], TN) + mm(hot_cls, cls_table[...], TN)
    emb_ref[...] = silu(emb).astype(BF)


def hot_rows(told, images, sig_count, cls_count):
    digit = lambda n: told[:, n * images : (n + 1) * images].astype(jnp.int32)
    sig = 32 * digit(0) + digit(1)
    cls = 32 * digit(2) + digit(3)

    def hot(index, count):
        line = lax.broadcasted_iota(jnp.int32, (count, images), 0)
        return jnp.where(line == index, 1.0, 0.0).astype(BF)

    return hot(sig, sig_count), hot(cls, cls_count)


def kernel_last_one(
    channels, size, parts, told_ref, emb_ref, out_in, out_got, ig_in, ig_got, out_ref, ig_ref,
    conv_ref, proj_ref, gain2_ref, bias2_ref, bconv_ref, gain1_ref, bias1_ref, sig_ref, cls_ref,
    wemb_ref, bemb_ref, rows, sems,
):
    other = 1 - lax.axis_index("pipe")
    placed = copies([(out_got, out_ref.at[other]), (ig_got, ig_ref.at[other])], sems)
    total = summed(parts, size)
    for i in range(3):
        for j in range(3):
            at = (3 * i + j) * channels
            conv_ref[i, j] = total[:, at : at + channels]
    proj_ref[...] = total[:, 9 * channels : 10 * channels]
    rest = total[:, 10 * channels :]
    lines = rest[:, :128].T
    for n, ref in enumerate((gain2_ref, bias2_ref, bconv_ref, gain1_ref, bias1_ref)):
        ref[...] = lines[n]
    told = told_ref[...]
    images = told.shape[1] // 4
    part = lambda n: rest[:, 128 + n * images : 128 + (n + 1) * images]
    hot_sig, hot_cls = hot_rows(told, images, sig_ref.shape[1], cls_ref.shape[1])
    into = [part(2), part(3)]
    interleave(sig_ref, [exact_right(v, hot_sig, NT) for v in into])
    interleave(cls_ref, [exact_right(v, hot_cls, NT) for v in into])
    affine = [part(0), part(1)]
    interleave(wemb_ref, [exact_right(v, emb_ref[...]) for v in affine])
    interleave(rows, [jnp.broadcast_to(rowsum(v), (v.shape[0], 128)) for v in affine])
    bemb_ref[...] = rows[...].T[0]
    for one in placed:
        one.wait()


VM = pl.BlockSpec(memory_space=pltpu.VMEM)
ANY = pl.BlockSpec(memory_space=pl.ANY)
HBM = pl.BlockSpec(memory_space=pltpu.HBM)
SM = pl.BlockSpec(memory_space=pltpu.SMEM)


def vmem(shape, dtype=BF):
    return pltpu.VMEM(shape, dtype)


def call(kernel, operands, outs, scratch, after=(), alias=(), limit=20, flops=0, name=None):
    count = len(operands)
    operands = [
        (pltpu.with_memory_space_constraint(v, pltpu.HBM) if spec is HBM else v, spec)
        for v, spec in operands
    ]
    operands += [(v, ANY) for v in after]

    def ordered(*refs):
        kernel(*refs[:count], *refs[len(operands) :])

    return pl.pallas_call(
        ordered,
        out_shape=[jax.ShapeDtypeStruct(shape, dtype) for shape, dtype, _ in outs],
        in_specs=[spec for _, spec in operands],
        out_specs=[spec for _, _, spec in outs],
        scratch_shapes=scratch,
        input_output_aliases=dict(alias),
        compiler_params=pltpu.CompilerParams(vmem_limit_bytes=limit * 2**20),
        cost_estimate=pl.CostEstimate(flops=flops, bytes_accessed=10**6, transcendentals=0),
        name=name,
    )(*[operand for operand, _ in operands])


def swap_core(v):
    return lax.ppermute(v, "pipe", [(0, 1), (1, 0)])


def joint(v, target):
    pairs = []
    for dp in range(lax.axis_size("dp")):
        for core in range(2):
            to_dp, to_core = target(dp, core)
            pairs.append((2 * dp + core, 2 * to_dp + to_core))
    return lax.ppermute(v, ("dp", "pipe"), pairs)


def exchange(v, step, bits, late=False):
    return joint(v, lambda dp, core: (dp ^ (1 << stream_order(core, bits, late)[step]), core))


def cross(v, bits):
    return joint(v, lambda dp, core: (dp ^ (1 << stream_order(1 - core, bits)[0]), 1 - core))


def leaving(parts, rows):
    return sum(part[rows // 2 : rows].astype(F32) for part in parts).astype(BF)


def gathered(own, to_core, to_same, to_cross, bits):
    return [own, swap_core(to_core), exchange(to_same, 0, bits), cross(to_cross, bits)]


def body(
    block_input, cotangent, sigma_index, class_label, sigma_table, class_table, w_emb, b_emb,
    norm1_gain, norm1_bias, w_conv1, b_conv1, norm2_gain, norm2_bias, w_conv2, b_conv2,
    norm3_gain, norm3_bias, w_qkv, b_qv, w_proj, b_proj,
):
    data = lax.axis_size("dp")
    bits = data.bit_length() - 1
    images, pix, c = block_input.shape
    total = 2 * data
    width = sigma_table.shape[1]
    head, half, quarter, size = c // HEADS, c // 2, c // 4, c // (2 * data)
    dma = lambda count: pltpu.SemaphoreType.DMA((count,))
    field = ((c, pix), BF)
    vectors = [b_emb, norm1_gain, norm1_bias, b_conv1, norm2_gain, norm2_bias, b_conv2, norm3_gain,
               norm3_bias, b_qv, b_proj]
    told = 4 * total
    places = vectors + [w_emb, sigma_table, class_table]
    stat, acts, u1, u2 = call(
        lambda *refs: kernel_start(total, *refs),
        [(sigma_index, SM), (class_label, SM), (block_input, HBM), (w_conv1, HBM)]
        + [(v, HBM) for v in places],
        [((c, 128), F32, VM), ((2 * c + 16, pix), BF, ANY), ((c, pix), F32, ANY),
         ((c, pix), F32, ANY)],
        [vmem((pix, c)), vmem(w_conv1.shape), vmem((c, pix)), vmem((c, pix)), vmem((16, pix)),
         vmem((c, pix), F32), vmem((c, pix), F32), vmem((3 * c, 3 * c)), vmem((3 * c, pix)),
         dma(21)] + [vmem(v.shape) for v in places],
        limit=60, flops=10**11, name="start",
    )
    acts = gathered(acts, acts, acts, acts, bits)
    nat = vmem((HEADS, pix, head))
    piece = lambda more: [((quarter, pix + more), BF, VM)] * 4
    more2 = 3 * c + 128
    out, out_send, hg, gown, gsame, gcore, gcross, gproj = call(
        lambda *refs: kernel_attention(bits, *refs),
        [(stat, HBM), (acts[0], HBM), (block_input, HBM),
         (cotangent, HBM), (w_conv2, HBM), (w_qkv, HBM), (w_proj, HBM)],
        [((images, pix // 2, c), BF, ANY), ((pix // 2, c), BF, ANY),
         field + (VM,)] + piece(more2) + [((c, c), BF, VM)],
        [vmem((c, pix)), vmem((pix, c)), vmem((pix, c)), vmem(w_conv2.shape), vmem(w_qkv.shape),
         vmem(w_proj.shape), vmem((3 * c, 3 * c)), vmem((3 * c, pix)),
         vmem((c // 128, 3 * c, 128), F32), vmem((2 * c, 128), F32), nat, nat,
         vmem((HEADS, pix, 2 * head)), vmem((c, pix)), vmem((c, pix)), vmem((c, pix)),
         vmem((c, pix)), vmem((c, pix)), vmem((3 * c, pix)), vmem((c, pix)), vmem((pix, c)),
         vmem((c, 128), F32), dma(9)],
        limit=48, flops=400 * 10**9, name="attention",
    )
    grads2 = gathered(gown, gcore, gsame, gcross, bits)
    out_got = swap_core(out_send)
    stat, dc, gown, gsame, gcore, gcross = call(
        lambda *refs: kernel_second(bits, *refs),
        [(hg, VM), (stat, VM), (gproj, VM), (w_conv2, ANY), (u2, ANY)],
        [((c, 128), F32, VM), field + (VM,)] + piece(c),
        [vmem((3 * c, 3 * c)), vmem((c, pix), F32), vmem((3 * c, pix)), vmem((c, pix), F32),
         vmem((2 * c, 128), F32), dma(10)],
        after=acts[1:], flops=200 * 10**9, name="second",
    )
    grads1 = gathered(gown, gcore, gsame, gcross, bits)

    def weight(which, grads, count, side, after, name):
        more = grads[0].shape[1] - pix
        columns = 9 * c + more + 4 * count + (side[0].shape[1] if side else 0)
        return call(
            lambda *refs: kernel_weight(which, count, len(side), *refs),
            [(v, ANY) for v in acts + grads] + [(v, VM) for v in side],
            [((quarter // 2, columns), F32, VM), ((quarter // 2, columns), BF, VM)],
            [vmem((4, c, pix)), vmem((4, quarter, pix + more)), vmem((4, 16, pix)),
             vmem((4, 9 * quarter, pix)), vmem((9 * quarter, c), F32), dma(12)],
            after=after, limit=28, flops=200 * 10**9, name=name,
        )

    rows = [quarter >> step for step in range(bits)]
    keep2, send2 = weight(1, grads2, total, [], [dc, out_got], "weight_two")
    two = [keep2, exchange(send2, 1, bits, True)]
    dp, stat, own, same, to_core, to_cross = call(
        lambda *refs: kernel_first(bits, *refs),
        [(dc, VM), (stat, VM), (w_conv1, ANY), (u1, ANY), (w_emb, ANY)],
        [((c, pix), F32, VM), ((c, 128), F32, VM), ((quarter, 128 + told), F32, VM)]
        + [((quarter, 128 + told), BF, VM)] * 3,
        [vmem((3 * c, 3 * c)), vmem((c, pix), F32), vmem((3 * c, pix)), vmem((c, pix), F32),
         vmem(w_emb.shape), vmem((2 * c, 128), F32), dma(11)],
        after=[keep2] + grads1[1:], flops=200 * 10**9, name="first",
    )
    side = gathered(own, to_core, same, to_cross, bits)
    keep1, send1 = weight(0, grads1, 0, side, [own, two[1]], "weight_one")
    one = [keep1, exchange(send1, 1, bits)]
    two[1], send1 = lax.optimization_barrier((two[1], send1))
    two.append(exchange(leaving(two, rows[1]), 2, bits, True))
    send1 = leaving(one, rows[1])
    one.append(exchange(send1, 2, bits))
    ig, ig_send = call(
        kernel_input,
        [(dp, VM), (u1, HBM), (hg, VM), (stat, VM)],
        [((images, pix // 2, c), BF, ANY), ((pix // 2, c), BF, ANY)],
        [vmem((pix, c)), vmem((c, pix), F32), dma(3)],
        after=[send1], flops=200 * 10**9, name="input",
    )
    two[2], ig_send = lax.optimization_barrier((two[2], ig_send))
    ig_got = swap_core(ig_send)
    for step in range(3, bits):
        two.append(exchange(leaving(two, rows[step - 1]), step, bits, True))
    for step in range(3, bits):
        one.append(exchange(leaving(one, rows[step - 1]), step, bits))
    line = lambda n: ((n,), F32, VM)
    conv = ((3, 3, size, c), F32, VM)
    count = len(two)
    g_conv2, g_qkv, g_bconv2, g_gain3, g_bias3, g_bqv, g_bproj, emb, index = call(
        lambda *refs: kernel_last_two(c, size, refs[:count], *refs[count:]),
        [(v, VM) for v in two] + [(sigma_table, HBM), (class_table, HBM)],
        [conv, ((3 * size, c), F32, VM), line(size), line(size), line(size),
         line(2 * size), line(size), ((total, width), BF, VM), ((1, told), F32, VM)],
        [vmem((2 * size, 128), F32), vmem(sigma_table.shape), vmem(class_table.shape), dma(2)],
        name="last_two",
    )
    one[-1], emb = lax.optimization_barrier((one[-1], emb))
    tables = lambda count: ((2 * size, count), F32, VM)
    count_one = len(one)
    image_half = (out.shape, BF, ANY)
    (output, input_grad, g_conv1, g_proj, g_gain2, g_bias2, g_bconv1, g_gain1, g_bias1, g_sigma, g_class, g_wemb,
     g_bemb) = call(
        lambda *refs: kernel_last_one(c, size, refs[:count_one], *refs[count_one:]),
        [(v, VM) for v in one]
        + [(index, VM), (emb, VM), (out, ANY), (out_got, VM), (ig, ANY), (ig_got, VM)],
        [image_half, image_half, conv, ((size, c), F32, VM)] + [line(size)] * 5
        + [tables(sigma_table.shape[0]), tables(class_table.shape[0]), tables(width), line(2 * size)],
        [vmem((2 * size, 128), F32), dma(2)],
        alias=[(count_one + 2, 0), (count_one + 4, 1)], name="last_one",
    )
    place = lambda v: jnp.transpose(v, (0, 1, 3, 2))
    return (
        output, input_grad, g_sigma.T, g_class.T, g_wemb.T, g_bemb, g_gain1, g_bias1, place(g_conv1),
        g_bconv1, g_gain2, g_bias2, place(g_conv2), g_bconv2, g_gain3, g_bias3, g_qkv.T, g_bqv,
        g_proj.T, g_bproj,
    )


def solution(mesh):
    every = ("dp", "pipe")
    return jax.shard_map(
        body,
        mesh=mesh,
        in_specs=(P("dp", None, None), P("dp", None, None), P("dp"), P("dp")) + (P(),) * 18,
        out_specs=(
            P("dp", "pipe", None), P("dp", "pipe", None), P(None, every), P(None, every),
            P(None, every), P(every), P(every), P(every), P(None, None, None, every), P(every),
            P(every), P(every), P(None, None, None, every), P(every), P(every), P(every),
            P(None, every), P(every), P(None, every), P(every),
        ),
        check_vma=False,
    )
```

```python
import jax
import jax.numpy as jnp
from jax import lax
from jax.experimental import pallas as pl
from jax.experimental.pallas import tpu as pltpu
from jax.sharding import PartitionSpec as P

HEADS = 6
GROUPS = 32
SIDE = 32
EPS = 1e-05
LOG2E = 1.4426950408889634
BF = jnp.bfloat16
F32 = jnp.float32
NN = (((1,), (0,)), ((), ()))
NT = (((1,), (1,)), ((), ()))
TN = (((0,), (0,)), ((), ()))


def mm(a, b, dims=NN):
    return lax.dot_general(a, b, dims, preferred_element_type=F32)


def silu(v):
    return v * jax.nn.sigmoid(v)


def silu_slope(v):
    s = jax.nn.sigmoid(v)
    return s * (1.0 + v * (1.0 - s))


def lanes(shape):
    return lax.broadcasted_iota(jnp.int32, shape, 1)


def rowsum(v):
    return jnp.sum(v, axis=1, keepdims=True)


def shift_cols(a, d):
    if d == 0:
        return a
    n = a.shape[1]
    col = lanes(a.shape) & (SIDE - 1)
    ok = (col + d >= 0) & (col + d < SIDE)
    return jnp.where(ok, pltpu.roll(a, (-d) % n, 1), 0)


def shift_rows(a, d):
    if d == 0:
        return a
    n = a.shape[1]
    at = lanes(a.shape) + SIDE * d
    return jnp.where((at >= 0) & (at < n), pltpu.roll(a, (-SIDE * d) % n, 1), 0)


def split3(v):
    hi = v.astype(BF).astype(F32)
    mid = (v - hi).astype(BF).astype(F32)
    return hi, mid, v - hi - mid


def exact_left(matrix, v, dims=NN):
    return sum(mm(matrix, part.astype(BF), dims) for part in split3(v))


def exact_right(v, matrix, dims=NN):
    return sum(mm(part.astype(BF), matrix, dims) for part in split3(v))


def with_columns(block, start, extra):
    lane = lanes(block.shape)
    for n, c in enumerate(extra):
        block = jnp.where(lane == start + n, c, block)
    return block


def exact_columns(matrix, cols):
    parts = [part for col in cols for part in split3(col)]
    block = with_columns(jnp.zeros((cols[0].shape[0], 128), F32), 0, parts)
    got = mm(matrix, block.astype(BF))
    return [rowsum(got[:, 3 * at : 3 * at + 3]) for at in range(len(cols))]


def divide(v, size, top):
    scale = -(-(1 << 19) // size)
    assert all((n * scale) >> 19 == n // size for n in range(top))
    return (v * scale) >> 19


def group_matrix(channels):
    size = channels // GROUPS
    shape = (channels, channels)
    row = divide(lax.broadcasted_iota(jnp.int32, (channels, 1), 0), size, channels)
    col = divide(lax.broadcasted_iota(jnp.int32, (1, channels), 1), size, channels)
    return jnp.where(row == col, 1.0, jnp.zeros(shape, F32)).astype(BF)


def group_means(cols, pixels):
    channels = cols[0].shape[0]
    count = channels // GROUPS * pixels
    return [got * (1.0 / count) for got in exact_columns(group_matrix(channels), cols)]


def group_stats(v):
    pixels = v.shape[1]
    (mean,) = group_means([rowsum(v)], pixels)
    centred = v - mean
    (var,) = group_means([rowsum(centred * centred)], pixels)
    inverse = lax.rsqrt(var + EPS)
    return centred * inverse, inverse


def group_back(t, u, inverse, gain, sum_t, sum_tu):
    first, second = group_means([gain * sum_t, gain * sum_tu], t.shape[1])
    return (inverse * gain) * t - inverse * first - u * (inverse * second)


def fill_cols(ref, a, sign):
    c = a.shape[0]
    for j in range(3):
        ref[j * c : (j + 1) * c, :] = shift_cols(a, sign * (j - 1)).astype(BF)


def conv_apply(w_ref, cat_ref, sign, channels):
    total = None
    for i in range(3):
        y = mm(w_ref[i * channels : (i + 1) * channels, :], cat_ref[...])
        y = shift_rows(y, sign * (i - 1))
        total = y if total is None else total + y
    return total


def fill_forward(wf, w_ref, channels):
    for i in range(3):
        for j in range(3):
            at = (slice(i * channels, (i + 1) * channels), slice(j * channels, (j + 1) * channels))
            wf[at] = w_ref[i, j].T


def copies(pairs, sems):
    made = [pltpu.make_async_copy(src, dst, sems.at[n]) for n, (src, dst) in enumerate(pairs)]
    for one in made:
        one.start()
    return made


def tap_pairs(w_ref, wb, channels):
    return [
        (
            w_ref.at[i, j],
            wb.at[
                i * channels : (i + 1) * channels, j * channels : (j + 1) * channels
            ],
        )
        for i in range(3)
        for j in range(3)
    ]


def stream_order(core, bits):
    order = list(range(bits))
    if core:
        for at in range(0, bits - 1, 2):
            order[at], order[at + 1] = order[at + 1], order[at]
    return order


def row_matrix(channels, bits):
    dp, core = lax.axis_index("dp"), lax.axis_index("pipe")
    size = channels // (2 << bits)
    quarter = channels // 4
    row = lax.broadcasted_iota(jnp.int32, (channels, 1), 0)
    part_of = sum(jnp.where(row >= quarter * n, 1, 0) for n in (1, 2, 3))
    rest = row - part_of * quarter
    at = divide(rest, size, quarter)
    within = rest - at * size
    part = jnp.where(part_of < 2, core, 1 - core)
    flips = []
    for p in (0, 1):
        order = stream_order(p, bits)
        flip = (part_of & 1) << order[0]
        for t in range(bits - 1):
            flip = flip | (((at >> (bits - 2 - t)) & 1) << order[t + 1])
        flips.append(flip)
    peer = dp ^ jnp.where(part == 0, flips[0], flips[1])
    wanted = (2 * peer + part) * size + within
    shape = (channels, channels)
    return jnp.where(wanted == lanes((1, channels)), 1.0, jnp.zeros(shape, F32)).astype(BF)


def own_image():
    return 2 * lax.axis_index("dp") + lax.axis_index("pipe")


def kernel_start(
    total, sig_at, cls_at, x_ref, w1_ref, *refs
):
    count = 14
    places, rest = refs[:count], refs[count:]
    stat_ref, acts_ref, u1_ref, u2_ref = rest[:4]
    x, w1, act1, act2, told, u1, u2, wf, cat, sems = rest[4:14]
    held = rest[14:]
    bemb, g1, b1, bc1, g2, b2, bc2, g3, b3, bqv, bp, wemb, sig_table, cls_table = held
    core = lax.axis_index("pipe")
    channels = x.shape[1]
    loads = copies(
        [(x_ref.at[core], x), (w1_ref, w1)] + list(zip(places, held)), sems.at[: 2 + count]
    )
    sig = jnp.where(core == 0, sig_at[0], sig_at[1])
    cls = jnp.where(core == 0, cls_at[0], cls_at[1])
    lane = lanes(told.shape)
    line = jnp.zeros(told.shape, F32)
    for n, digit in enumerate((sig // 32, sig % 32, cls // 32, cls % 32)):
        line = jnp.where(lane == n * total + own_image(), digit.astype(F32), line)
    told[...] = line.astype(BF)
    loads[0].wait()
    v1, inv1 = group_stats(x[...].astype(F32).T)
    u1[...] = v1
    loads[1].wait()
    fill_forward(wf, w1, channels)
    for one in loads[2:]:
        one.wait()

    def table_row(table, found):
        hot = jnp.where(lanes((16, table.shape[0])) == found, 1.0, 0.0).astype(BF)
        return mm(hot, table[...])[0:1]

    emb = table_row(sig_table, sig) + table_row(cls_table, cls)
    flat = lambda ref: ref[...].astype(F32).reshape(1, ref.shape[0])
    bqv_row = flat(bqv)
    rows = [flat(ref) for ref in (g1, b1, bc1, g2, b2, bc2, g3, b3)]
    rows += [bqv_row[:, :channels], bqv_row[:, channels:], flat(bp)]
    low = jnp.broadcast_to(silu(emb), (16, emb.shape[1])).astype(BF)
    affine = mm(low, wemb[...])[0:1] + flat(bemb)
    rows += [affine[:, :channels], affine[:, channels:], emb[:, :channels], emb[:, channels:]]
    prm = jnp.zeros((128, channels), F32)
    at = lax.broadcasted_iota(jnp.int32, prm.shape, 0)
    for n, line in enumerate(rows):
        prm = jnp.where(at == n, line, prm)
    stat = prm.T
    col = lambda n: stat[:, n : n + 1]
    a1 = silu(v1 * col(0) + col(1))
    act1[...] = a1.astype(BF)
    stores = copies(
        [(u1, u1_ref), (act1, acts_ref.at[:channels]), (told, acts_ref.at[2 * channels :])],
        sems.at[16:19],
    )
    fill_cols(cat, a1, 1)
    v2, inv2 = group_stats(conv_apply(wf, cat, 1, channels) + col(2))
    u2[...] = v2
    scale, shift = col(11), col(12)
    a2 = silu(v2 * (col(3) * (1.0 + scale)) + (col(4) * (1.0 + scale) + shift))
    act2[...] = a2.astype(BF)
    stores += copies([(u2, u2_ref), (act2, acts_ref.at[channels : 2 * channels])], sems.at[19:21])
    stat_ref[...] = with_columns(stat, 32, [inv1, inv2])
    for one in stores:
        one.wait()


def prepare_heads(q_t, k_t, v_t, q_nt, k_nt, v_nt, head):
    pix = q_t.shape[1]
    ones = jnp.where(lanes((pix, head)) < 2, 1.0, 0.0).astype(BF)
    for h in range(HEADS):
        at = slice(h * head, (h + 1) * head)
        q_nt[h] = q_t[at, :].T
        k_nt[h] = k_t[at, :].T
        v_nt[h, :, :head] = v_t[at, :].T
        v_nt[h, :, head:] = ones


def largest_score(q_t, k_t, head):
    worst = jnp.zeros((1, 1), F32)
    for h in range(HEADS):
        longest = []
        for ref in (q_t, k_t):
            v = ref[h * head : (h + 1) * head, :].astype(F32)
            longest.append(
                jnp.max(jnp.sum(v * v, axis=0, keepdims=True), axis=1, keepdims=True)
            )
        worst = jnp.maximum(worst, longest[0] * longest[1])
    return worst[0, 0]


def head_forward(bounded, h, head, q_t, v_t, ga_t, k_nt, at_t):
    pix = q_t.shape[1]
    at = pl.ds(pl.multiple_of(h * head, head), head)
    s = mm(k_nt[h], q_t[at, :])
    if not bounded:
        s = s - jnp.max(s, axis=0, keepdims=True)
    exact = jnp.exp2(s * (head ** (-0.5) * LOG2E))
    e = exact.astype(BF)
    o = mm(jnp.concatenate([v_t[at, :], jnp.ones((16, pix), BF)], axis=0), e)
    inv = 1.0 / o[head : head + 1]
    o = o[:head] * inv
    at_t[at, :] = o.astype(BF)
    g = ga_t[at, :].astype(F32)
    centre = -jnp.sum(g * o, axis=0, keepdims=True)
    g = (g * inv).astype(BF)
    hi = centre.astype(BF).astype(F32)
    line = lax.broadcasted_iota(jnp.int32, (head, pix), 0)
    tail = jnp.where(line == 0, hi, jnp.where(line == 1, centre - hi, 0.0)).astype(BF)
    return exact, e, inv, g, jnp.concatenate([ga_t[at, :], tail], axis=0)


def head_backward(h, head, exact, e, inv, g, upstream, k_t, q_nt, v_nt, gq_t):
    channels = k_t.shape[0]
    factor = head ** (-0.5)
    rows = lambda base: pl.ds(pl.multiple_of(base + h * head, head), head)
    ds = (exact * (mm(v_nt[h], upstream) * inv)).astype(BF)
    gq_t[rows(2 * channels), :] = mm(e, g.T).T.astype(BF)
    gq_t[rows(0), :] = (mm(k_t[rows(0), :], ds) * factor).astype(BF)
    gq_t[rows(channels), :] = (mm(ds, q_nt[h]) * factor).T.astype(BF)


def kernel_attention(
    bits, stat_ref, acts_ref, x_ref, cot_ref, w2_ref, wqkv_ref, wproj_ref,
    out_ref, outs_ref, hg_ref, gown_ref, gsame_ref, gcore_ref, gcross_ref, gproj_ref,
    act2, x, cot, w2, wqkv, wproj, wf, cat, wide, tall, q_nt, k_nt, v_nt, q_t, k_t, v_t, ga_t, at_t,
    gq_t, cot_t, out, stat, sems,
):
    core = lax.axis_index("pipe")
    channels, pix = act2.shape
    head = channels // HEADS
    half = channels // 2
    loads = copies(
        [(acts_ref.at[channels : 2 * channels], act2), (w2_ref, w2), (x_ref.at[core], x), (wqkv_ref, wqkv),
         (cot_ref.at[core], cot), (wproj_ref, wproj), (stat_ref, stat)],
        sems,
    )
    col = lambda n: stat[:, n : n + 1]
    loads[0].wait()
    fill_cols(cat, act2[...].astype(F32), 1)
    loads[1].wait()
    fill_forward(wf, w2, channels)
    loads[6].wait()
    conv = conv_apply(wf, cat, 1, channels) + col(5)
    loads[2].wait()
    hidden = (x[...].astype(F32).T + conv).astype(BF).astype(F32)
    u3, inv3 = group_stats(hidden)
    normed = (u3 * col(6) + col(7)).astype(BF)
    loads[3].wait()
    projected = mm(wqkv[...], normed, TN)
    q_t[...] = (projected[:channels] + col(8)).astype(BF)
    k_t[...] = projected[channels : 2 * channels].astype(BF)
    v_t[...] = (projected[2 * channels :] + col(9)).astype(BF)
    loads[4].wait()
    cot_t[...] = cot[...].T
    loads[5].wait()
    ga_t[...] = mm(wproj[...], cot_t[...]).astype(BF)
    prepare_heads(q_t, k_t, v_t, q_nt, k_nt, v_nt, head)

    forward = lambda bounded, h: head_forward(bounded, h, head, q_t, v_t, ga_t, k_nt, at_t)
    backward = lambda h, kept: head_backward(h, head, *kept, k_t, q_nt, v_nt, gq_t)

    def all_heads(bounded):
        def some_heads(t, _):
            for n in range(2):
                backward(2 * t + n, forward(bounded, 2 * t + n))
            return 0

        lax.fori_loop(0, HEADS // 2, some_heads, 0)

    small = largest_score(q_t, k_t, head) <= (60.0 / head ** (-0.5)) ** 2
    pl.when(small)(lambda: all_heads(True))
    pl.when(jnp.logical_not(small))(lambda: all_heads(False))
    out[...] = (hidden + mm(wproj[...], at_t[...], TN) + col(10)).T.astype(BF)
    rows = lambda c: pl.ds(pl.multiple_of(c * (pix // 2), pix // 2), pix // 2)
    stores = copies(
        [(out.at[rows(core)], out_ref.at[core]), (out.at[rows(1 - core)], outs_ref)], sems.at[7:9]
    )
    perm = row_matrix(channels, bits)
    got = mm(gq_t[...], normed, NT)
    tiles = channels // 128
    for t in range(tiles):
        wide[t] = got[:, t * 128 : (t + 1) * 128]
    quarter = channels // 4
    pieces = (gown_ref, gsame_ref, gcore_ref, gcross_ref)

    def spread(base, rows):
        for n, ref in enumerate(pieces):
            ref[:, base : base + rows.shape[1]] = rows[n * quarter : (n + 1) * quarter].astype(BF)

    for n in range(3):
        part = jnp.concatenate(
            [wide[t, pl.ds(n, channels, stride=3), :] for t in range(tiles)], axis=1
        )
        spread(pix + n * channels, mm(perm, part.astype(BF)))
    gproj_ref[...] = mm(perm, mm(cot_t[...], at_t[...], NT).astype(BF)).astype(BF)
    gn = mm(wqkv[...], gq_t[...])
    s3 = rowsum(gn)
    su3 = rowsum(gn * u3)
    cot_f = cot_t[...].astype(F32)
    hg = (cot_f + group_back(gn, u3, inv3, col(6), s3, su3)).astype(BF)
    hg_ref[...] = hg
    spread(0, mm(perm, hg))
    gq = gq_t[...].astype(F32)
    tall[:channels] = jnp.broadcast_to(rowsum(gq[:channels]), (channels, 128))
    tall[channels:] = jnp.broadcast_to(rowsum(gq[2 * channels :]), (channels, 128))
    side = with_columns(
        jnp.zeros((channels, 128), F32), 0,
        [su3, s3, tall[pl.ds(0, channels, stride=2), :], tall[pl.ds(1, channels, stride=2), :],
         rowsum(cot_f), rowsum(hg.astype(F32))],
    )
    spread(pix + 3 * channels, exact_left(perm, side))
    for one in stores:
        one.wait()


def kernel_second(
    bits, hg, stat_in, gproj, w2_ref, u2_ref,
    stat_ref, dc_ref, gown_ref, gsame_ref, gcore_ref, gcross_ref,
    wb, u2v, cat, slope, tall, sems,
):
    channels = hg.shape[0]
    loads = copies(tap_pairs(w2_ref, wb, channels) + [(u2_ref, u2v)], sems)
    stat = stat_in[...]
    col = lambda n: stat[:, n : n + 1]
    g2, b2, scale, shift, inv2 = col(3), col(4), col(11), col(12), col(33)
    gm = g2 * (1.0 + scale)
    fill_cols(cat, hg[...].astype(F32), -1)
    for one in loads:
        one.wait()
    slope[...] = silu_slope(u2v[...] * gm + (b2 * (1.0 + scale) + shift))
    u2 = u2v[...]
    dm = conv_apply(wb, cat, -1, channels) * slope[...]
    s = rowsum(dm)
    su = rowsum(dm * u2)
    dc = group_back(dm, u2, inv2, gm, s, su).astype(BF)
    dc_ref[...] = dc
    parts = mm(row_matrix(channels, bits), dc).astype(BF)
    quarter = channels // 4
    for n, ref in enumerate((gown_ref, gsame_ref, gcore_ref, gcross_ref)):
        at = slice(n * quarter, (n + 1) * quarter)
        ref[:, : hg.shape[1]] = parts[at]
        ref[:, hg.shape[1] :] = gproj[at, :]
    stat_ref[...] = with_columns(
        stat, 40,
        [(1.0 + scale) * su, (1.0 + scale) * s, rowsum(dc.astype(F32)), g2 * su + b2 * s, s],
    )


def kernel_first(
    bits, dc, stat_in, w1_ref, u1_ref, wemb_ref,
    dp_ref, stat_ref, own_ref, same_ref, core_ref, cross_ref,
    wb, u1v, cat, slope, wemb, tall, sems,
):
    channels = dc.shape[0]
    quarter = channels // 4
    loads = copies(
        tap_pairs(w1_ref, wb, channels) + [(u1_ref, u1v), (wemb_ref, wemb)], sems
    )
    stat = stat_in[...]
    col = lambda n: stat[:, n : n + 1]
    fill_cols(cat, dc[...].astype(F32), -1)
    for one in loads:
        one.wait()
    slope[...] = silu_slope(u1v[...] * col(0) + col(1))

    def even_odd(top, low):
        tall[:channels] = jnp.broadcast_to(top, (channels, 128))
        tall[channels:] = jnp.broadcast_to(low, (channels, 128))
        return [tall[pl.ds(n, channels, stride=2), :][:, :1] for n in range(2)]

    ga = even_odd(col(43), col(44))
    (ge,) = exact_columns(wemb[...], [tall[...][:, :1]])
    ge = even_odd(ge[:channels] * silu_slope(col(13)), ge[channels:] * silu_slope(col(14)))
    u1 = u1v[...]
    dp = conv_apply(wb, cat, -1, channels) * slope[...]
    s = rowsum(dp)
    su = rowsum(dp * u1)
    dp_ref[...] = dp
    stat_ref[...] = with_columns(stat, 43, [su, s])
    width = own_ref.shape[1]
    total = (width - 128) // 4
    side = with_columns(
        jnp.zeros((channels, width), F32), 0, [col(40), col(41), col(42), su, s]
    )
    lane = lanes((channels, width))
    for n, one in enumerate(ga + ge):
        side = jnp.where(lane == 128 + n * total + own_image(), one, side)
    side = exact_left(row_matrix(channels, bits), side)
    for n, ref in enumerate((own_ref, same_ref, core_ref, cross_ref)):
        ref[...] = side[n * quarter : (n + 1) * quarter].astype(ref.dtype)


def kernel_input(dp, u1_ref, hg, stat, ig_ref, igs_ref, ig, u1, sems):
    (load,) = copies([(u1_ref, u1)], sems.at[2:3])
    core = lax.axis_index("pipe")
    pix = hg.shape[1]
    col = lambda n: stat[:, n : n + 1]
    first, second = group_means([col(0) * col(44), col(0) * col(43)], pix)
    back = (col(32) * col(0)) * dp[...] - col(32) * first
    load.wait()
    back -= u1[...] * (col(32) * second)
    ig[...] = (hg[...].astype(F32) + back).T.astype(BF)
    rows = lambda c: pl.ds(pl.multiple_of(c * (pix // 2), pix // 2), pix // 2)
    stores = copies(
        [(ig.at[rows(core)], ig_ref.at[core]), (ig.at[rows(1 - core)], igs_ref)], sems.at[0:2]
    )
    for one in stores:
        one.wait()


def kernel_weight(which, total_images, sides, *refs):
    acts, pieces, side = refs[:4], refs[4:8], refs[8 : 8 + sides]
    keep_ref, send_ref, act, piece, told, stack, total, sems = refs[8 + sides :]
    rows, channels, pix = piece.shape[1], act.shape[1], act.shape[2]
    half = rows // 2
    at = slice(which * channels, (which + 1) * channels)
    pairs = [(ref, piece.at[n]) for n, ref in enumerate(pieces)]
    pairs += [(ref.at[at], act.at[n]) for n, ref in enumerate(acts)]
    if total_images:
        pairs += [(ref.at[2 * channels :], told.at[n]) for n, ref in enumerate(acts)]
    loads = copies(pairs, sems)

    def build(n):
        g = piece[n, :, :pix].astype(F32)
        for j in range(3):
            moved = shift_cols(g, 1 - j)
            for i in range(3):
                base = (3 * i + j) * rows
                stack[n, base : base + rows, :] = shift_rows(moved, 1 - i).astype(BF)

    loads[0].wait()
    build(0)
    for one in loads[1:8]:
        one.wait()
    for n in range(4):
        if n < 3:
            build(n + 1)
        got = mm(stack[n], act[n], NT)
        total[...] = got if n == 0 else total[...] + got
    for tap in range(9):
        at = slice(tap * channels, (tap + 1) * channels)
        keep_ref[:, at] = total[tap * rows : tap * rows + half, :]
        send_ref[:, at] = total[tap * rows + half : (tap + 1) * rows, :].astype(BF)
    at = slice(9 * channels, 9 * channels + piece.shape[2] - pix)
    more = sum(piece[n, :, pix:].astype(F32) for n in range(4))
    keep_ref[:, at] = more[:half]
    send_ref[:, at] = more[half:].astype(BF)
    if sides:
        more = sum(ref[...].astype(F32) for ref in side)
        keep_ref[:, at.stop :] = more[:half]
        send_ref[:, at.stop :] = more[half:].astype(BF)
    if total_images:
        for one in loads[8:]:
            one.wait()
        line = sum(told[n].astype(F32) for n in range(4))[:1, : 4 * total_images]
        line = jnp.broadcast_to(line, (half, 4 * total_images))
        keep_ref[:, at.stop :] = line
        send_ref[:, at.stop :] = line.astype(BF)


def interleave(ref, parts):
    size = parts[0].shape[0]
    for r in range(size):
        for n, part in enumerate(parts):
            at = len(parts) * r + n
            ref[at : at + 1, : part.shape[1]] = part[r : r + 1]


def summed(parts, size):
    return sum(part[:size].astype(F32) for part in parts)


def kernel_last_two(
    channels, size, parts, sig_ref, cls_ref, conv_ref, qkv_ref, bconv_ref, gain_ref, bias_ref, bqv_ref, bproj_ref, emb_ref, told_ref, rows,
    sig_table, cls_table, sems,
):
    loads = copies([(sig_ref, sig_table), (cls_ref, cls_table)], sems)
    total = summed(parts, size)
    for i in range(3):
        for j in range(3):
            at = (3 * i + j) * channels
            conv_ref[i, j] = total[:, at : at + channels]
    rest = total[:, 9 * channels :]
    interleave(qkv_ref, [rest[:, n * channels : (n + 1) * channels] for n in range(3)])
    side = rest[:, 3 * channels : 3 * channels + 128]
    lines = side.T
    for n, ref in ((0, gain_ref), (1, bias_ref), (4, bproj_ref), (5, bconv_ref)):
        ref[...] = lines[n]
    interleave(rows, [jnp.broadcast_to(side[:, n : n + 1], (size, 128)) for n in (2, 3)])
    bqv_ref[...] = rows[...].T[0]
    told = rest[0:1, 3 * channels + 128 :]
    told_ref[...] = told
    images = told.shape[1] // 4
    hot_sig, hot_cls = hot_rows(told, images, sig_table.shape[0], cls_table.shape[0])
    for one in loads:
        one.wait()
    emb = mm(hot_sig, sig_table[...], TN) + mm(hot_cls, cls_table[...], TN)
    emb_ref[...] = silu(emb).astype(BF)


def hot_rows(told, images, sig_count, cls_count):
    digit = lambda n: told[:, n * images : (n + 1) * images].astype(jnp.int32)
    sig = 32 * digit(0) + digit(1)
    cls = 32 * digit(2) + digit(3)

    def hot(index, count):
        line = lax.broadcasted_iota(jnp.int32, (count, images), 0)
        return jnp.where(line == index, 1.0, 0.0).astype(BF)

    return hot(sig, sig_count), hot(cls, cls_count)


def kernel_last_one(
    channels, size, parts, sides, both, told_ref, emb_ref, out_in, out_got, ig_in, ig_got, out_ref, ig_ref,
    conv_ref, proj_ref, gain2_ref, bias2_ref, bconv_ref, gain1_ref, bias1_ref, sig_ref, cls_ref,
    wemb_ref, bemb_ref, rows, sems,
):
    other = 1 - lax.axis_index("pipe")
    placed = copies([(out_got, out_ref.at[other]), (ig_got, ig_ref.at[other])], sems)
    joined = summed(both, size)
    total = summed(parts, size) + joined[:, : 10 * channels]
    for i in range(3):
        for j in range(3):
            at = (3 * i + j) * channels
            conv_ref[i, j] = total[:, at : at + channels]
    proj_ref[...] = total[:, 9 * channels : 10 * channels]
    rest = summed(sides, size) + joined[:, 10 * channels :]
    lines = rest[:, :128].T
    for n, ref in enumerate((gain2_ref, bias2_ref, bconv_ref, gain1_ref, bias1_ref)):
        ref[...] = lines[n]
    told = told_ref[...]
    images = told.shape[1] // 4
    part = lambda n: rest[:, 128 + n * images : 128 + (n + 1) * images]
    hot_sig, hot_cls = hot_rows(told, images, sig_ref.shape[1], cls_ref.shape[1])
    into = [part(2), part(3)]
    interleave(sig_ref, [exact_right(v, hot_sig, NT) for v in into])
    interleave(cls_ref, [exact_right(v, hot_cls, NT) for v in into])
    affine = [part(0), part(1)]
    interleave(wemb_ref, [exact_right(v, emb_ref[...]) for v in affine])
    interleave(rows, [jnp.broadcast_to(rowsum(v), (v.shape[0], 128)) for v in affine])
    bemb_ref[...] = rows[...].T[0]
    for one in placed:
        one.wait()


VM = pl.BlockSpec(memory_space=pltpu.VMEM)
ANY = pl.BlockSpec(memory_space=pl.ANY)
HBM = pl.BlockSpec(memory_space=pltpu.HBM)
SM = pl.BlockSpec(memory_space=pltpu.SMEM)


def vmem(shape, dtype=BF):
    return pltpu.VMEM(shape, dtype)


def call(kernel, operands, outs, scratch, after=(), alias=(), limit=20, flops=0, name=None):
    count = len(operands)
    operands = [
        (pltpu.with_memory_space_constraint(v, pltpu.HBM) if spec is HBM else v, spec)
        for v, spec in operands
    ]
    operands += [(v, ANY) for v in after]

    def ordered(*refs):
        kernel(*refs[:count], *refs[len(operands) :])

    return pl.pallas_call(
        ordered,
        out_shape=[jax.ShapeDtypeStruct(shape, dtype) for shape, dtype, _ in outs],
        in_specs=[spec for _, spec in operands],
        out_specs=[spec for _, _, spec in outs],
        scratch_shapes=scratch,
        input_output_aliases=dict(alias),
        compiler_params=pltpu.CompilerParams(vmem_limit_bytes=limit * 2**20),
        cost_estimate=pl.CostEstimate(flops=flops, bytes_accessed=10**6, transcendentals=0),
        name=name,
    )(*[operand for operand, _ in operands])


def swap_core(v):
    return lax.ppermute(v, "pipe", [(0, 1), (1, 0)])


def joint(v, target):
    pairs = []
    for dp in range(lax.axis_size("dp")):
        for core in range(2):
            to_dp, to_core = target(dp, core)
            pairs.append((2 * dp + core, 2 * to_dp + to_core))
    return lax.ppermute(v, ("dp", "pipe"), pairs)


def exchange(v, step, bits):
    return joint(v, lambda dp, core: (dp ^ (1 << stream_order(core, bits)[step]), core))


def cross(v, bits):
    return joint(v, lambda dp, core: (dp ^ (1 << stream_order(1 - core, bits)[0]), 1 - core))


def leaving(parts, rows):
    return sum(part[rows // 2 : rows].astype(F32) for part in parts).astype(BF)


def gathered(own, to_core, to_same, to_cross, bits):
    return [own, swap_core(to_core), exchange(to_same, 0, bits), cross(to_cross, bits)]


def body(
    block_input, cotangent, sigma_index, class_label, sigma_table, class_table, w_emb, b_emb,
    norm1_gain, norm1_bias, w_conv1, b_conv1, norm2_gain, norm2_bias, w_conv2, b_conv2,
    norm3_gain, norm3_bias, w_qkv, b_qv, w_proj, b_proj,
):
    data = lax.axis_size("dp")
    bits = data.bit_length() - 1
    images, pix, c = block_input.shape
    total = 2 * data
    width = sigma_table.shape[1]
    head, half, quarter, size = c // HEADS, c // 2, c // 4, c // (2 * data)
    dma = lambda count: pltpu.SemaphoreType.DMA((count,))
    field = ((c, pix), BF)
    vectors = [b_emb, norm1_gain, norm1_bias, b_conv1, norm2_gain, norm2_bias, b_conv2, norm3_gain,
               norm3_bias, b_qv, b_proj]
    told = 4 * total
    places = vectors + [w_emb, sigma_table, class_table]
    stat, acts, u1, u2 = call(
        lambda *refs: kernel_start(total, *refs),
        [(sigma_index, SM), (class_label, SM), (block_input, HBM), (w_conv1, HBM)]
        + [(v, HBM) for v in places],
        [((c, 128), F32, VM), ((2 * c + 16, pix), BF, ANY), ((c, pix), F32, ANY),
         ((c, pix), F32, ANY)],
        [vmem((pix, c)), vmem(w_conv1.shape), vmem((c, pix)), vmem((c, pix)), vmem((16, pix)),
         vmem((c, pix), F32), vmem((c, pix), F32), vmem((3 * c, 3 * c)), vmem((3 * c, pix)),
         dma(21)] + [vmem(v.shape) for v in places],
        limit=60, flops=10**11, name="start",
    )
    acts = gathered(acts, acts, acts, acts, bits)
    nat = vmem((HEADS, pix, head))
    piece = lambda more: [((quarter, pix + more), BF, VM)] * 4
    more2 = 3 * c + 128
    out, out_send, hg, gown, gsame, gcore, gcross, gproj = call(
        lambda *refs: kernel_attention(bits, *refs),
        [(stat, HBM), (acts[0], HBM), (block_input, HBM),
         (cotangent, HBM), (w_conv2, HBM), (w_qkv, HBM), (w_proj, HBM)],
        [((images, pix // 2, c), BF, ANY), ((pix // 2, c), BF, ANY),
         field + (VM,)] + piece(more2) + [((c, c), BF, VM)],
        [vmem((c, pix)), vmem((pix, c)), vmem((pix, c)), vmem(w_conv2.shape), vmem(w_qkv.shape),
         vmem(w_proj.shape), vmem((3 * c, 3 * c)), vmem((3 * c, pix)),
         vmem((c // 128, 3 * c, 128), F32), vmem((2 * c, 128), F32), nat, nat,
         vmem((HEADS, pix, 2 * head)), vmem((c, pix)), vmem((c, pix)), vmem((c, pix)),
         vmem((c, pix)), vmem((c, pix)), vmem((3 * c, pix)), vmem((c, pix)), vmem((pix, c)),
         vmem((c, 128), F32), dma(9)],
        limit=48, flops=400 * 10**9, name="attention",
    )
    grads2 = gathered(gown, gcore, gsame, gcross, bits)
    out_got = swap_core(out_send)
    stat, dc, gown, gsame, gcore, gcross = call(
        lambda *refs: kernel_second(bits, *refs),
        [(hg, VM), (stat, VM), (gproj, VM), (w_conv2, ANY), (u2, ANY)],
        [((c, 128), F32, VM), field + (VM,)] + piece(c),
        [vmem((3 * c, 3 * c)), vmem((c, pix), F32), vmem((3 * c, pix)), vmem((c, pix), F32),
         vmem((2 * c, 128), F32), dma(10)],
        after=acts[1:], flops=200 * 10**9, name="second",
    )
    grads1 = gathered(gown, gcore, gsame, gcross, bits)

    def weight(which, grads, count, side, after, name):
        more = grads[0].shape[1] - pix
        columns = 9 * c + more + 4 * count + (side[0].shape[1] if side else 0)
        return call(
            lambda *refs: kernel_weight(which, count, len(side), *refs),
            [(v, ANY) for v in acts + grads] + [(v, VM) for v in side],
            [((quarter // 2, columns), F32, VM), ((quarter // 2, columns), BF, VM)],
            [vmem((4, c, pix)), vmem((4, quarter, pix + more)), vmem((4, 16, pix)),
             vmem((4, 9 * quarter, pix)), vmem((9 * quarter, c), F32), dma(12)],
            after=after, limit=28, flops=200 * 10**9, name=name,
        )

    rows = [quarter >> step for step in range(bits)]
    keep2, send2 = weight(1, grads2, total, [], [dc, out_got], "weight_two")
    two = [keep2, exchange(send2, 1, bits)]
    keep1, send1 = weight(0, grads1, 0, [], [keep2], "weight_one")
    two[1], keep1, send1 = lax.optimization_barrier((two[1], keep1, send1))
    one = [keep1, exchange(send1, 1, bits)]
    send2 = leaving(two, rows[1])
    two.append(exchange(send2, 2, bits))
    dp, stat, own, same, to_core, to_cross = call(
        lambda *refs: kernel_first(bits, *refs),
        [(dc, VM), (stat, VM), (w_conv1, ANY), (u1, ANY), (w_emb, ANY)],
        [((c, pix), F32, VM), ((c, 128), F32, VM), ((quarter, 128 + told), F32, VM)]
        + [((quarter, 128 + told), BF, VM)] * 3,
        [vmem((3 * c, 3 * c)), vmem((c, pix), F32), vmem((3 * c, pix)), vmem((c, pix), F32),
         vmem(w_emb.shape), vmem((2 * c, 128), F32), dma(11)],
        after=[keep1, send2], flops=200 * 10**9, name="first",
    )
    side = gathered(own, to_core, same, to_cross, bits)
    ig, ig_send = call(
        kernel_input,
        [(dp, VM), (u1, HBM), (hg, VM), (stat, VM)],
        [((images, pix // 2, c), BF, ANY), ((pix // 2, c), BF, ANY)],
        [vmem((pix, c)), vmem((c, pix), F32), dma(3)],
        after=[own], flops=200 * 10**9, name="input",
    )
    one[1], two[2], *side, ig_send = lax.optimization_barrier((one[1], two[2], *side, ig_send))
    send1 = leaving(one, rows[1])
    one.append(exchange(send1, 2, bits))
    side[0], two[2], send1 = lax.optimization_barrier((side[0], two[2], send1))
    ig_got = swap_core(ig_send)
    for step in (1, 2):
        side.append(exchange(leaving(side, rows[step - 1]), step, bits))
    for step in range(3, bits):
        two.append(exchange(leaving(two, rows[step - 1]), step, bits))
    both = []
    for step in range(3, bits):
        n = rows[step - 1]
        ends = [leaving(one + [v[:, : 10 * c] for v in both], n),
                leaving(side + [v[:, 10 * c :] for v in both], n)]
        both.append(exchange(jnp.concatenate(ends, axis=1), step, bits))
    line = lambda n: ((n,), F32, VM)
    conv = ((3, 3, size, c), F32, VM)
    count = len(two)
    g_conv2, g_qkv, g_bconv2, g_gain3, g_bias3, g_bqv, g_bproj, emb, index = call(
        lambda *refs: kernel_last_two(c, size, refs[:count], *refs[count:]),
        [(v, VM) for v in two] + [(sigma_table, HBM), (class_table, HBM)],
        [conv, ((3 * size, c), F32, VM), line(size), line(size), line(size),
         line(2 * size), line(size), ((total, width), BF, VM), ((1, told), F32, VM)],
        [vmem((2 * size, 128), F32), vmem(sigma_table.shape), vmem(class_table.shape), dma(2)],
        name="last_two",
    )
    both[-1], emb = lax.optimization_barrier((both[-1], emb))
    tables = lambda count: ((2 * size, count), F32, VM)
    counts = (len(one), len(one) + len(side), len(one) + len(side) + len(both))
    image_half = (out.shape, BF, ANY)
    (output, input_grad, g_conv1, g_proj, g_gain2, g_bias2, g_bconv1, g_gain1, g_bias1, g_sigma, g_class, g_wemb,
     g_bemb) = call(
        lambda *refs: kernel_last_one(
            c, size, refs[: counts[0]], refs[counts[0] : counts[1]], refs[counts[1] : counts[2]],
            *refs[counts[2] :],
        ),
        [(v, VM) for v in one + side + both]
        + [(index, VM), (emb, VM), (out, ANY), (out_got, VM), (ig, ANY), (ig_got, VM)],
        [image_half, image_half, conv, ((size, c), F32, VM)] + [line(size)] * 5
        + [tables(sigma_table.shape[0]), tables(class_table.shape[0]), tables(width), line(2 * size)],
        [vmem((2 * size, 128), F32), dma(2)],
        alias=[(counts[2] + 2, 0), (counts[2] + 4, 1)], name="last_one",
    )
    place = lambda v: jnp.transpose(v, (0, 1, 3, 2))
    return (
        output, input_grad, g_sigma.T, g_class.T, g_wemb.T, g_bemb, g_gain1, g_bias1, place(g_conv1),
        g_bconv1, g_gain2, g_bias2, place(g_conv2), g_bconv2, g_gain3, g_bias3, g_qkv.T, g_bqv,
        g_proj.T, g_bproj,
    )


def solution(mesh):
    every = ("dp", "pipe")
    return jax.shard_map(
        body,
        mesh=mesh,
        in_specs=(P("dp", None, None), P("dp", None, None), P("dp"), P("dp")) + (P(),) * 18,
        out_specs=(
            P("dp", "pipe", None), P("dp", "pipe", None), P(None, every), P(None, every),
            P(None, every), P(every), P(every), P(every), P(None, None, None, every), P(every),
            P(every), P(every), P(None, None, None, every), P(every), P(every), P(every),
            P(None, every), P(every), P(None, every), P(every),
        ),
        check_vma=False,
    )
```

```python
import jax
import jax.numpy as jnp
from jax import lax
from jax.experimental import pallas as pl
from jax.experimental.pallas import tpu as pltpu
from jax.sharding import PartitionSpec as P

HEADS = 6
GROUPS = 32
SIDE = 32
EPS = 1e-05
LOG2E = 1.4426950408889634
BF = jnp.bfloat16
F32 = jnp.float32
NN = (((1,), (0,)), ((), ()))
NT = (((1,), (1,)), ((), ()))
TN = (((0,), (0,)), ((), ()))


def mm(a, b, dims=NN):
    return lax.dot_general(a, b, dims, preferred_element_type=F32)


def silu(v):
    return v * jax.nn.sigmoid(v)


def silu_slope(v):
    s = jax.nn.sigmoid(v)
    return s * (1.0 + v * (1.0 - s))


def lanes(shape):
    return lax.broadcasted_iota(jnp.int32, shape, 1)


def rowsum(v):
    return jnp.sum(v, axis=1, keepdims=True)


def shift_cols(a, d):
    if d == 0:
        return a
    n = a.shape[1]
    col = lanes(a.shape) & (SIDE - 1)
    ok = (col + d >= 0) & (col + d < SIDE)
    return jnp.where(ok, pltpu.roll(a, (-d) % n, 1), 0)


def shift_rows(a, d):
    if d == 0:
        return a
    n = a.shape[1]
    at = lanes(a.shape) + SIDE * d
    return jnp.where((at >= 0) & (at < n), pltpu.roll(a, (-SIDE * d) % n, 1), 0)


def split3(v):
    hi = v.astype(BF).astype(F32)
    mid = (v - hi).astype(BF).astype(F32)
    return hi, mid, v - hi - mid


def exact_left(matrix, v, dims=NN):
    return sum(mm(matrix, part.astype(BF), dims) for part in split3(v))


def exact_right(v, matrix, dims=NN):
    return sum(mm(part.astype(BF), matrix, dims) for part in split3(v))


def with_columns(block, start, extra):
    lane = lanes(block.shape)
    for n, c in enumerate(extra):
        block = jnp.where(lane == start + n, c, block)
    return block


def exact_columns(matrix, cols):
    parts = [part for col in cols for part in split3(col)]
    block = with_columns(jnp.zeros((cols[0].shape[0], 128), F32), 0, parts)
    got = mm(matrix, block.astype(BF))
    return [rowsum(got[:, 3 * at : 3 * at + 3]) for at in range(len(cols))]


def divide(v, size, top):
    scale = -(-(1 << 19) // size)
    assert all((n * scale) >> 19 == n // size for n in range(top))
    return (v * scale) >> 19


def group_matrix(channels):
    size = channels // GROUPS
    shape = (channels, channels)
    row = divide(lax.broadcasted_iota(jnp.int32, (channels, 1), 0), size, channels)
    col = divide(lax.broadcasted_iota(jnp.int32, (1, channels), 1), size, channels)
    return jnp.where(row == col, 1.0, jnp.zeros(shape, F32)).astype(BF)


def group_means(cols, pixels):
    channels = cols[0].shape[0]
    count = channels // GROUPS * pixels
    return [got * (1.0 / count) for got in exact_columns(group_matrix(channels), cols)]


def group_stats(v):
    pixels = v.shape[1]
    (mean,) = group_means([rowsum(v)], pixels)
    centred = v - mean
    (var,) = group_means([rowsum(centred * centred)], pixels)
    inverse = lax.rsqrt(var + EPS)
    return centred * inverse, inverse


def group_back(t, u, inverse, gain, sum_t, sum_tu):
    first, second = group_means([gain * sum_t, gain * sum_tu], t.shape[1])
    return (inverse * gain) * t - inverse * first - u * (inverse * second)


def fill_cols(ref, a, sign):
    c = a.shape[0]
    for j in range(3):
        ref[j * c : (j + 1) * c, :] = shift_cols(a, sign * (j - 1)).astype(BF)


def conv_apply(w_ref, cat_ref, sign, channels):
    total = None
    for i in range(3):
        y = mm(w_ref[i * channels : (i + 1) * channels, :], cat_ref[...])
        y = shift_rows(y, sign * (i - 1))
        total = y if total is None else total + y
    return total


def fill_forward(wf, w_ref, channels):
    for i in range(3):
        for j in range(3):
            at = (slice(i * channels, (i + 1) * channels), slice(j * channels, (j + 1) * channels))
            wf[at] = w_ref[i, j].T


def copies(pairs, sems):
    made = [pltpu.make_async_copy(src, dst, sems.at[n]) for n, (src, dst) in enumerate(pairs)]
    for one in made:
        one.start()
    return made


def tap_pairs(w_ref, wb, channels):
    return [
        (
            w_ref.at[i, j],
            wb.at[
                i * channels : (i + 1) * channels, j * channels : (j + 1) * channels
            ],
        )
        for i in range(3)
        for j in range(3)
    ]


def stream_order(core, bits):
    order = list(range(bits))
    if core:
        for at in range(0, bits - 1, 2):
            order[at], order[at + 1] = order[at + 1], order[at]
    return order


def row_matrix(channels, bits):
    dp, core = lax.axis_index("dp"), lax.axis_index("pipe")
    size = channels // (2 << bits)
    quarter = channels // 4
    row = lax.broadcasted_iota(jnp.int32, (channels, 1), 0)
    part_of = sum(jnp.where(row >= quarter * n, 1, 0) for n in (1, 2, 3))
    rest = row - part_of * quarter
    at = divide(rest, size, quarter)
    within = rest - at * size
    part = jnp.where(part_of < 2, core, 1 - core)
    flips = []
    for p in (0, 1):
        order = stream_order(p, bits)
        flip = (part_of & 1) << order[0]
        for t in range(bits - 1):
            flip = flip | (((at >> (bits - 2 - t)) & 1) << order[t + 1])
        flips.append(flip)
    peer = dp ^ jnp.where(part == 0, flips[0], flips[1])
    wanted = (2 * peer + part) * size + within
    shape = (channels, channels)
    return jnp.where(wanted == lanes((1, channels)), 1.0, jnp.zeros(shape, F32)).astype(BF)


def own_image():
    return 2 * lax.axis_index("dp") + lax.axis_index("pipe")


def kernel_start(
    total, sig_at, cls_at, x_ref, w1_ref, *refs
):
    count = 14
    places, rest = refs[:count], refs[count:]
    stat_ref, acts_ref, u1_ref, u2_ref = rest[:4]
    x, w1, act1, act2, told, u1, u2, wf, cat, sems = rest[4:14]
    held = rest[14:]
    bemb, g1, b1, bc1, g2, b2, bc2, g3, b3, bqv, bp, wemb, sig_table, cls_table = held
    core = lax.axis_index("pipe")
    channels = x.shape[1]
    loads = copies(
        [(x_ref.at[core], x), (w1_ref, w1)] + list(zip(places, held)), sems.at[: 2 + count]
    )
    sig = jnp.where(core == 0, sig_at[0], sig_at[1])
    cls = jnp.where(core == 0, cls_at[0], cls_at[1])
    lane = lanes(told.shape)
    line = jnp.zeros(told.shape, F32)
    for n, digit in enumerate((sig // 32, sig % 32, cls // 32, cls % 32)):
        line = jnp.where(lane == n * total + own_image(), digit.astype(F32), line)
    told[...] = line.astype(BF)
    loads[0].wait()
    v1, inv1 = group_stats(x[...].astype(F32).T)
    u1[...] = v1
    loads[1].wait()
    fill_forward(wf, w1, channels)
    for one in loads[2:]:
        one.wait()

    def table_row(table, found):
        hot = jnp.where(lanes((16, table.shape[0])) == found, 1.0, 0.0).astype(BF)
        return mm(hot, table[...])[0:1]

    emb = table_row(sig_table, sig) + table_row(cls_table, cls)
    flat = lambda ref: ref[...].astype(F32).reshape(1, ref.shape[0])
    bqv_row = flat(bqv)
    rows = [flat(ref) for ref in (g1, b1, bc1, g2, b2, bc2, g3, b3)]
    rows += [bqv_row[:, :channels], bqv_row[:, channels:], flat(bp)]
    low = jnp.broadcast_to(silu(emb), (16, emb.shape[1])).astype(BF)
    affine = mm(low, wemb[...])[0:1] + flat(bemb)
    rows += [affine[:, :channels], affine[:, channels:], emb[:, :channels], emb[:, channels:]]
    prm = jnp.zeros((128, channels), F32)
    at = lax.broadcasted_iota(jnp.int32, prm.shape, 0)
    for n, line in enumerate(rows):
        prm = jnp.where(at == n, line, prm)
    stat = prm.T
    col = lambda n: stat[:, n : n + 1]
    a1 = silu(v1 * col(0) + col(1))
    act1[...] = a1.astype(BF)
    stores = copies(
        [(u1, u1_ref), (act1, acts_ref.at[:channels]), (told, acts_ref.at[2 * channels :])],
        sems.at[16:19],
    )
    fill_cols(cat, a1, 1)
    v2, inv2 = group_stats(conv_apply(wf, cat, 1, channels) + col(2))
    u2[...] = v2
    scale, shift = col(11), col(12)
    a2 = silu(v2 * (col(3) * (1.0 + scale)) + (col(4) * (1.0 + scale) + shift))
    act2[...] = a2.astype(BF)
    stores += copies([(u2, u2_ref), (act2, acts_ref.at[channels : 2 * channels])], sems.at[19:21])
    stat_ref[...] = with_columns(stat, 32, [inv1, inv2])
    for one in stores:
        one.wait()


def prepare_heads(q_t, k_t, v_t, q_nt, k_nt, v_nt, head):
    pix = q_t.shape[1]
    ones = jnp.where(lanes((pix, head)) < 2, 1.0, 0.0).astype(BF)
    for h in range(HEADS):
        at = slice(h * head, (h + 1) * head)
        q_nt[h] = q_t[at, :].T
        k_nt[h] = k_t[at, :].T
        v_nt[h, :, :head] = v_t[at, :].T
        v_nt[h, :, head:] = ones


def largest_score(q_t, k_t, head):
    worst = jnp.zeros((1, 1), F32)
    for h in range(HEADS):
        longest = []
        for ref in (q_t, k_t):
            v = ref[h * head : (h + 1) * head, :].astype(F32)
            longest.append(
                jnp.max(jnp.sum(v * v, axis=0, keepdims=True), axis=1, keepdims=True)
            )
        worst = jnp.maximum(worst, longest[0] * longest[1])
    return worst[0, 0]


def head_forward(bounded, h, head, q_t, v_t, ga_t, k_nt, at_t):
    pix = q_t.shape[1]
    at = pl.ds(pl.multiple_of(h * head, head), head)
    s = mm(k_nt[h], q_t[at, :])
    if not bounded:
        s = s - jnp.max(s, axis=0, keepdims=True)
    exact = jnp.exp2(s * (head ** (-0.5) * LOG2E))
    e = exact.astype(BF)
    o = mm(jnp.concatenate([v_t[at, :], jnp.ones((16, pix), BF)], axis=0), e)
    inv = 1.0 / o[head : head + 1]
    o = o[:head] * inv
    at_t[at, :] = o.astype(BF)
    g = ga_t[at, :].astype(F32)
    centre = -jnp.sum(g * o, axis=0, keepdims=True)
    g = (g * inv).astype(BF)
    hi = centre.astype(BF).astype(F32)
    line = lax.broadcasted_iota(jnp.int32, (head, pix), 0)
    tail = jnp.where(line == 0, hi, jnp.where(line == 1, centre - hi, 0.0)).astype(BF)
    return exact, e, inv, g, jnp.concatenate([ga_t[at, :], tail], axis=0)


def head_backward(h, head, exact, e, inv, g, upstream, k_t, q_nt, v_nt, gq_t):
    channels = k_t.shape[0]
    factor = head ** (-0.5)
    rows = lambda base: pl.ds(pl.multiple_of(base + h * head, head), head)
    ds = (exact * (mm(v_nt[h], upstream) * inv)).astype(BF)
    gq_t[rows(2 * channels), :] = mm(e, g.T).T.astype(BF)
    gq_t[rows(0), :] = (mm(k_t[rows(0), :], ds) * factor).astype(BF)
    gq_t[rows(channels), :] = (mm(ds, q_nt[h]) * factor).T.astype(BF)


def kernel_attention(
    bits, stat_ref, acts_ref, x_ref, cot_ref, w2_ref, wqkv_ref, wproj_ref,
    out_ref, outs_ref, hg_ref, gown_ref, gsame_ref, gcore_ref, gcross_ref, gproj_ref,
    act2, x, cot, w2, wqkv, wproj, wf, cat, wide, tall, q_nt, k_nt, v_nt, q_t, k_t, v_t, ga_t, at_t,
    gq_t, cot_t, out, stat, sems,
):
    core = lax.axis_index("pipe")
    channels, pix = act2.shape
    head = channels // HEADS
    half = channels // 2
    loads = copies(
        [(acts_ref.at[channels : 2 * channels], act2), (w2_ref, w2), (x_ref.at[core], x), (wqkv_ref, wqkv),
         (cot_ref.at[core], cot), (wproj_ref, wproj), (stat_ref, stat)],
        sems,
    )
    col = lambda n: stat[:, n : n + 1]
    loads[0].wait()
    fill_cols(cat, act2[...].astype(F32), 1)
    loads[1].wait()
    fill_forward(wf, w2, channels)
    loads[6].wait()
    conv = conv_apply(wf, cat, 1, channels) + col(5)
    loads[2].wait()
    hidden = (x[...].astype(F32).T + conv).astype(BF).astype(F32)
    u3, inv3 = group_stats(hidden)
    normed = (u3 * col(6) + col(7)).astype(BF)
    loads[3].wait()
    projected = mm(wqkv[...], normed, TN)
    q_t[...] = (projected[:channels] + col(8)).astype(BF)
    k_t[...] = projected[channels : 2 * channels].astype(BF)
    v_t[...] = (projected[2 * channels :] + col(9)).astype(BF)
    loads[4].wait()
    cot_t[...] = cot[...].T
    loads[5].wait()
    ga_t[...] = mm(wproj[...], cot_t[...]).astype(BF)
    prepare_heads(q_t, k_t, v_t, q_nt, k_nt, v_nt, head)

    forward = lambda bounded, h: head_forward(bounded, h, head, q_t, v_t, ga_t, k_nt, at_t)
    backward = lambda h, kept: head_backward(h, head, *kept, k_t, q_nt, v_nt, gq_t)

    def all_heads(bounded):
        def some_heads(t, _):
            for n in range(2):
                backward(2 * t + n, forward(bounded, 2 * t + n))
            return 0

        lax.fori_loop(0, HEADS // 2, some_heads, 0)

    small = largest_score(q_t, k_t, head) <= (60.0 / head ** (-0.5)) ** 2
    pl.when(small)(lambda: all_heads(True))
    pl.when(jnp.logical_not(small))(lambda: all_heads(False))
    out[...] = (hidden + mm(wproj[...], at_t[...], TN) + col(10)).T.astype(BF)
    rows = lambda c: pl.ds(pl.multiple_of(c * (pix // 2), pix // 2), pix // 2)
    stores = copies(
        [(out.at[rows(core)], out_ref.at[core]), (out.at[rows(1 - core)], outs_ref)], sems.at[7:9]
    )
    perm = row_matrix(channels, bits)
    got = mm(gq_t[...], normed, NT)
    tiles = channels // 128
    for t in range(tiles):
        wide[t, : 3 * channels] = got[:, t * 128 : (t + 1) * 128]
    quarter = channels // 4
    pieces = (gown_ref, gsame_ref, gcore_ref, gcross_ref)

    def spread(base, rows):
        for n, ref in enumerate(pieces):
            ref[:, base : base + rows.shape[1]] = rows[n * quarter : (n + 1) * quarter].astype(BF)

    for n in range(3):
        part = jnp.concatenate(
            [wide[t, pl.ds(n, channels, stride=3), :] for t in range(tiles)], axis=1
        )
        spread(pix + n * channels, mm(perm, part.astype(BF)))
    gproj_ref[...] = mm(perm, mm(cot_t[...], at_t[...], NT).astype(BF)).astype(BF)
    gn = mm(wqkv[...], gq_t[...])
    s3 = rowsum(gn)
    su3 = rowsum(gn * u3)
    cot_f = cot_t[...].astype(F32)
    hg = (cot_f + group_back(gn, u3, inv3, col(6), s3, su3)).astype(BF)
    hg_ref[...] = hg
    spread(0, mm(perm, hg))
    gq = gq_t[...].astype(F32)
    tall[:channels] = jnp.broadcast_to(rowsum(gq[:channels]), (channels, 128))
    tall[channels : 2 * channels] = jnp.broadcast_to(
        rowsum(gq[2 * channels :]), (channels, 128)
    )
    side = with_columns(
        jnp.zeros((channels, 128), F32), 0,
        [su3, s3, tall[pl.ds(0, channels, stride=2), :], tall[pl.ds(1, channels, stride=2), :],
         rowsum(cot_f), rowsum(hg.astype(F32))],
    )
    spread(pix + 3 * channels, exact_left(perm, side))
    for one in stores:
        one.wait()


def kernel_second(
    bits, hg, stat_in, gproj, w2_ref, u2_ref,
    stat_ref, dc_ref, gown_ref, gsame_ref, gcore_ref, gcross_ref,
    wb, u2v, cat, slope, tall, sems,
):
    channels = hg.shape[0]
    loads = copies(tap_pairs(w2_ref, wb, channels) + [(u2_ref, u2v)], sems)
    stat = stat_in[...]
    col = lambda n: stat[:, n : n + 1]
    g2, b2, scale, shift, inv2 = col(3), col(4), col(11), col(12), col(33)
    gm = g2 * (1.0 + scale)
    fill_cols(cat, hg[...].astype(F32), -1)
    for one in loads:
        one.wait()
    slope[...] = silu_slope(u2v[...] * gm + (b2 * (1.0 + scale) + shift))
    u2 = u2v[...]
    dm = conv_apply(wb, cat, -1, channels) * slope[...]
    s = rowsum(dm)
    su = rowsum(dm * u2)
    dc = group_back(dm, u2, inv2, gm, s, su).astype(BF)
    dc_ref[...] = dc
    parts = mm(row_matrix(channels, bits), dc).astype(BF)
    quarter = channels // 4
    for n, ref in enumerate((gown_ref, gsame_ref, gcore_ref, gcross_ref)):
        at = slice(n * quarter, (n + 1) * quarter)
        ref[:, : hg.shape[1]] = parts[at]
        ref[:, hg.shape[1] :] = gproj[at, :]
    stat_ref[...] = with_columns(
        stat, 40,
        [(1.0 + scale) * su, (1.0 + scale) * s, rowsum(dc.astype(F32)), g2 * su + b2 * s, s],
    )


def kernel_first(
    bits, dc, stat_in, w1_ref, u1_ref, wemb_ref,
    dp_ref, stat_ref, own_ref, same_ref, core_ref, cross_ref,
    wb, u1v, cat, slope, wemb, tall, sems,
):
    channels = dc.shape[0]
    quarter = channels // 4
    loads = copies(
        tap_pairs(w1_ref, wb, channels) + [(u1_ref, u1v), (wemb_ref, wemb)], sems
    )
    stat = stat_in[...]
    col = lambda n: stat[:, n : n + 1]
    fill_cols(cat, dc[...].astype(F32), -1)
    for one in loads:
        one.wait()
    slope[...] = silu_slope(u1v[...] * col(0) + col(1))

    def even_odd(top, low):
        tall[:channels] = jnp.broadcast_to(top, (channels, 128))
        tall[channels : 2 * channels] = jnp.broadcast_to(low, (channels, 128))
        return [tall[pl.ds(n, channels, stride=2), :][:, :1] for n in range(2)]

    ga = even_odd(col(43), col(44))
    (ge,) = exact_columns(wemb[...], [tall[: 2 * channels, :][:, :1]])
    ge = even_odd(ge[:channels] * silu_slope(col(13)), ge[channels:] * silu_slope(col(14)))
    u1 = u1v[...]
    dp = conv_apply(wb, cat, -1, channels) * slope[...]
    s = rowsum(dp)
    su = rowsum(dp * u1)
    dp_ref[...] = dp
    stat_ref[...] = with_columns(stat, 43, [su, s])
    width = own_ref.shape[1]
    total = (width - 128) // 4
    side = with_columns(
        jnp.zeros((channels, width), F32), 0, [col(40), col(41), col(42), su, s]
    )
    lane = lanes((channels, width))
    for n, one in enumerate(ga + ge):
        side = jnp.where(lane == 128 + n * total + own_image(), one, side)
    side = exact_left(row_matrix(channels, bits), side)
    for n, ref in enumerate((own_ref, same_ref, core_ref, cross_ref)):
        ref[...] = side[n * quarter : (n + 1) * quarter].astype(ref.dtype)


def kernel_input(dp, u1_ref, hg, stat, ig_ref, igs_ref, ig, u1, sems):
    (load,) = copies([(u1_ref, u1)], sems.at[2:3])
    core = lax.axis_index("pipe")
    pix = hg.shape[1]
    col = lambda n: stat[:, n : n + 1]
    first, second = group_means([col(0) * col(44), col(0) * col(43)], pix)
    back = (col(32) * col(0)) * dp[...] - col(32) * first
    load.wait()
    back -= u1[...] * (col(32) * second)
    ig[...] = (hg[...].astype(F32) + back).T.astype(BF)
    rows = lambda c: pl.ds(pl.multiple_of(c * (pix // 2), pix // 2), pix // 2)
    stores = copies(
        [(ig.at[rows(core)], ig_ref.at[core]), (ig.at[rows(1 - core)], igs_ref)], sems.at[0:2]
    )
    for one in stores:
        one.wait()


def kernel_weight(which, total_images, sides, *refs):
    acts, pieces, side = refs[:4], refs[4:8], refs[8 : 8 + sides]
    keep_ref, send_ref, act, piece, told, stack, total, sems = refs[8 + sides :]
    rows, channels, pix = piece.shape[1], act.shape[1], act.shape[2]
    half = rows // 2
    at = slice(which * channels, (which + 1) * channels)
    pairs = [(ref, piece.at[n]) for n, ref in enumerate(pieces)]
    pairs += [(ref.at[at], act.at[n]) for n, ref in enumerate(acts)]
    if total_images:
        pairs += [(ref.at[2 * channels :], told.at[n]) for n, ref in enumerate(acts)]
    loads = copies(pairs, sems)

    def build(n):
        g = piece[n, :, :pix].astype(F32)
        for j in range(3):
            moved = shift_cols(g, 1 - j)
            for i in range(3):
                base = (3 * i + j) * rows
                stack[n, base : base + rows, :] = shift_rows(moved, 1 - i).astype(BF)

    loads[0].wait()
    build(0)
    for one in loads[1:8]:
        one.wait()
    for n in range(4):
        if n < 3:
            build(n + 1)
        got = mm(stack[n], act[n], NT)
        total[...] = got if n == 0 else total[...] + got
    for tap in range(9):
        at = slice(tap * channels, (tap + 1) * channels)
        keep_ref[:, at] = total[tap * rows : tap * rows + half, :]
        send_ref[:, at] = total[tap * rows + half : (tap + 1) * rows, :].astype(BF)
    at = slice(9 * channels, 9 * channels + piece.shape[2] - pix)
    more = sum(piece[n, :, pix:].astype(F32) for n in range(4))
    keep_ref[:, at] = more[:half]
    send_ref[:, at] = more[half:].astype(BF)
    if sides:
        more = sum(ref[...].astype(F32) for ref in side)
        keep_ref[:, at.stop :] = more[:half]
        send_ref[:, at.stop :] = more[half:].astype(BF)
    if total_images:
        for one in loads[8:]:
            one.wait()
        line = sum(told[n].astype(F32) for n in range(4))[:1, : 4 * total_images]
        line = jnp.broadcast_to(line, (half, 4 * total_images))
        keep_ref[:, at.stop :] = line
        send_ref[:, at.stop :] = line.astype(BF)


def interleave(ref, parts):
    size = parts[0].shape[0]
    for r in range(size):
        for n, part in enumerate(parts):
            at = len(parts) * r + n
            ref[at : at + 1, : part.shape[1]] = part[r : r + 1]


def summed(parts, size):
    return sum(part[:size].astype(F32) for part in parts)


def kernel_last_two(
    channels, size, parts, sig_ref, cls_ref, conv_ref, qkv_ref, bconv_ref, gain_ref, bias_ref, bqv_ref, bproj_ref, emb_ref, told_ref, rows,
    sig_table, cls_table, sems,
):
    loads = copies([(sig_ref, sig_table), (cls_ref, cls_table)], sems)
    total = summed(parts, size)
    for i in range(3):
        for j in range(3):
            at = (3 * i + j) * channels
            conv_ref[i, j] = total[:, at : at + channels]
    rest = total[:, 9 * channels :]
    interleave(qkv_ref, [rest[:, n * channels : (n + 1) * channels] for n in range(3)])
    side = rest[:, 3 * channels : 3 * channels + 128]
    lines = side.T
    for n, ref in ((0, gain_ref), (1, bias_ref), (4, bproj_ref), (5, bconv_ref)):
        ref[...] = lines[n]
    interleave(rows, [jnp.broadcast_to(side[:, n : n + 1], (size, 128)) for n in (2, 3)])
    bqv_ref[...] = rows[...].T[0]
    told = rest[0:1, 3 * channels + 128 :]
    told_ref[...] = told
    images = told.shape[1] // 4
    hot_sig, hot_cls = hot_rows(told, images, sig_table.shape[0], cls_table.shape[0])
    for one in loads:
        one.wait()
    emb = mm(hot_sig, sig_table[...], TN) + mm(hot_cls, cls_table[...], TN)
    emb_ref[...] = silu(emb).astype(BF)


def hot_rows(told, images, sig_count, cls_count):
    digit = lambda n: told[:, n * images : (n + 1) * images].astype(jnp.int32)
    sig = 32 * digit(0) + digit(1)
    cls = 32 * digit(2) + digit(3)

    def hot(index, count):
        line = lax.broadcasted_iota(jnp.int32, (count, images), 0)
        return jnp.where(line == index, 1.0, 0.0).astype(BF)

    return hot(sig, sig_count), hot(cls, cls_count)


def kernel_last_one(
    channels, size, parts, sides, both, told_ref, emb_ref, out_in, out_got, ig_in, ig_got, out_ref, ig_ref,
    conv_ref, proj_ref, gain2_ref, bias2_ref, bconv_ref, gain1_ref, bias1_ref, sig_ref, cls_ref,
    wemb_ref, bemb_ref, rows, sems,
):
    other = 1 - lax.axis_index("pipe")
    placed = copies([(out_got, out_ref.at[other]), (ig_got, ig_ref.at[other])], sems)
    joined = summed(both, size)
    total = summed(parts, size) + joined[:, : 10 * channels]
    for i in range(3):
        for j in range(3):
            at = (3 * i + j) * channels
            conv_ref[i, j] = total[:, at : at + channels]
    proj_ref[...] = total[:, 9 * channels : 10 * channels]
    rest = summed(sides, size) + joined[:, 10 * channels :]
    lines = rest[:, :128].T
    for n, ref in enumerate((gain2_ref, bias2_ref, bconv_ref, gain1_ref, bias1_ref)):
        ref[...] = lines[n]
    told = told_ref[...]
    images = told.shape[1] // 4
    part = lambda n: rest[:, 128 + n * images : 128 + (n + 1) * images]
    hot_sig, hot_cls = hot_rows(told, images, sig_ref.shape[1], cls_ref.shape[1])
    into = [part(2), part(3)]
    interleave(sig_ref, [exact_right(v, hot_sig, NT) for v in into])
    interleave(cls_ref, [exact_right(v, hot_cls, NT) for v in into])
    affine = [part(0), part(1)]
    interleave(wemb_ref, [exact_right(v, emb_ref[...]) for v in affine])
    interleave(rows, [jnp.broadcast_to(rowsum(v), (v.shape[0], 128)) for v in affine])
    bemb_ref[...] = rows[...].T[0]
    for one in placed:
        one.wait()


VM = pl.BlockSpec(memory_space=pltpu.VMEM)
ANY = pl.BlockSpec(memory_space=pl.ANY)
HBM = pl.BlockSpec(memory_space=pltpu.HBM)
SM = pl.BlockSpec(memory_space=pltpu.SMEM)


def vmem(shape, dtype=BF):
    return pltpu.VMEM(shape, dtype)


def call(kernel, operands, outs, scratch, after=(), alias=(), limit=20, flops=0, name=None):
    count = len(operands)
    operands = [
        (pltpu.with_memory_space_constraint(v, pltpu.HBM) if spec is HBM else v, spec)
        for v, spec in operands
    ]
    operands += [(v, ANY) for v in after]

    def ordered(*refs):
        kernel(*refs[:count], *refs[len(operands) :])

    return pl.pallas_call(
        ordered,
        out_shape=[jax.ShapeDtypeStruct(shape, dtype) for shape, dtype, _ in outs],
        in_specs=[spec for _, spec in operands],
        out_specs=[spec for _, _, spec in outs],
        scratch_shapes=scratch,
        input_output_aliases=dict(alias),
        compiler_params=pltpu.CompilerParams(vmem_limit_bytes=limit * 2**20),
        cost_estimate=pl.CostEstimate(flops=flops, bytes_accessed=10**6, transcendentals=0),
        name=name,
    )(*[operand for operand, _ in operands])


def swap_core(v):
    return lax.ppermute(v, "pipe", [(0, 1), (1, 0)])


def joint(v, target):
    pairs = []
    for dp in range(lax.axis_size("dp")):
        for core in range(2):
            to_dp, to_core = target(dp, core)
            pairs.append((2 * dp + core, 2 * to_dp + to_core))
    return lax.ppermute(v, ("dp", "pipe"), pairs)


def exchange(v, step, bits):
    return joint(v, lambda dp, core: (dp ^ (1 << stream_order(core, bits)[step]), core))


def cross(v, bits):
    return joint(v, lambda dp, core: (dp ^ (1 << stream_order(1 - core, bits)[0]), 1 - core))


def leaving(parts, rows):
    return sum(part[rows // 2 : rows].astype(F32) for part in parts).astype(BF)


def gathered(own, to_core, to_same, to_cross, bits):
    return [own, swap_core(to_core), exchange(to_same, 0, bits), cross(to_cross, bits)]


def body(
    block_input, cotangent, sigma_index, class_label, sigma_table, class_table, w_emb, b_emb,
    norm1_gain, norm1_bias, w_conv1, b_conv1, norm2_gain, norm2_bias, w_conv2, b_conv2,
    norm3_gain, norm3_bias, w_qkv, b_qv, w_proj, b_proj,
):
    data = lax.axis_size("dp")
    bits = data.bit_length() - 1
    images, pix, c = block_input.shape
    total = 2 * data
    width = sigma_table.shape[1]
    head, half, quarter, size = c // HEADS, c // 2, c // 4, c // (2 * data)
    dma = lambda count: pltpu.SemaphoreType.DMA((count,))
    field = ((c, pix), BF)
    vectors = [b_emb, norm1_gain, norm1_bias, b_conv1, norm2_gain, norm2_bias, b_conv2, norm3_gain,
               norm3_bias, b_qv, b_proj]
    told = 4 * total
    places = vectors + [w_emb, sigma_table, class_table]
    stat, acts, u1, u2 = call(
        lambda *refs: kernel_start(total, *refs),
        [(sigma_index, SM), (class_label, SM), (block_input, HBM), (w_conv1, HBM)]
        + [(v, HBM) for v in places],
        [((c, 128), F32, VM), ((2 * c + 16, pix), BF, ANY), ((c, pix), F32, ANY),
         ((c, pix), F32, ANY)],
        [vmem((pix, c)), vmem(w_conv1.shape), vmem((c, pix)), vmem((c, pix)), vmem((16, pix)),
         vmem((c, pix), F32), vmem((c, pix), F32), vmem((3 * c, 3 * c)), vmem((3 * c, pix)),
         dma(21)] + [vmem(v.shape) for v in places],
        limit=60, flops=10**11, name="start",
    )
    acts = gathered(acts, acts, acts, acts, bits)
    nat = vmem((HEADS, pix, head))
    piece = lambda more: [((quarter, pix + more), BF, VM)] * 4
    more2 = 3 * c + 128
    out, out_send, hg, gown, gsame, gcore, gcross, gproj = call(
        lambda *refs: kernel_attention(bits, *refs),
        [(stat, HBM), (acts[0], HBM), (block_input, HBM),
         (cotangent, HBM), (w_conv2, HBM), (w_qkv, HBM), (w_proj, HBM)],
        [((images, pix // 2, c), BF, ANY), ((pix // 2, c), BF, ANY),
         field + (VM,)] + piece(more2) + [((c, c), BF, VM)],
        [vmem((c, pix)), vmem((pix, c)), vmem((pix, c)), vmem(w_conv2.shape), vmem(w_qkv.shape),
         vmem(w_proj.shape), vmem((3 * c, 3 * c)), vmem((3 * c, pix)),
         vmem((c // 128, 3 * c + 8, 128), F32), vmem((2 * c + 8, 128), F32), nat, nat,
         vmem((HEADS, pix, 2 * head)), vmem((c, pix)), vmem((c, pix)), vmem((c, pix)),
         vmem((c, pix)), vmem((c, pix)), vmem((3 * c, pix)), vmem((c, pix)), vmem((pix, c)),
         vmem((c, 128), F32), dma(9)],
        limit=48, flops=400 * 10**9, name="attention",
    )
    grads2 = gathered(gown, gcore, gsame, gcross, bits)
    out_got = swap_core(out_send)
    stat, dc, gown, gsame, gcore, gcross = call(
        lambda *refs: kernel_second(bits, *refs),
        [(hg, VM), (stat, VM), (gproj, VM), (w_conv2, ANY), (u2, ANY)],
        [((c, 128), F32, VM), field + (VM,)] + piece(c),
        [vmem((3 * c, 3 * c)), vmem((c, pix), F32), vmem((3 * c, pix)), vmem((c, pix), F32),
         vmem((2 * c, 128), F32), dma(10)],
        after=acts[1:], flops=200 * 10**9, name="second",
    )
    grads1 = gathered(gown, gcore, gsame, gcross, bits)

    def weight(which, grads, count, side, after, name):
        more = grads[0].shape[1] - pix
        columns = 9 * c + more + 4 * count + (side[0].shape[1] if side else 0)
        return call(
            lambda *refs: kernel_weight(which, count, len(side), *refs),
            [(v, ANY) for v in acts + grads] + [(v, VM) for v in side],
            [((quarter // 2, columns), F32, VM), ((quarter // 2, columns), BF, VM)],
            [vmem((4, c, pix)), vmem((4, quarter, pix + more)), vmem((4, 16, pix)),
             vmem((4, 9 * quarter, pix)), vmem((9 * quarter, c), F32), dma(12)],
            after=after, limit=28, flops=200 * 10**9, name=name,
        )

    rows = [quarter >> step for step in range(bits)]
    keep2, send2 = weight(1, grads2, total, [], [dc, out_got], "weight_two")
    two = [keep2, exchange(send2, 1, bits)]
    keep1, send1 = weight(0, grads1, 0, [], [keep2], "weight_one")
    two[1], keep1, send1 = lax.optimization_barrier((two[1], keep1, send1))
    one = [keep1, exchange(send1, 1, bits)]
    send2 = leaving(two, rows[1])
    two.append(exchange(send2, 2, bits))
    dp, stat, own, same, to_core, to_cross = call(
        lambda *refs: kernel_first(bits, *refs),
        [(dc, VM), (stat, VM), (w_conv1, ANY), (u1, ANY), (w_emb, ANY)],
        [((c, pix), F32, VM), ((c, 128), F32, VM), ((quarter, 128 + told), F32, VM)]
        + [((quarter, 128 + told), BF, VM)] * 3,
        [vmem((3 * c, 3 * c)), vmem((c, pix), F32), vmem((3 * c, pix)), vmem((c, pix), F32),
         vmem(w_emb.shape), vmem((2 * c + 8, 128), F32), dma(11)],
        after=[keep1, send2], flops=200 * 10**9, name="first",
    )
    side = gathered(own, to_core, same, to_cross, bits)
    ig, ig_send = call(
        kernel_input,
        [(dp, VM), (u1, HBM), (hg, VM), (stat, VM)],
        [((images, pix // 2, c), BF, ANY), ((pix // 2, c), BF, ANY)],
        [vmem((pix, c)), vmem((c, pix), F32), dma(3)],
        after=[own], flops=200 * 10**9, name="input",
    )
    one[1], two[2], *side, ig_send = lax.optimization_barrier((one[1], two[2], *side, ig_send))
    send1 = leaving(one, rows[1])
    one.append(exchange(send1, 2, bits))
    side[0], two[2], send1 = lax.optimization_barrier((side[0], two[2], send1))
    ig_got = swap_core(ig_send)
    for step in (1, 2):
        side.append(exchange(leaving(side, rows[step - 1]), step, bits))
    for step in range(3, bits):
        two.append(exchange(leaving(two, rows[step - 1]), step, bits))
    both = []
    for step in range(3, bits):
        n = rows[step - 1]
        ends = [leaving(one + [v[:, : 10 * c] for v in both], n),
                leaving(side + [v[:, 10 * c :] for v in both], n)]
        both.append(exchange(jnp.concatenate(ends, axis=1), step, bits))
    line = lambda n: ((n,), F32, VM)
    conv = ((3, 3, size, c), F32, VM)
    count = len(two)
    g_conv2, g_qkv, g_bconv2, g_gain3, g_bias3, g_bqv, g_bproj, emb, index = call(
        lambda *refs: kernel_last_two(c, size, refs[:count], *refs[count:]),
        [(v, VM) for v in two] + [(sigma_table, HBM), (class_table, HBM)],
        [conv, ((3 * size, c), F32, VM), line(size), line(size), line(size),
         line(2 * size), line(size), ((total, width), BF, VM), ((1, told), F32, VM)],
        [vmem((2 * size, 128), F32), vmem(sigma_table.shape), vmem(class_table.shape), dma(2)],
        name="last_two",
    )
    both[-1], emb = lax.optimization_barrier((both[-1], emb))
    tables = lambda count: ((2 * size, count), F32, VM)
    counts = (len(one), len(one) + len(side), len(one) + len(side) + len(both))
    image_half = (out.shape, BF, ANY)
    (output, input_grad, g_conv1, g_proj, g_gain2, g_bias2, g_bconv1, g_gain1, g_bias1, g_sigma, g_class, g_wemb,
     g_bemb) = call(
        lambda *refs: kernel_last_one(
            c, size, refs[: counts[0]], refs[counts[0] : counts[1]], refs[counts[1] : counts[2]],
            *refs[counts[2] :],
        ),
        [(v, VM) for v in one + side + both]
        + [(index, VM), (emb, VM), (out, ANY), (out_got, VM), (ig, ANY), (ig_got, VM)],
        [image_half, image_half, conv, ((size, c), F32, VM)] + [line(size)] * 5
        + [tables(sigma_table.shape[0]), tables(class_table.shape[0]), tables(width), line(2 * size)],
        [vmem((2 * size, 128), F32), dma(2)],
        alias=[(counts[2] + 2, 0), (counts[2] + 4, 1)], name="last_one",
    )
    place = lambda v: jnp.transpose(v, (0, 1, 3, 2))
    return (
        output, input_grad, g_sigma.T, g_class.T, g_wemb.T, g_bemb, g_gain1, g_bias1, place(g_conv1),
        g_bconv1, g_gain2, g_bias2, place(g_conv2), g_bconv2, g_gain3, g_bias3, g_qkv.T, g_bqv,
        g_proj.T, g_bproj,
    )


def solution(mesh):
    every = ("dp", "pipe")
    return jax.shard_map(
        body,
        mesh=mesh,
        in_specs=(P("dp", None, None), P("dp", None, None), P("dp"), P("dp")) + (P(),) * 18,
        out_specs=(
            P("dp", "pipe", None), P("dp", "pipe", None), P(None, every), P(None, every),
            P(None, every), P(every), P(every), P(every), P(None, None, None, every), P(every),
            P(every), P(every), P(None, None, None, every), P(every), P(every), P(every),
            P(None, every), P(every), P(None, every), P(every),
        ),
        check_vma=False,
    )
```
